32 devices in a mesh: dp: 16 (over z, y, x), mp: 2 (over core).
Axes of the slice: x: 2, y: 2, z: 4, core: 2. Of those that a mesh axis runs over, the one named last changes fastest.
Arguments:
- patches: bfloat16 [32, 784, 768], P('dp'), may hold values from -6 to 6
- ctx_index: int32 [32, 512], P('dp'), may hold values from 0 to 783, as said below
- tgt_index: int32 [32, 256], P('dp'), may hold values from 0 to 783, as said below
- group: int32 [32], P('dp'), may hold values from 0 to 1
- tgt_count: int32 [32], P('dp'), may hold values from 64 to 256
- embed: float32 [768, 768], P('dp'), may hold values from -0.21875 to 0.21875
- embed_m: float32 [768, 768], P('dp'), may hold values from -2.3841858e-07 to 2.3841858e-07
- embed_v: float32 [768, 768], P('dp'), may hold values from 2.4914533e-17 to 9.965813e-17
- bridge: float32 [768, 768], P('dp'), may hold values from -0.21875 to 0.21875
- bridge_m: float32 [768, 768], P('dp'), may hold values from -2.3841858e-07 to 2.3841858e-07
- bridge_v: float32 [768, 768], P('dp'), may hold values from 2.4914533e-17 to 9.965813e-17
- enc_in: float32 [768, 5376], P('dp', 'mp'), may hold values from -0.21875 to 0.21875
- enc_in_m: float32 [768, 5376], P('dp', 'mp'), may hold values from -2.3841858e-07 to 2.3841858e-07
- enc_in_v: float32 [768, 5376], P('dp', 'mp'), may hold values from 2.4914533e-17 to 9.965813e-17
- enc_out: float32 [3840, 768], P('mp', 'dp'), may hold values from -0.21875 to 0.21875
- enc_out_m: float32 [3840, 768], P('mp', 'dp'), may hold values from -2.3841858e-07 to 2.3841858e-07
- enc_out_v: float32 [3840, 768], P('mp', 'dp'), may hold values from 2.4914533e-17 to 9.965813e-17
- enc_gains: float32 [6, 768], P(None, 'dp')
- enc_gains_m: float32 [6, 768], P(None, 'dp'), may hold values from -2.3841858e-07 to 2.3841858e-07
- enc_gains_v: float32 [6, 768], P(None, 'dp'), may hold values from 2.4914533e-17 to 9.965813e-17
- pred_in: float32 [384, 2688], P('dp', 'mp'), may hold values from -0.3125 to 0.3125
- pred_in_m: float32 [384, 2688], P('dp', 'mp'), may hold values from -2.3841858e-07 to 2.3841858e-07
- pred_in_v: float32 [384, 2688], P('dp', 'mp'), may hold values from 2.4914533e-17 to 9.965813e-17
- pred_out: float32 [1920, 384], P('mp', 'dp'), may hold values from -0.3125 to 0.3125
- pred_out_m: float32 [1920, 384], P('mp', 'dp'), may hold values from -2.3841858e-07 to 2.3841858e-07
- pred_out_v: float32 [1920, 384], P('mp', 'dp'), may hold values from 2.4914533e-17 to 9.965813e-17
- pred_gains: float32 [7, 384], P(None, 'dp')
- pred_gains_m: float32 [7, 384], P(None, 'dp'), may hold values from -2.3841858e-07 to 2.3841858e-07
- pred_gains_v: float32 [7, 384], P(None, 'dp'), may hold values from 2.4914533e-17 to 9.965813e-17
- t_embed: float32 [768, 768], P('dp'), may hold values from -0.21875 to 0.21875
- t_in: float32 [768, 5376], P('dp', 'mp'), may hold values from -0.21875 to 0.21875
- t_out: float32 [3840, 768], P('mp', 'dp'), may hold values from -0.21875 to 0.21875
- t_gains: float32 [6, 768], P(None, 'dp')
Outputs:
- embed_new: float32 [768, 768], P('dp')
- embed_m_new: float32 [768, 768], P('dp')
- embed_v_new: float32 [768, 768], P('dp')
- bridge_new: float32 [768, 768], P('dp')
- bridge_m_new: float32 [768, 768], P('dp')
- bridge_v_new: float32 [768, 768], P('dp')
- enc_in_new: float32 [768, 5376], P('dp', 'mp')
- enc_in_m_new: float32 [768, 5376], P('dp', 'mp')
- enc_in_v_new: float32 [768, 5376], P('dp', 'mp')
- enc_out_new: float32 [3840, 768], P('mp', 'dp')
- enc_out_m_new: float32 [3840, 768], P('mp', 'dp')
- enc_out_v_new: float32 [3840, 768], P('mp', 'dp')
- enc_gains_new: float32 [6, 768], P(None, 'dp')
- enc_gains_m_new: float32 [6, 768], P(None, 'dp')
- enc_gains_v_new: float32 [6, 768], P(None, 'dp')
- pred_in_new: float32 [384, 2688], P('dp', 'mp')
- pred_in_m_new: float32 [384, 2688], P('dp', 'mp')
- pred_in_v_new: float32 [384, 2688], P('dp', 'mp')
- pred_out_new: float32 [1920, 384], P('mp', 'dp')
- pred_out_m_new: float32 [1920, 384], P('mp', 'dp')
- pred_out_v_new: float32 [1920, 384], P('mp', 'dp')
- pred_gains_new: float32 [7, 384], P(None, 'dp')
- pred_gains_m_new: float32 [7, 384], P(None, 'dp')
- pred_gains_v_new: float32 [7, 384], P(None, 'dp')
- loss_sum: float32 [], replicated
- grad_norm: float32 [], replicated
The draws below stay inside these ranges and needn't reach their ends.
Inputs may be any that keep to these rules, and one draw needn't show every extreme that they name: `ctx_index`: each row holds 512 distinct positions in increasing order, none of them in the same row of tgt_index. `tgt_index`: each row holds 256 distinct positions in increasing order.
All inputs are finite; a program needn't handle non-finite values.
Results may differ from the reference program's by a relative error of at most 0.04.
Values may be sent and summed in bfloat16 or wider, within the bound.
No kernel may reach another device: no remote copies, remote signals or barrier semaphores. Data moves between devices by JAX's collectives and lax.ppermute only.
A program may use at most 320 MiB of HBM per device.

```python
import math
import jax
import jax.numpy as jnp
from jax import lax

D = 768
HEADS = 12
FF = 3072
PW = 384
PHEADS = 12
PF = 1536
PIX = 768
SIDE = 14
SMALLP = 196
SEQ = 784
CTX = 512
TGT = 256
SLOTS = 32
COUNT = 6291456
STEP = 10
NPARAM = 10034304
N_MP = 2


def slot_orders(key):
    slot_keys = jax.random.split(key, SLOTS)
    return jax.vmap(lambda one_key: jax.random.permutation(one_key, SEQ))(slot_keys)


def draw_ctx_index(key, part):
    orders = slot_orders(key)
    return jnp.sort(orders[:, :CTX], axis=1).astype(jnp.int32)


def draw_tgt_index(key, part):
    orders = slot_orders(key)
    return jnp.sort(orders[:, CTX:CTX + TGT], axis=1).astype(jnp.int32)


def draw_tgt_count(key, part):
    key = jax.random.fold_in(key, 14)
    lowest = TGT // 4
    slot_ids = jnp.arange(SLOTS).astype(jnp.int32)
    base = lowest + (TGT - lowest) * slot_ids // (SLOTS - 1)
    jitter_size = max(1, TGT // 8)
    jitter = jax.random.randint(key, (SLOTS,), -jitter_size, jitter_size + 1).astype(jnp.int32)
    counts = jnp.clip(base + jitter, lowest, TGT)
    counts = jnp.where(slot_ids == 0, lowest, counts)
    counts = jnp.where(slot_ids == SLOTS - 1, TGT, counts)
    return counts.astype(jnp.int32)


def rising_rows(key, width, shift_scale):
    key_gain, key_shift = jax.random.split(key, 2)
    ramp = 1.0 + 2.0 * jnp.arange(width).astype(jnp.float32) / (width - 1)
    gains = ramp * jax.random.uniform(key_gain, (3, width), jnp.float32, 0.8, 1.2)
    shifts = shift_scale * jax.random.normal(key_shift, (3, width), jnp.float32)
    return jnp.stack([gains[0], shifts[0], gains[1], shifts[1], gains[2], shifts[2]])


def draw_enc_gains(key, part):
    key = jax.random.fold_in(key, 11)
    return rising_rows(key, D, 0.3)


def draw_t_gains(key, part):
    key = jax.random.fold_in(key, 12)
    return rising_rows(key, D, 0.3)


def draw_pred_gains(key, part):
    key = jax.random.fold_in(key, 13)
    key_rows, key_token = jax.random.split(key, 2)
    rows_part = rising_rows(key_rows, PW, 0.3)
    token = jax.random.normal(key_token, (1, PW), jnp.float32)
    return jnp.concatenate([rows_part, token], 0)


def set_ends(entries, key, least, largest):
    index_at = [jax.random.randint(jax.random.fold_in(key, axis), (), 0, length) for axis, length in enumerate(entries.shape)]
    longest = entries.shape.index(max(entries.shape))
    beside = index_at[:longest] + [(index_at[longest] + 1) % entries.shape[longest]] + index_at[longest + 1:]
    return entries.at[tuple(index_at)].set(least).at[tuple(beside)].set(largest)


def block_levels(own_key, shape, cuts, least, largest):
    loudness, own = 1.0, jax.random.fold_in(own_key, 6)
    for dim, shards_of in cuts:
        draws = jnp.exp(jax.random.uniform(jax.random.fold_in(own, dim), (shards_of,), jnp.float32, least / len(cuts), largest / len(cuts)))
        loudness = loudness * jnp.repeat(draws, shape[dim] // shards_of).reshape([-1 if axis == dim else 1 for axis in range(len(shape))])
    return loudness


def scatter_about(stream_key, shape, scale, bound, cuts=(), dtype=jnp.bfloat16):
    values = jax.random.normal(stream_key, shape, jnp.float32) * scale
    if len(cuts) > 0:
        values = block_levels(stream_key, shape, cuts, -0.22, 0.18) * values
    return jnp.clip(values, min=-bound, max=bound).astype(dtype)


def setup_inputs(seed: int = 0) -> dict:
    key_list = jax.random.split(jax.random.key(seed), 34)
    patches = scatter_about(key_list[0], (SLOTS, SEQ, PIX), 1.0, 6.0, ((0, 16),))
    ctx_index = draw_ctx_index(jax.random.fold_in(key_list[33], 71), 0)
    tgt_index = draw_tgt_index(jax.random.fold_in(key_list[33], 71), 0)
    group = set_ends(jax.random.randint(key_list[3], (SLOTS,), 0, 2), jax.random.fold_in(key_list[3], 1), 0, 1).astype(jnp.int32)
    tgt_count = draw_tgt_count(jax.random.fold_in(key_list[33], 71), 0)
    embed = scatter_about(key_list[5], (PIX, D), PIX ** -0.5, 0.21875, ((0, 16),), jnp.float32)
    embed_m = scatter_about(key_list[6], (PIX, D), (0.000055 * NPARAM ** -0.5), 2.384185791015625e-07, ((0, 16),), jnp.float32)
    embed_v = jnp.clip(jnp.exp(math.log(9.965813124779264e-17) - 1.3862944 * jax.random.uniform(key_list[7], (PIX, D), jnp.float32) ** block_levels(key_list[7], (PIX, D), ((0, 16),), -0.2, 0.2)), 2.491453281194816e-17, 9.965813124779264e-17)
    bridge = scatter_about(key_list[8], (D, 2 * PW), D ** -0.5, 0.21875, ((0, 16),), jnp.float32)
    bridge_m = scatter_about(key_list[9], (D, 2 * PW), (0.000055 * NPARAM ** -0.5), 2.384185791015625e-07, ((0, 16),), jnp.float32)
    bridge_v = jnp.clip(jnp.exp(math.log(9.965813124779264e-17) - 1.3862944 * jax.random.uniform(key_list[10], (D, 2 * PW), jnp.float32) ** block_levels(key_list[10], (D, 2 * PW), ((0, 16),), -0.2, 0.2)), 2.491453281194816e-17, 9.965813124779264e-17)
    enc_in = scatter_about(key_list[11], (D, 3 * D + FF), D ** -0.5, 0.21875, ((0, 16), (1, 2)), jnp.float32)
    enc_in_m = scatter_about(key_list[12], (D, 3 * D + FF), (0.000055 * NPARAM ** -0.5), 2.384185791015625e-07, ((0, 16), (1, 2)), jnp.float32)
    enc_in_v = jnp.clip(jnp.exp(math.log(9.965813124779264e-17) - 1.3862944 * jax.random.uniform(key_list[13], (D, 3 * D + FF), jnp.float32) ** block_levels(key_list[13], (D, 3 * D + FF), ((0, 16), (1, 2)), -0.2, 0.2)), 2.491453281194816e-17, 9.965813124779264e-17)
    enc_out = scatter_about(key_list[14], (D + FF, D), D ** -0.5, 0.21875, ((0, 2), (1, 16)), jnp.float32)
    enc_out_m = scatter_about(key_list[15], (D + FF, D), (0.000055 * NPARAM ** -0.5), 2.384185791015625e-07, ((0, 2), (1, 16)), jnp.float32)
    enc_out_v = jnp.clip(jnp.exp(math.log(9.965813124779264e-17) - 1.3862944 * jax.random.uniform(key_list[16], (D + FF, D), jnp.float32) ** block_levels(key_list[16], (D + FF, D), ((0, 2), (1, 16)), -0.2, 0.2)), 2.491453281194816e-17, 9.965813124779264e-17)
    enc_gains = draw_enc_gains(jax.random.fold_in(key_list[33], 71), 0)
    enc_gains_m = scatter_about(key_list[18], (6, D), (0.000055 * NPARAM ** -0.5), 2.384185791015625e-07, ((1, 16),), jnp.float32)
    enc_gains_v = jnp.clip(jnp.exp(math.log(9.965813124779264e-17) - 1.3862944 * jax.random.uniform(key_list[19], (6, D), jnp.float32) ** block_levels(key_list[19], (6, D), ((1, 16),), -0.2, 0.2)), 2.491453281194816e-17, 9.965813124779264e-17)
    pred_in = scatter_about(key_list[20], (PW, 3 * PW + PF), PW ** -0.5, 0.3125, ((0, 16), (1, 2)), jnp.float32)
    pred_in_m = scatter_about(key_list[21], (PW, 3 * PW + PF), (0.000055 * NPARAM ** -0.5), 2.384185791015625e-07, ((0, 16), (1, 2)), jnp.float32)
    pred_in_v = jnp.clip(jnp.exp(math.log(9.965813124779264e-17) - 1.3862944 * jax.random.uniform(key_list[22], (PW, 3 * PW + PF), jnp.float32) ** block_levels(key_list[22], (PW, 3 * PW + PF), ((0, 16), (1, 2)), -0.2, 0.2)), 2.491453281194816e-17, 9.965813124779264e-17)
    pred_out = scatter_about(key_list[23], (PW + PF, PW), PW ** -0.5, 0.3125, ((0, 2), (1, 16)), jnp.float32)
    pred_out_m = scatter_about(key_list[24], (PW + PF, PW), (0.000055 * NPARAM ** -0.5), 2.384185791015625e-07, ((0, 2), (1, 16)), jnp.float32)
    pred_out_v = jnp.clip(jnp.exp(math.log(9.965813124779264e-17) - 1.3862944 * jax.random.uniform(key_list[25], (PW + PF, PW), jnp.float32) ** block_levels(key_list[25], (PW + PF, PW), ((0, 2), (1, 16)), -0.2, 0.2)), 2.491453281194816e-17, 9.965813124779264e-17)
    pred_gains = draw_pred_gains(jax.random.fold_in(key_list[33], 71), 0)
    pred_gains_m = scatter_about(key_list[27], (7, PW), (0.000055 * NPARAM ** -0.5), 2.384185791015625e-07, ((1, 16),), jnp.float32)
    pred_gains_v = jnp.clip(jnp.exp(math.log(9.965813124779264e-17) - 1.3862944 * jax.random.uniform(key_list[28], (7, PW), jnp.float32) ** block_levels(key_list[28], (7, PW), ((1, 16),), -0.2, 0.2)), 2.491453281194816e-17, 9.965813124779264e-17)
    t_embed = scatter_about(key_list[29], (PIX, D), PIX ** -0.5, 0.21875, ((0, 16),), jnp.float32)
    t_in = scatter_about(key_list[30], (D, 3 * D + FF), D ** -0.5, 0.21875, ((0, 16), (1, 2)), jnp.float32)
    t_out = scatter_about(key_list[31], (D + FF, D), D ** -0.5, 0.21875, ((0, 2), (1, 16)), jnp.float32)
    t_gains = draw_t_gains(jax.random.fold_in(key_list[33], 71), 0)
    return {"patches": patches, "ctx_index": ctx_index, "tgt_index": tgt_index, "group": group, "tgt_count": tgt_count, "embed": embed, "embed_m": embed_m, "embed_v": embed_v, "bridge": bridge, "bridge_m": bridge_m, "bridge_v": bridge_v, "enc_in": enc_in, "enc_in_m": enc_in_m, "enc_in_v": enc_in_v, "enc_out": enc_out, "enc_out_m": enc_out_m, "enc_out_v": enc_out_v, "enc_gains": enc_gains, "enc_gains_m": enc_gains_m, "enc_gains_v": enc_gains_v, "pred_in": pred_in, "pred_in_m": pred_in_m, "pred_in_v": pred_in_v, "pred_out": pred_out, "pred_out_m": pred_out_m, "pred_out_v": pred_out_v, "pred_gains": pred_gains, "pred_gains_m": pred_gains_m, "pred_gains_v": pred_gains_v, "t_embed": t_embed, "t_in": t_in, "t_out": t_out, "t_gains": t_gains}


@jax.custom_vjp
def low(v):
    return lax.optimization_barrier(v.astype(jnp.bfloat16)).astype(jnp.float32)

@jax.custom_vjp
def low_back(v):
    return v

def low_keep(v):
    return (low(v), None)

def low_pass(kept, grad):
    return (grad,)

def back_keep(v):
    return (v, None)

def back_low(kept, grad):
    return (low(grad),)
low.defvjp(low_keep, low_pass)
low_back.defvjp(back_keep, back_low)
CLIP_NORM = 0.0005
LEARN_RATE = 0.05
GAIN_RATE = 1.0
BETA_ONE = 0.9
BETA_TWO = 0.999
EPSILON = 1e-08
WEIGHT_DECAY = 0.05
HIGHEST = lax.Precision.HIGHEST

def product(left, right):
    return jnp.dot(left, right, precision=HIGHEST)

def norm_rows(values, gain_row, shift_row):
    centred = values - lax.optimization_barrier(jnp.mean(values, -1, keepdims=True))
    spread = lax.optimization_barrier(jnp.mean(centred * centred, -1, keepdims=True))
    return centred * lax.rsqrt(spread + 1e-06) * gain_row + shift_row

def place(group_id, positions):
    single = group_id == 1
    image_id = jnp.where(single, 0, positions // SMALLP)
    within = jnp.where(single, positions, positions % SMALLP)
    side_len = jnp.where(single, 2 * SIDE, SIDE)
    return (image_id, within // side_len, within % side_len)

def sincos(row_pos, col_pos, width):
    quarter = width // 4
    omega = 10000.0 ** (-jnp.arange(quarter).astype(jnp.float32) / quarter)
    row_angle = row_pos.astype(jnp.float32)[..., None] * omega
    col_angle = col_pos.astype(jnp.float32)[..., None] * omega
    return jnp.concatenate([jnp.sin(row_angle), jnp.cos(row_angle), jnp.sin(col_angle), jnp.cos(col_angle)], -1)

@jax.checkpoint
def attend(query, key_part, value_part, image_id):
    scale = query.shape[-1] ** (-0.5)
    scores = low_back(jnp.einsum('rha,sha->hrs', query, key_part, precision=HIGHEST) * scale)
    same_image = image_id[:, None] == image_id[None, :]
    scores = jnp.where(same_image[None], scores, -1e+30)
    soft = low(jax.nn.softmax(scores, -1))
    return jnp.einsum('hrs,sha->rha', soft, value_part, precision=HIGHEST)

def block(hidden, image_id, w_in, w_out, gains, heads):
    width = hidden.shape[-1]
    local = width // N_MP
    head_dim = width // heads
    row_count = hidden.shape[0]
    inward = w_in.reshape(width, N_MP, w_in.shape[1] // N_MP)
    outward = w_out.reshape(N_MP, w_out.shape[0] // N_MP, width)
    normed = low(norm_rows(hidden, gains[0], gains[1]))
    total = jnp.zeros_like(hidden)
    for group_index in range(N_MP):
        projected = low(low_back(product(normed, inward[:, group_index, :3 * local])))
        shaped = projected.reshape(row_count, 3, heads // N_MP, head_dim)
        mixed = attend(shaped[:, 0], shaped[:, 1], shaped[:, 2], image_id)
        mixed = low(low_back(mixed.reshape(row_count, local)))
        total = total + product(mixed, outward[group_index, :local])
    middle = hidden + low_back(total)
    normed = low(norm_rows(middle, gains[2], gains[3]))
    total = jnp.zeros_like(hidden)
    for group_index in range(N_MP):
        pre_act = low_back(product(normed, inward[:, group_index, 3 * local:]))
        activated = low(jax.nn.gelu(pre_act, approximate=False))
        total = total + product(activated, outward[group_index, local:])
    return middle + low_back(total)

def adam(weight, moment_one, moment_two, gradient, decay, rate):
    moment_one = BETA_ONE * moment_one + (1.0 - BETA_ONE) * gradient
    moment_two = BETA_TWO * moment_two + (1.0 - BETA_TWO) * gradient * gradient
    fixed_one = moment_one / (1.0 - BETA_ONE ** STEP)
    fixed_two = moment_two / (1.0 - BETA_TWO ** STEP)
    weight = weight - rate * (fixed_one / (jnp.sqrt(fixed_two) + EPSILON) + decay * weight)
    return [weight, moment_one, moment_two]

def reference(patches, ctx_index, tgt_index, group, tgt_count, embed, embed_m, embed_v, bridge, bridge_m, bridge_v, enc_in, enc_in_m, enc_in_v, enc_out, enc_out_m, enc_out_v, enc_gains, enc_gains_m, enc_gains_v, pred_in, pred_in_m, pred_in_v, pred_out, pred_out_m, pred_out_v, pred_gains, pred_gains_m, pred_gains_v, t_embed, t_in, t_out, t_gains):
    masters = (embed, bridge, enc_in, enc_out, enc_gains, pred_in, pred_out, pred_gains)
    firsts = (embed_m, bridge_m, enc_in_m, enc_out_m, enc_gains_m, pred_in_m, pred_out_m, pred_gains_m)
    seconds = (embed_v, bridge_v, enc_in_v, enc_out_v, enc_gains_v, pred_in_v, pred_out_v, pred_gains_v)
    positions = jnp.arange(SEQ).astype(jnp.int32)
    target_slots = jnp.arange(TGT).astype(jnp.int32)
    target_embed, target_in, target_out = (low(t_embed), low(t_in), low(t_out))

    def target_slot(inputs):
        patch, tgt, group_id = inputs
        image_id, row_pos, col_pos = place(group_id, positions)
        start = product(patch.astype(jnp.float32), target_embed) + sincos(row_pos, col_pos, D)
        hidden = block(start, image_id, target_in, target_out, t_gains, HEADS)
        chosen = norm_rows(hidden[tgt], t_gains[4], t_gains[5])
        return norm_rows(chosen, 1.0, 0.0)
    targets = lax.map(target_slot, (patches, tgt_index, group))

    def total_loss(params):
        embed_w, bridge_w, enc_in_w, enc_out_w, enc_gain, pred_in_w, pred_out_w, pred_gain = params
        embed_w, bridge_w = (low(embed_w), low(bridge_w))
        enc_in_w, enc_out_w = (low(enc_in_w), low(enc_out_w))
        pred_in_w, pred_out_w = (low(pred_in_w), low(pred_out_w))

        def slot_loss(inputs):
            patch, ctx, tgt, group_id, target, count_used = inputs
            image_id, row_pos, col_pos = place(group_id, positions)
            table = sincos(row_pos, col_pos, D)
            small_table = sincos(row_pos, col_pos, PW)
            seen = patch[ctx].astype(jnp.float32)
            start = low_back(product(seen, embed_w)) + table[ctx]
            hidden = block(start, image_id[ctx], enc_in_w, enc_out_w, enc_gain, HEADS)
            context = low(norm_rows(hidden, enc_gain[4], enc_gain[5]))
            inward = low_back(product(context, bridge_w[:, :PW]))
            joined = jnp.concatenate([inward + small_table[ctx], pred_gain[6] + small_table[tgt]], 0)
            joined_id = jnp.concatenate([image_id[ctx], image_id[tgt]], 0)
            predicted = block(joined, joined_id, pred_in_w, pred_out_w, pred_gain, PHEADS)
            final = low(norm_rows(predicted[CTX:], pred_gain[4], pred_gain[5]))
            guess = low_back(product(final, bridge_w[:, PW:].T))
            diff = guess - target
            size_abs = jnp.abs(diff)
            terms = jnp.where(size_abs < 1.0, 0.5 * diff * diff, size_abs - 0.5)
            keep = (target_slots < count_used)[:, None]
            return jnp.sum(jnp.where(keep, terms, 0.0))
        terms = lax.map(jax.checkpoint(slot_loss), (patches, ctx_index, tgt_index, group, targets, tgt_count))
        return jnp.sum(terms)
    loss_sum, pullback = jax.vjp(total_loss, masters)
    grads = pullback(jnp.ones_like(loss_sum) / COUNT)[0]
    grad_norm = jnp.sqrt(sum((jnp.sum(item * item) for item in grads)))
    factor = jnp.minimum(1.0, CLIP_NORM / (grad_norm + 1e-06))
    results = []
    for index_pos in range(8):
        is_gain = index_pos in (4, 7)
        decay = 0.0 if is_gain else WEIGHT_DECAY
        rate = GAIN_RATE if is_gain else LEARN_RATE
        results.extend(adam(masters[index_pos], firsts[index_pos], seconds[index_pos], grads[index_pos] * factor, decay, rate))
    return (results[0], results[1], results[2], results[3], results[4], results[5], results[6], results[7], results[8], results[9], results[10], results[11], results[12], results[13], results[14], results[15], results[16], results[17], results[18], results[19], results[20], results[21], results[22], results[23], loss_sum, grad_norm)
```

```python
import functools

import jax
import jax.numpy as jnp
from jax import lax
from jax.experimental import pallas as pl
from jax.experimental.pallas import tpu as pltpu
from jax.sharding import PartitionSpec as P

D = 768
HEADS = 12
PW = 384
PHEADS = 12
SIDE = 14
SMALLP = 196
CTX = 512
TGT = 256
STEP = 10


LOW = jnp.bfloat16
WIDE = jnp.float32
CLIP_NORM = 0.0005
LEARN_RATE = 0.05
GAIN_RATE = 1.0
BETA_ONE = 0.9
BETA_TWO = 0.999
EPSILON = 1e-08
WEIGHT_DECAY = 0.05


LANES = 128


def norm_rows(values, gain_row, shift_row):
    centred = values - jnp.mean(values, -1, keepdims=True)
    spread = jnp.mean(centred * centred, -1, keepdims=True)
    return centred * lax.rsqrt(spread + 1e-06) * gain_row + shift_row


def norm_back(values, gain_row, grad):
    centred = values - jnp.mean(values, -1, keepdims=True)
    rstd = lax.rsqrt(jnp.mean(centred * centred, -1, keepdims=True) + 1e-06)
    unit = centred * rstd
    scaled = grad * gain_row
    d_values = rstd * (
        scaled
        - jnp.mean(scaled, -1, keepdims=True)
        - unit * jnp.mean(scaled * unit, -1, keepdims=True)
    )
    return d_values, jnp.sum(grad * unit, 0), jnp.sum(grad, 0)


def gelu_parts(pre):
    bell = jnp.exp(-0.5 * pre * pre)
    turn = 1.0 / (1.0 + 0.3275911 * 0.7071067811865476 * jnp.abs(pre))
    series = 0.5 * 1.061405429
    for factor in (-1.453152027, 1.421413741, -0.284496736, 0.254829592):
        series = series * turn + 0.5 * factor
    tail = series * turn * bell
    return jnp.where(pre < 0.0, tail, 1.0 - tail), bell * 0.3989422804014327


def gelu_both(pre):
    phi, density = gelu_parts(pre)
    return (pre * phi).astype(LOW), (phi + pre * density).astype(LOW)


def place(single, positions):
    image_id = jnp.where(single, 0, positions // SMALLP)
    within = jnp.where(single, positions, positions % SMALLP)
    side_len = jnp.where(single, 2 * SIDE, SIDE)
    return (image_id, within // side_len, within % side_len)


def three_parts(values):
    high = lax.reduce_precision(values, 8, 7)
    rest = values - high
    middle = lax.reduce_precision(rest, 8, 7)
    return jnp.concatenate([high, middle, rest - middle], 0).astype(LOW)


def sincos(row_pos, col_pos, width, order):
    quarter = width // 4
    omega = 10000.0 ** (-jnp.arange(quarter).astype(WIDE) / quarter)
    steps = jnp.arange(2 * SIDE)
    angle = steps.astype(WIDE)[:, None] * omega
    table = jnp.concatenate([jnp.sin(angle), jnp.cos(angle)], -1)
    blank = jnp.zeros_like(table)
    table = jnp.concatenate(
        [jnp.concatenate([table, blank], 1), jnp.concatenate([blank, table], 1)], 0
    )
    parts = three_parts(table)
    if order is not None:
        parts = mm(parts, order).astype(LOW)
    pick = jnp.concatenate([row_pos[:, None] == steps, col_pos[:, None] == steps], 1)
    pick = pick.astype(LOW)
    return mm(jnp.concatenate([pick, pick, pick], 1), parts)


def mm(left, right):
    return jnp.dot(left, right, preferred_element_type=WIDE)


def mm_t(left, right):
    return lax.dot_general(left, right, (((1,), (1,)), ((), ())), preferred_element_type=WIDE)


def t_mm(left, right):
    return lax.dot_general(left, right, (((0,), (0,)), ((), ())), preferred_element_type=WIDE)


def head_forward(query, keys, values, bias, size):
    scores = mm_t(keys, query) + bias
    soft = jnp.exp((scores - jnp.max(scores, 0, keepdims=True)) * size**-0.5)
    total = jnp.sum(soft, 0, keepdims=True)
    return (t_mm(values, soft.astype(LOW)) / total).T


def head_backward(query, keys, values, d_out, bias, size):
    scale = size**-0.5
    scores = mm_t(keys, query) + bias
    soft = jnp.exp((scores - jnp.max(scores, 0, keepdims=True)) * scale)
    soft = soft * (1.0 / jnp.sum(soft, 0, keepdims=True))
    d_soft = mm_t(values, d_out)
    row_sum = jnp.sum(d_soft * soft, 0, keepdims=True)
    d_scores = (soft * (d_soft - row_sum)).astype(LOW)
    d_values = mm(soft.astype(LOW), d_out)
    d_keys = mm(d_scores, query) * scale
    d_query = (t_mm(keys, d_scores) * scale).T
    return d_query.astype(LOW), d_keys.astype(LOW), d_values.astype(LOW)


WHOLE = pl.BlockSpec(memory_space=pltpu.VMEM)
CHUNK = 64


def on_chip(kernel, ins, outs, scratch, macs, exps=0):
    outs = [jax.ShapeDtypeStruct(shape, kind) for shape, kind in outs]
    moved = sum(value.size * value.dtype.itemsize for value in list(ins) + outs)
    return pl.pallas_call(
        kernel,
        in_specs=[WHOLE] * len(ins),
        out_specs=[WHOLE] * len(outs),
        out_shape=outs,
        scratch_shapes=[pltpu.VMEM(shape, kind) for shape, kind in scratch],
        cost_estimate=pl.CostEstimate(flops=2 * macs, bytes_accessed=moved, transcendentals=exps),
        compiler_params=pltpu.CompilerParams(vmem_limit_bytes=56 * 1024 * 1024),
    )(*ins)


def tiles(count, width, body):
    def step(at, carry):
        body(pl.ds(pl.multiple_of(at * width, width), width))
        return carry

    lax.fori_loop(0, count // width, step, 0)


def norm_back_rows(values_ref, grad_ref, gain, write, sums_ref, at):
    rows, width = values_ref.shape

    def step(number, carry):
        span = pl.ds(pl.multiple_of(number * CHUNK, CHUNK), CHUNK)
        values, grad = values_ref[span, :], grad_ref[span, :]
        centred = values - jnp.mean(values, -1, keepdims=True)
        rstd = lax.rsqrt(jnp.mean(centred * centred, -1, keepdims=True) + 1e-06)
        unit = centred * rstd
        scaled = grad * gain
        d_values = rstd * (
            scaled
            - jnp.mean(scaled, -1, keepdims=True)
            - unit * jnp.mean(scaled * unit, -1, keepdims=True)
        )
        write(span, d_values)
        return (
            carry[0] + jnp.sum(grad * unit, 0, keepdims=True),
            carry[1] + jnp.sum(grad, 0, keepdims=True),
        )

    blank = jnp.zeros((1, width), WIDE)
    gains, shifts = lax.fori_loop(0, rows // CHUNK, step, (blank, blank))
    sums_ref[at : at + 1, :] = gains
    sums_ref[at + 1 : at + 2, :] = shifts


def ff_back_kernel(*refs):
    (d_inward, bridge_in, hidden, middle, normed, order, gains) = refs[0:7]
    acts, slopes, ups, downs = refs[7:9], refs[9:11], refs[11:13], refs[13:15]
    grads, branch_out, d_middle, sums = refs[15:19], refs[19], refs[20], refs[21]
    grad, d_hidden, branch, branch_t, normed_t, d_pre = refs[22:28]
    ff = acts[0].shape[1]
    wide = 768

    def first(span):
        grad[:, span] = mm_t(d_inward[...], bridge_in[span, :])

    tiles(D, wide, first)

    def write_hidden(span, values):
        d_hidden[span, :] = values
        branch[span, :] = values.astype(LOW)

    norm_back_rows(hidden, grad, gains[4:5, :], write_hidden, sums, 0)
    branch_t[...] = mm_t(order[...], branch[...]).astype(LOW)
    normed_t[...] = mm_t(order[...], normed[...]).astype(LOW)
    for side in (0, 1):
        act, slope, down = acts[side], slopes[side], downs[side]
        out_up, out_down = grads[2 * side], grads[2 * side + 1]

        def second(
            span, act=act, slope=slope, down=down, out_up=out_up, out_down=out_down, side=side
        ):
            d_act = mm(branch[...], down[:, span])
            values = (d_act * slope[:, span].astype(WIDE)).astype(LOW)
            d_pre[side, :, span] = values
            out_up[:, span] = mm(normed_t[...], values).astype(LOW)
            out_down[:, span] = mm(branch_t[...], act[:, span]).astype(LOW)

        tiles(ff, wide, second)

    def third(span):
        grad[:, span] = mm_t(d_pre[0], ups[0][span, :]) + mm_t(d_pre[1], ups[1][span, :])

    tiles(D, wide, third)

    def write_middle(span, values):
        values = values + d_hidden[span, :]
        d_middle[span, :] = values
        branch_out[span, :] = values.astype(LOW)

    norm_back_rows(middle, grad, gains[2:3, :], write_middle, sums, 2)


def ff_back(d_inward, bridge_in, hidden, middle, normed, order, gains, acts, slopes, ups, downs):
    rows, ff = acts[0].shape
    return on_chip(
        ff_back_kernel,
        [d_inward, bridge_in, hidden, middle, normed, order, gains]
        + [*acts, *slopes, *ups, *downs],
        [((D, ff), LOW)] * 4 + [((rows, D), LOW), ((rows, D), WIDE), ((8, D), WIDE)],
        [((rows, D), WIDE)] * 2
        + [((rows, D), LOW), ((D, rows), LOW), ((D, rows), LOW), ((2, rows, ff), LOW)],
        8 * rows * D * ff,
    )


def attn_back_kernel(size, branch, ids_row, ids_col, *refs):
    rests, projs, d_projs, d_mixed = refs[0:2], refs[2:4], refs[4:6], refs[6]
    width = D // 2
    bias = jnp.where(ids_col[...] == ids_row[...], 0.0, -1e30)
    for rest, proj, d_proj in zip(rests, projs, d_projs):
        d_mixed[...] = mm(branch[...], rest[:, width : 2 * width]).astype(LOW)

        def step(block, carry, proj=proj, d_proj=d_proj):
            at = [pl.multiple_of(part * width + block * LANES, LANES) for part in range(3)]
            query, keys, values = [proj[:, pl.ds(col, LANES)] for col in at]
            d_out = d_mixed[:, pl.ds(at[0], LANES)]
            found = []
            for low in range(0, LANES, size):
                cols = slice(low, low + size)
                found.append(
                    head_backward(
                        query[:, cols], keys[:, cols], values[:, cols], d_out[:, cols], bias, size
                    )
                )
            for col, parts in zip(at, zip(*found)):
                d_proj[:, pl.ds(col, LANES)] = jnp.concatenate(parts, -1)
            return carry

        lax.fori_loop(0, width // LANES, step, 0)


def attn_back(size, branch, ids, rests, projs):
    rows = branch.shape[0]
    return on_chip(
        functools.partial(attn_back_kernel, size),
        [branch, ids[None, :], ids[:, None], *rests, *projs],
        [(projs[0].shape, LOW)] * 2,
        [((rows, D // 2), LOW)],
        rows * D * D + rows * rows * D * 5,
        rows * rows * D // size,
    )


def qkv_back_kernel(*refs):
    branch, d_middle, start, normed, seen, eye, gains, sums_ff, sums_p, spread = refs[0:10]
    d_projs, mixeds, qkvs, orders = refs[10:12], refs[12:14], refs[14:16], refs[16:18]
    out_qkv, out_rest = refs[18:20], refs[20:22]
    grad, flipped, d_start, sums = refs[22:26]
    width = D // 2
    flipped[...] = mm_t(eye[...], branch[...]).astype(LOW)
    for side in (0, 1):
        out_rest[side][:, width : 2 * width] = mm(flipped[...], mixeds[side][...]).astype(LOW)
    flipped[...] = mm_t(eye[...], normed[...]).astype(LOW)
    for side in (0, 1):
        out_qkv[side][...] = mm(flipped[...], d_projs[side][...]).astype(LOW)
    grad[...] = mm_t(d_projs[0][...], qkvs[0][...]) + mm_t(d_projs[1][...], qkvs[1][...])

    def write(span, values):
        d_start[span, :] = (values + d_middle[span, :]).astype(LOW)

    norm_back_rows(start, grad, gains[0:1, :], write, sums, 0)
    flipped[...] = mm_t(eye[...], seen[...]).astype(LOW)
    sums[2:4, :] = sums_ff[2:4, :]
    sums[4:6, :] = sums_ff[0:2, :]
    sums[6:8, :] = jnp.zeros((2, D), WIDE)
    rows = jnp.concatenate(
        [sums[...].astype(LOW), mm(sums_p[...].astype(LOW), spread[...]).astype(LOW)], 0
    )
    cols = t_mm(rows, eye[0:16, 0:LANES]).astype(LOW)
    for side in (0, 1):
        moved = mm_t(d_start[...], orders[side][...]).astype(LOW)
        out_rest[side][:, 0:width] = mm(flipped[...], moved).astype(LOW)
        out_rest[side][:, 2 * width :] = cols


def qkv_back(branch, d_middle, start, normed, seen, eye, gains, sums_ff, sums_p, spread, pairs):
    rows, width = branch.shape[0], D // 2
    return on_chip(
        qkv_back_kernel,
        [branch, d_middle, start, normed, seen, eye, gains, sums_ff, sums_p, spread]
        + [value for pair in pairs for value in pair],
        [((D, 3 * width), LOW)] * 2 + [((D, 2 * width + LANES), LOW)] * 2,
        [((rows, D), WIDE), ((D, rows), LOW), ((rows, D), LOW), ((8, D), WIDE)],
        rows * D * D * 10,
    )


def row_spans(rows, chunk, body):
    def step(number, carry):
        body(pl.ds(pl.multiple_of(number * chunk, chunk), chunk))
        return carry

    lax.fori_loop(0, rows // chunk, step, 0)


def heads_forward(query_ref, keys_ref, values_ref, out_ref, bias, size, at):
    width = out_ref.shape[1]

    def step(block, carry):
        cols = [pl.multiple_of(first + block * LANES, LANES) for first in at]
        query = query_ref[:, pl.ds(cols[0], LANES)]
        keys = keys_ref[:, pl.ds(cols[1], LANES)]
        values = values_ref[:, pl.ds(cols[2], LANES)]
        found = []
        for low in range(0, LANES, size):
            part = slice(low, low + size)
            found.append(head_forward(query[:, part], keys[:, part], values[:, part], bias, size))
        place_at = pl.ds(pl.multiple_of(block * LANES, LANES), LANES)
        out_ref[:, place_at] = jnp.concatenate(found, -1).astype(LOW)
        return carry

    lax.fori_loop(0, width // LANES, step, 0)


def ctx_kernel(size, *refs):
    seen, pos, gains, ids_row, ids_col = refs[0:5]
    orders, rests, qkvs = refs[5:7], refs[7:9], refs[9:11]
    start, normed, middle, normed_two = refs[11:15]
    projs, mixeds = refs[15:17], refs[17:19]
    embed_w = refs[19]
    width = orders[0].shape[0]
    rows = seen.shape[0]
    embed_w[...] = (
        mm(rests[0][:, 0:width], orders[0][...]) + mm(rests[1][:, 0:width], orders[1][...])
    ).astype(LOW)
    start[...] = mm(seen[...], embed_w[...]) + pos[...]

    def first_norm(span):
        normed[span, :] = norm_rows(start[span, :], gains[0:1, :], gains[1:2, :]).astype(LOW)

    row_spans(rows, CHUNK, first_norm)
    bias = jnp.where(ids_col[...] == ids_row[...], 0.0, -1e30)
    for side in (0, 1):
        projs[side][...] = mm(normed[...], qkvs[side][...]).astype(LOW)
        heads_forward(
            projs[side], projs[side], projs[side], mixeds[side], bias, size, (0, width, 2 * width)
        )
    middle[...] = (
        start[...]
        + mm_t(mixeds[0][...], rests[0][:, width : 2 * width])
        + mm_t(mixeds[1][...], rests[1][:, width : 2 * width])
    )

    def second_norm(span):
        normed_two[span, :] = norm_rows(middle[span, :], gains[2:3, :], gains[3:4, :]).astype(LOW)

    row_spans(rows, CHUNK, second_norm)


def ctx_forward(size, seen, pos, gains, ids, orders, rests, qkvs):
    rows, width = seen.shape[0], orders[0].shape[0]
    return on_chip(
        functools.partial(ctx_kernel, size),
        [seen, pos, gains, ids[None, :], ids[:, None], *orders, *rests, *qkvs],
        [((rows, D), WIDE), ((rows, D), LOW), ((rows, D), WIDE), ((rows, D), LOW)]
        + [((rows, 3 * width), LOW)] * 2
        + [((rows, width), LOW)] * 2,
        [((D, D), LOW)],
        rows * D * D * 6 + D * D * D + rows * rows * D * 2,
        rows * rows * D // size,
    )


def gelu_rows(pre_ref, act_ref, slope_ref, span):
    def body(rows):
        act, slope = gelu_both(pre_ref[rows, :])
        act_ref[rows, span] = act
        if slope_ref is not None:
            slope_ref[rows, span] = slope

    row_spans(pre_ref.shape[0], 32, body)


def ff_kernel(*refs):
    normed, middle, gains, ups, downs = *refs[0:3], refs[3:5], refs[5:7]
    hidden, context, acts, slopes, pre = refs[7], refs[8], refs[9:11], refs[11:13], refs[13]
    rows, ff = acts[0].shape
    for side in (0, 1):

        def first(span, side=side):
            pre[...] = mm(normed[...], ups[side][:, span])
            gelu_rows(pre, acts[side], slopes[side], span)

        tiles(ff, 512, first)
    hidden[...] = (
        middle[...] + mm_t(acts[0][...], downs[0][...]) + mm_t(acts[1][...], downs[1][...])
    )

    def last(span):
        context[span, :] = norm_rows(hidden[span, :], gains[4:5, :], gains[5:6, :]).astype(LOW)

    row_spans(rows, CHUNK, last)


def ff_forward(normed, middle, gains, ups, downs):
    rows, ff = normed.shape[0], ups[0].shape[1]
    return on_chip(
        ff_kernel,
        [normed, middle, gains, *ups, *downs],
        [((rows, D), WIDE), ((rows, D), LOW)] + [((rows, ff), LOW)] * 4,
        [((rows, 512), WIDE)],
        rows * D * ff * 4 + rows * D * D,
        rows * ff * 2,
    )


def target_kernel(size, *refs):
    patch, seen, pos_all, pos_tgt, gains, ids_row, ids_col = refs[0:7]
    orders, weights, (t_middle, t_two), (embed_w, hidden, normed, start, query, keys, mixed) = (
        refs[7:9],
        refs[9:11],
        refs[11:13],
        refs[13:],
    )
    width = D // 2
    own, other = [part[:, 3 * width : 4 * width] for part in weights]
    embed_w[...] = (mm(own, orders[0][...]) + mm(other, orders[1][...])).astype(LOW)
    hidden[...] = mm(patch[...], embed_w[...]) + pos_all[...]

    def first_norm(span):
        normed[span, :] = norm_rows(hidden[span, :], gains[0:1, :], gains[1:2, :]).astype(LOW)

    row_spans(patch.shape[0], 112, first_norm)
    start[...] = mm(seen[...], embed_w[...]) + pos_tgt[...]
    t_normed = norm_rows(start[...], gains[0:1, :], gains[1:2, :]).astype(LOW)
    bias = jnp.where(ids_col[...] == ids_row[...], 0.0, -1e30)
    total = start[...]
    for part in weights:
        query[...] = mm(t_normed, part[:, 0:width]).astype(LOW)
        keys[...] = mm(normed[...], part[:, width : 3 * width]).astype(LOW)
        heads_forward(query, keys, keys, mixed, bias, size, (0, 0, width))
        total = total + mm_t(mixed[...], part[:, 4 * width : 5 * width])
    t_middle[...] = total
    t_two[...] = norm_rows(total, gains[2:3, :], gains[3:4, :]).astype(LOW)


def target_forward(
    size, patch, seen, pos_all, pos_tgt, gains, idq, idk, orders, weights
):
    rows, count, width = seen.shape[0], patch.shape[0], D // 2
    return on_chip(
        functools.partial(target_kernel, size),
        [patch, seen, pos_all, pos_tgt, gains, idq[None, :], idk[:, None], *orders, *weights],
        [((rows, D), WIDE), ((rows, D), LOW)],
        [
            ((D, D), LOW),
            ((count, D), WIDE),
            ((count, D), LOW),
            ((rows, D), WIDE),
            ((rows, width), LOW),
            ((count, 2 * width), LOW),
            ((rows, width), LOW),
        ],
        count * D * D * 3 + rows * D * D * 3 + 2 * rows * count * D,
        rows * count * D // size,
    )


def pred_forward_kernel(size, *refs):
    context, bridge_in, bridge_out, pos, gains, ids_row, ids_col = refs[0:7]
    downs, ups, qks, rights = refs[7:9], refs[9:11], refs[11:13], refs[13:15]
    joined, normed, middle, normed_two, predicted, final, guess = refs[15:22]
    out_qk, out_v, mixeds, acts, slopes = (
        refs[22:24],
        refs[24:26],
        refs[26:28],
        refs[28:30],
        refs[30:32],
    )
    width = out_v[0].shape[1]
    rows = middle.shape[0]
    joined[0:CTX, :] = mm(context[...], bridge_in[...]) + pos[0:CTX, :]
    joined[CTX:, :] = gains[6:7, :] + pos[CTX:, :]

    def first(span):
        normed[span, :] = norm_rows(joined[span, :], gains[0:1, :], gains[1:2, :]).astype(LOW)

    row_spans(joined.shape[0], 128, first)
    bias = jnp.where(ids_col[...] == ids_row[...], 0.0, -1e30)
    total = joined[CTX:, :]
    for qk, right, qk_ref, v_ref, mixed in zip(qks, rights, out_qk, out_v, mixeds):
        qk_ref[...] = mm(normed[...], qk[...]).astype(LOW)
        v_ref[...] = mm(normed[...], right[:, 0:width]).astype(LOW)
        found = []
        for low in range(0, width, size):
            found.append(
                head_forward(
                    qk_ref[CTX:, low : low + size],
                    qk_ref[:, width + low : width + low + size],
                    v_ref[:, low : low + size],
                    bias,
                    size,
                )
            )
        mixed[...] = jnp.concatenate(found, -1).astype(LOW)
        total = total + mm_t(mixed[...], right[:, width:])
    middle[...] = total
    normed_two[...] = norm_rows(total, gains[2:3, :], gains[3:4, :]).astype(LOW)
    total = middle[...]
    for up, down, act, slope in zip(ups, downs, acts, slopes):
        values, tilt = gelu_both(mm(normed_two[...], up[...]))
        act[...] = values
        slope[...] = tilt
        total = total + mm_t(act[...], down[...])
    predicted[...] = total
    final[...] = norm_rows(total, gains[4:5, :], gains[5:6, :]).astype(LOW)
    guess[...] = mm_t(final[...], bridge_out[...])


def pred_forward(
    size, context, bridge_in, bridge_out, pos, gains, idq, idk, downs, ups, qks, rights
):
    rows, count, width, ff = idq.shape[0], idk.shape[0], qks[0].shape[1] // 2, ups[0].shape[1]
    low, wide = LOW, WIDE
    return on_chip(
        functools.partial(pred_forward_kernel, size),
        [context, bridge_in, bridge_out, pos, gains, idq[None, :], idk[:, None]]
        + [*downs, *ups, *qks, *rights],
        [((count, PW), wide), ((count, PW), low), ((rows, PW), wide), ((rows, PW), low)]
        + [((rows, PW), wide), ((rows, PW), low), ((rows, D), wide)]
        + [((count, 2 * width), low)] * 2
        + [((count, width), low)] * 2
        + [((rows, width), low)] * 2
        + [((rows, ff), low)] * 4,
        [],
        1_000_000_000,
        rows * count * PW // size,
    )


def target_ff_kernel(t_two, t_middle, gains, *refs):
    ups, downs, (target, pre, act, total) = refs[0:2], refs[2:4], refs[4:8]
    total[...] = t_middle[...]
    for up, down in zip(ups, downs):

        def first(span, up=up):
            pre[...] = mm(t_two[...], up[:, span])
            gelu_rows(pre, act, None, span)

        tiles(act.shape[1], 512, first)
        total[...] = total[...] + mm_t(act[...], down[...])
    chosen = norm_rows(total[...], gains[4:5, :], gains[5:6, :])
    target[...] = norm_rows(chosen, 1.0, 0.0)


def target_ff(t_two, t_middle, gains, ups, downs):
    rows, ff = t_two.shape[0], ups[0].shape[1]
    return on_chip(
        target_ff_kernel,
        [t_two, t_middle, gains, *ups, *downs],
        [((rows, D), WIDE)],
        [((rows, 512), WIDE), ((rows, ff), LOW), ((rows, D), WIDE)],
        rows * D * ff * 4,
        rows * ff * 2,
    )[0]


def pred_back_all_kernel(size, count_all, *refs):
    (guess, target, used, context, final, bridge_in, bridge_out, gains, ids_row, ids_col) = refs[
        0:10
    ]
    predicted, middle, joined, normed, normed_two = refs[10:15]
    downs, ups, qks, rights = refs[15:17], refs[17:19], refs[19:21], refs[21:23]
    acts, slopes, in_qk, in_v, mixeds = (
        refs[23:25],
        refs[25:27],
        refs[27:29],
        refs[29:31],
        refs[31:33],
    )
    loss, d_inward, g_bridge_in, g_bridge_out, sums = refs[33:38]
    g_left, g_right = refs[38:40], refs[40:42]
    d_qk, d_v, d_normed = refs[42:45]
    width = in_v[0].shape[1]
    ff = acts[0].shape[1]
    diff = guess[...] - target[...]
    size_abs = jnp.abs(diff)
    keep = lax.broadcasted_iota(jnp.int32, diff.shape, 0) < used[0]
    terms = jnp.where(
        keep, jnp.where(size_abs < 1.0, 0.5 * diff * diff, size_abs - 0.5), 0.0
    )
    loss[...] = jnp.sum(jnp.sum(terms, 0, keepdims=True), 1, keepdims=True)
    d_guess = jnp.where(keep, jnp.clip(diff, -1.0, 1.0) / count_all, 0.0).astype(LOW)
    g_bridge_out[...] = t_mm(d_guess, final[...]).astype(LOW)

    def back(values, gain, grad, at):
        d_values, gain_sum, shift_sum = norm_back(values, gain, grad)
        sums[at : at + 1, :] = gain_sum[None, :]
        sums[at + 1 : at + 2, :] = shift_sum[None, :]
        return d_values

    d_tail = back(predicted[...], gains[4:5, :], mm(d_guess, bridge_out[...]), 4)
    branch = d_tail.astype(LOW)
    total = None
    for side in (0, 1):
        d_pre = (mm(branch, downs[side][...]) * slopes[side][...].astype(WIDE)).astype(LOW)
        g_left[side][:, 0:ff] = t_mm(branch, acts[side][...]).astype(LOW)
        g_right[side][:, 0:ff] = t_mm(normed_two[...], d_pre).astype(LOW)
        part = mm_t(d_pre, ups[side][...])
        total = part if total is None else total + part
    d_middle = d_tail + back(middle[...], gains[2:3, :], total, 2)
    branch = d_middle.astype(LOW)
    bias = jnp.where(ids_col[...] == ids_row[...], 0.0, -1e30)
    total = None
    for side in (0, 1):
        qk_ref, v_ref, right = in_qk[side], in_v[side], rights[side]
        d_mixed = mm(branch, right[:, width:]).astype(LOW)
        g_right[side][:, ff + width :] = t_mm(branch, mixeds[side][...]).astype(LOW)
        found = []
        for low in range(0, width, size):
            found.append(
                head_backward(
                    qk_ref[CTX:, low : low + size],
                    qk_ref[:, width + low : width + low + size],
                    v_ref[:, low : low + size],
                    d_mixed[:, low : low + size],
                    bias,
                    size,
                )
            )
        d_query, d_keys, d_values = [jnp.concatenate(parts, -1) for parts in zip(*found)]
        d_qk[0:CTX, 0:width] = jnp.zeros((CTX, width), LOW)
        d_qk[CTX:, 0:width] = d_query
        d_qk[:, width:] = d_keys
        d_v[...] = d_values
        g_left[side][:, ff:] = t_mm(normed[...], d_qk[...]).astype(LOW)
        g_right[side][:, ff : ff + width] = t_mm(normed[...], d_v[...]).astype(LOW)
        part = mm_t(d_qk[...], qks[side][...]) + mm_t(d_v[...], right[:, 0:width])
        d_normed[...] = part if side == 0 else d_normed[...] + part
    d_joined = back(joined[...], gains[0:1, :], d_normed[...], 0)
    sums[6:7, :] = jnp.sum(d_joined[CTX:] + d_middle, 0, keepdims=True)
    sums[7:8, :] = jnp.zeros((1, PW), WIDE)
    d_inward[...] = d_joined[0:CTX].astype(LOW)
    g_bridge_in[...] = t_mm(context[...], d_inward[...]).astype(LOW)


def pred_back_all(size, count_all, used, values, pairs, idq, idk):
    (guess, target, context, final, bridge_in, bridge_out, gains) = values[:7]
    ff, width, count = pairs[0][0].shape[1], pairs[2][0].shape[1] // 2, idk.shape[0]
    ins = [guess, target, used, context, final, bridge_in, bridge_out, gains]
    ins += [idq[None, :], idk[:, None], *values[7:]] + [part for pair in pairs for part in pair]
    outs = [((1, 1), WIDE), ((CTX, PW), LOW), ((D, PW), LOW), ((D, PW), LOW), ((8, PW), WIDE)]
    outs += [((PW, ff + 2 * width), LOW)] * 4
    specs = [WHOLE] * len(ins)
    specs[2] = pl.BlockSpec(memory_space=pltpu.SMEM)
    return pl.pallas_call(
        functools.partial(pred_back_all_kernel, size, count_all),
        in_specs=specs,
        out_specs=[WHOLE] * len(outs),
        out_shape=[jax.ShapeDtypeStruct(shape, kind) for shape, kind in outs],
        scratch_shapes=[
            pltpu.VMEM((count, 2 * width), LOW),
            pltpu.VMEM((count, width), LOW),
            pltpu.VMEM((count, PW), WIDE),
        ],
        cost_estimate=pl.CostEstimate(
            flops=4_000_000_000, bytes_accessed=20_000_000, transcendentals=3_000_000
        ),
        compiler_params=pltpu.CompilerParams(vmem_limit_bytes=56 * 1024 * 1024),
    )(*ins)


class Lines:
    def __init__(self, count):
        self.count = count
        self.stride = count // 4
        bits = list(range(self.stride.bit_length() - 1))
        turn = len(bits) // 2
        self.bits = bits
        self.orders = (bits, bits[turn:] + bits[:turn])
        self.turn = turn

    def flip(self, values, bit):
        pairs = [(at, at ^ (1 << bit)) for at in range(self.count)]
        return lax.ppermute(values, "dp", pairs)

    def shift(self, values, steps):
        pairs = [(at, (at + steps * self.stride) % self.count) for at in range(self.count)]
        return lax.ppermute(values, "dp", pairs)

    def order(self, index, width):
        rows = width // self.count
        column = jnp.arange(width)
        block = column // rows
        far = (block // self.stride - index // self.stride) % 4
        near = (block ^ index) % self.stride
        target = (near * 4 + far) * rows + column % rows
        return (target[:, None] == column).astype(LOW)


def swap(values):
    return lax.ppermute(values, "mp", [(0, 1), (1, 0)])


def swap_all(values):
    return [swap(value) for value in values]


def gather_far(lines, shards):
    wide = jnp.concatenate(shards, 1)
    found = [wide] + [lines.shift(wide, -steps) for steps in (1, 2, 3)]
    cut = shards[0].shape[1]
    return [jnp.stack([block[:, :cut] for block in found]), jnp.stack([block[:, cut:] for block in found])]


def gather_near(lines, held, phase):
    results = []
    for values, order in zip(held, lines.orders):
        done = list(order[: lines.turn]) if phase else []
        for bit in order[lines.turn :] if phase else order[: lines.turn]:
            axis = sum(1 for other in done if other > bit)
            values = jnp.stack([values, lines.flip(values, bit)], axis)
            done.append(bit)
        results.append(values)
    return results


def flat(values):
    return values.reshape(-1, values.shape[-1])


class Terms:
    def __init__(self, lines, own, other, order, rows):
        self.lines, self.order, self.left, self.rows = lines, order, list(lines.bits), rows
        self.terms = [[own, []]]
        self.other = other

    def shaped(self, values):
        return values.reshape((2,) * len(self.lines.bits) + (4, self.rows, values.shape[-1]))

    def total(self, *last):
        found = None
        for values, axes, *_ in self.terms:
            for axis, at in [(axis, 0) for axis in axes] + list(last):
                values = lax.index_in_dim(values, at, axis, keepdims=False)
            values = values.astype(WIDE)
            found = values if found is None else found + values
        return found

    def swap(self):
        self.terms = [[self.shaped(self.terms[0][0]), [], True], [self.shaped(swap(self.other)), []]]
        self.other = None

    def near(self, phase):
        turn = self.lines.turn
        for bit in self.order[turn:] if phase else self.order[:turn]:
            axis = sum(1 for other in self.left if other > bit)
            self.left.remove(bit)
            got = self.lines.flip(self.total((axis, 1)).astype(LOW), bit)
            for term in self.terms:
                term[1].append(axis)
            self.terms.append([got, []])

    def far(self):
        got = [
            self.lines.shift(self.total((0, steps)).astype(LOW), steps) for steps in (1, 2, 3)
        ]
        for term in self.terms:
            term[1].append(0)
        self.terms += [[values, []] for values in got]

    def hold(self):
        self.fresh = [term for term in self.terms if len(term) == 2]
        return [term[0] for term in self.fresh] + ([] if self.other is None else [self.other])

    def keep(self, values):
        for term, value in zip(self.fresh, values):
            term[0] = value
            term.append(True)
        if self.other is not None:
            self.other = values[-1]


class Sums:
    def __init__(self, lines, own, other, rows):
        self.parts = [
            Terms(lines, mine, rest, order, rows)
            for mine, rest, order in zip(own, other, lines.orders)
        ]

    def swap(self):
        for part in self.parts:
            part.swap()

    def near(self, phase):
        for part in self.parts:
            part.near(phase)

    def far(self):
        for part in self.parts:
            part.far()

    def hold(self):
        return [part.hold() for part in self.parts]

    def keep(self, values):
        for part, value in zip(self.parts, values):
            part.keep(value)

    def results(self):
        return [part.total() for part in self.parts]


def fence_sums(sums, *values):
    held, values = lax.optimization_barrier(([one.hold() for one in sums], values))
    for one, value in zip(sums, held):
        one.keep(value)
    return values


def reduce_swap(own, other):
    return [
        (mine.astype(WIDE) + swap(rest).astype(WIDE)).astype(LOW)
        for mine, rest in zip(own, other)
    ]


def fence(*values):
    return lax.optimization_barrier(values)


def adam(weight, moment_one, moment_two, gradient, decay, rate):
    moment_one = BETA_ONE * moment_one + (1.0 - BETA_ONE) * gradient
    moment_two = BETA_TWO * moment_two + (1.0 - BETA_TWO) * gradient * gradient
    fixed_one = moment_one / (1.0 - BETA_ONE**STEP)
    fixed_two = moment_two / (1.0 - BETA_TWO**STEP)
    weight = weight - rate * (fixed_one / (jnp.sqrt(fixed_two) + EPSILON) + decay * weight)
    return [weight, moment_one, moment_two]


def two_parts(values):
    high = lax.reduce_precision(values, 8, 7)
    return jnp.concatenate([high, values - high], 1).astype(LOW)


def widen_rows(values, rows):
    return jnp.pad(values, ((0, rows - values.shape[0]), (0, 0)))


def shards(
    patches,
    ctx_index,
    tgt_index,
    group,
    tgt_count,
    embed,
    embed_m,
    embed_v,
    bridge,
    bridge_m,
    bridge_v,
    enc_in,
    enc_in_m,
    enc_in_v,
    enc_out,
    enc_out_m,
    enc_out_v,
    enc_gains,
    enc_gains_m,
    enc_gains_v,
    pred_in,
    pred_in_m,
    pred_in_v,
    pred_out,
    pred_out_m,
    pred_out_v,
    pred_gains,
    pred_gains_m,
    pred_gains_v,
    t_embed,
    t_in,
    t_out,
    t_gains,
):
    index = lax.axis_index("dp")
    side = lax.axis_index("mp")
    dp_count = lax.axis_size("dp")
    lines = Lines(dp_count)
    assert patches.shape[0] == lax.axis_size("mp")
    count = patches.shape[0] * dp_count * TGT * D
    rows = D // dp_count
    p_rows = PW // dp_count
    half_d = D // 2
    local = D // 2
    ff = enc_in.shape[1] - 3 * local
    p_local = PW // 2
    p_ff = pred_in.shape[1] - 3 * p_local
    first = side == 0
    size = D // HEADS
    p_size = PW // PHEADS

    def own_half(values):
        return lax.dynamic_slice_in_dim(values, side * half_d, half_d, 1).astype(LOW)

    gains_pack = jnp.concatenate(
        [
            two_parts(enc_gains.T),
            two_parts(t_gains.T),
            widen_rows(two_parts(pred_gains.T), rows),
            jnp.zeros((rows, LANES - 38), LOW),
        ],
        1,
    )
    enc_in_low, t_in_low = enc_in.astype(LOW), t_in.astype(LOW)
    enc_out_low, t_out_low = enc_out.T.astype(LOW), t_out.T.astype(LOW)
    pred_in_low, pred_out_low = pred_in.astype(LOW), pred_out.T.astype(LOW)
    pred_main = jnp.concatenate([pred_out_low[:, p_local:], pred_in_low[:, 3 * p_local :]], 0)
    pred_rest = jnp.concatenate(
        [
            pred_in_low[:, : 2 * p_local],
            jnp.concatenate(
                [pred_in_low[:, 2 * p_local : 3 * p_local], pred_out_low[:, :p_local]], 1
            ),
        ],
        0,
    )
    packs = [
        [
            enc_in_low[:, : 3 * local],
            jnp.concatenate([own_half(embed), enc_out_low[:, :local], gains_pack], 1),
        ],
        [enc_in_low[:, 3 * local :], enc_out_low[:, local:]],
        [
            jnp.concatenate(
                [t_in_low[:, : 3 * local], own_half(t_embed), t_out_low[:, :local]], 1
            ),
            jnp.concatenate([own_half(bridge), pred_main, pred_rest], 1),
        ],
        [t_in_low[:, 3 * local :], t_out_low[:, local:]],
    ]

    order = lines.order(index, D)
    p_order = lines.order(index, PW)
    eye = jnp.eye(D, dtype=LOW)
    patch = lax.dynamic_index_in_dim(patches, side, 0, keepdims=False)
    ctx = lax.dynamic_index_in_dim(ctx_index, side, 0, keepdims=False)
    tgt = lax.dynamic_index_in_dim(tgt_index, side, 0, keepdims=False)
    single = lax.dynamic_index_in_dim(group, side, 0, keepdims=False) == 1
    used = lax.dynamic_index_in_dim(tgt_count, side, 0, keepdims=False)
    positions = jnp.arange(patch.shape[0])
    chosen = jnp.concatenate([ctx, tgt])
    all_id, all_row, all_col = place(single, positions)
    joined_id, joined_row, joined_col = place(single, chosen)
    ctx_id, tgt_id = joined_id[:CTX], joined_id[CTX:]

    far_a = gather_far(lines, packs[0])
    pos_all = sincos(all_row, all_col, D, order)
    pos_joined = sincos(joined_row, joined_col, D, order)
    pos_small = sincos(joined_row, joined_col, PW, p_order)
    patch = mm(patch, order).astype(LOW)
    seen = mm((chosen[:, None] == positions).astype(LOW), patch).astype(LOW)
    far_a, packs[1] = fence(far_a, packs[1])
    near_a = gather_near(lines, far_a, 0)
    near_a, packs[1] = fence(near_a, packs[1])
    held_a = gather_near(lines, near_a, 1)
    far_b = gather_far(lines, packs[1])
    held_a, far_b, pos_all, pos_joined, pos_small, patch, seen, packs[2] = fence(
        held_a, far_b, pos_all, pos_joined, pos_small, patch, seen, packs[2]
    )
    other_a = swap_all(held_a)
    near_b = gather_near(lines, far_b, 0)
    held_a, other_a, near_b, packs[2] = fence(held_a, other_a, near_b, packs[2])

    def widths(values, *sizes):
        found, at = [], 0
        for wide in sizes:
            found.append(values[:, at : at + wide])
            at += wide
        return found

    enc_qkv = (flat(held_a[0]), flat(other_a[0]))
    enc_rest = (flat(held_a[1]), flat(other_a[1]))
    gains_w = enc_rest[0][:, 2 * local :]
    gains_wide = gains_w.astype(WIDE)
    enc_gain = (gains_wide[:, 0:6] + gains_wide[:, 6:12]).T
    target_gain = (gains_wide[:, 12:18] + gains_wide[:, 18:24]).T
    pred_wide = gains_wide.reshape(dp_count, rows, LANES)[:, :p_rows].reshape(PW, LANES)
    pred_gain = (pred_wide[:, 24:31] + pred_wide[:, 31:38]).T
    order_own = lax.dynamic_slice_in_dim(order, side * half_d, half_d, 0)
    order_other = lax.dynamic_slice_in_dim(order, (1 - side) * half_d, half_d, 0)

    held_b = gather_near(lines, near_b, 1)
    far_c = gather_far(lines, packs[2])
    start, normed_one, middle, normed_two, *pairs = ctx_forward(
        size,
        seen[:CTX],
        pos_joined[:CTX],
        enc_gain,
        ctx_id,
        (order_own, order_other),
        enc_rest,
        enc_qkv,
    )
    projected, mixed = pairs[:2], pairs[2:]
    held_b, far_c, normed_two, middle, packs[3] = fence(
        held_b, far_c, normed_two, middle, packs[3]
    )
    other_b = swap_all(held_b)
    near_c = gather_near(lines, far_c, 0)
    held_b, other_b, near_c, packs[3] = fence(held_b, other_b, near_c, packs[3])
    held_c = gather_near(lines, near_c, 1)
    far_d = gather_far(lines, packs[3])
    enc_up, enc_down = [(flat(own), flat(other)) for own, other in zip(held_b, other_b)]
    hidden, context, *pairs = ff_forward(
        normed_two, middle, enc_gain, enc_up, enc_down
    )
    activated, slope = pairs[:2], pairs[2:]
    held_c, far_d, hidden, context, activated, slope = fence(
        held_c, far_d, hidden, context, activated, slope
    )
    other_c = swap_all(held_c)
    near_d = gather_near(lines, far_d, 0)
    held_c, other_c, near_d = fence(held_c, other_c, near_d)
    held_d = gather_near(lines, near_d, 1)
    t_middle, t_two = target_forward(
        size,
        patch,
        seen[CTX:],
        pos_all,
        pos_joined[CTX:],
        target_gain,
        tgt_id,
        all_id,
        (order_own, order_other),
        (flat(held_c[0]), flat(other_c[0])),
    )
    held_d, t_two, t_middle = fence(held_d, t_two, t_middle)
    other_d = swap_all(held_d)

    pred_all = [flat(part[1]) for part in (held_c, other_c)]
    bridges = [part[:, :local] for part in pred_all]
    main = [part[:, local : 3 * local].reshape(dp_count, 2, p_rows, -1) for part in pred_all]
    rest = [part[:, 3 * local :].reshape(dp_count, 2, p_rows, -1) for part in pred_all]
    bridge_in = mm(jnp.where(first, bridges[0], bridges[1]), p_order).astype(LOW)
    bridge_out = mm(jnp.where(first, bridges[1], bridges[0]), p_order).astype(LOW)
    pred_down = [flat(part[:, 0]) for part in main]
    pred_up = [flat(part[:, 1]) for part in main]
    pred_qk = [flat(part[:, 0]) for part in rest]
    pred_right = [flat(part[:, 1]) for part in rest]
    (
        joined,
        p_normed_one,
        p_middle,
        p_normed_two,
        predicted,
        final,
        guess,
        *pairs,
    ) = pred_forward(
        p_size,
        context,
        bridge_in,
        bridge_out,
        pos_small,
        pred_gain,
        tgt_id,
        joined_id,
        pred_down,
        pred_up,
        pred_qk,
        pred_right,
    )
    p_qk, p_values, p_mixed, p_activated, p_slope = [
        pairs[at : at + 2] for at in range(0, 10, 2)
    ]
    other_d, guess = fence(other_d, guess)
    target = target_ff(
        t_two,
        t_middle,
        target_gain,
        (flat(held_d[0]), flat(other_d[0])),
        (flat(held_d[1]), flat(other_d[1])),
    )
    (
        loss_local,
        d_inward,
        grad_bridge_in,
        grad_bridge_out,
        sums_pred,
        *pairs,
    ) = pred_back_all(
        p_size,
        count,
        used[None],
        [
            guess,
            target,
            context,
            final,
            bridge_in,
            bridge_out,
            pred_gain,
            predicted,
            p_middle,
            joined,
            p_normed_one,
            p_normed_two,
        ],
        [
            pred_down,
            pred_up,
            pred_qk,
            pred_right,
            p_activated,
            p_slope,
            p_qk,
            p_values,
            p_mixed,
        ],
        tgt_id,
        joined_id,
    )
    loss_local = loss_local[0, 0]
    grads_left, grads_right = pairs[:2], pairs[2:]

    def blocks(values):
        return values.reshape(dp_count, p_rows, -1)

    bridge_pair = [
        mm_t(jnp.where(first, low, high), p_order).astype(LOW).reshape(dp_count, rows, -1)
        for low, high in (
            (grad_bridge_in, grad_bridge_out),
            (grad_bridge_out, grad_bridge_in),
        )
    ]
    pair_p = [
        [
            jnp.concatenate([blocks(grads_left[at]), bridge_pair[at][:, :p_rows]], 2),
            jnp.concatenate([blocks(grads_right[at]), bridge_pair[at][:, p_rows:]], 2),
        ]
        for at in (0, 1)
    ]
    sum_p = Sums(lines, *pair_p, p_rows)
    (d_inward,) = fence_sums([sum_p], d_inward)
    sum_p.swap()
    *pairs, branch, d_middle, sums_ff = ff_back(
        d_inward,
        bridge_in,
        hidden,
        middle,
        normed_two,
        eye,
        enc_gain,
        activated,
        slope,
        enc_up,
        enc_down,
    )
    sum_f = Sums(lines, pairs[0:2], pairs[2:4], rows)
    branch, d_middle = fence_sums([sum_p, sum_f], branch, d_middle)
    sum_p.near(0)
    sum_f.swap()
    d_proj = attn_back(size, branch, ctx_id, enc_rest, projected)
    (d_proj,) = fence_sums([sum_p, sum_f], d_proj)
    sum_p.near(1)
    sum_f.near(0)
    spread = jnp.arange(D) // rows * p_rows + jnp.arange(D) % rows
    spread = (jnp.arange(PW)[:, None] == spread) & (jnp.arange(D) % rows < p_rows)
    qkv_own, qkv_other, rest_own, rest_other = qkv_back(
        branch,
        d_middle,
        start,
        normed_one,
        seen[:CTX],
        eye,
        enc_gain,
        sums_ff,
        sums_pred,
        spread.astype(LOW),
        [d_proj, mixed, enc_qkv, (order_own, order_other)],
    )
    sum_a = Sums(lines, [qkv_own, rest_own], [qkv_other, rest_other], rows)
    fence_sums([sum_p, sum_f, sum_a])
    sum_p.far()
    sum_a.swap()
    sum_f.near(1)
    fence_sums([sum_p, sum_f, sum_a])
    sum_f.far()
    sum_a.near(0)
    fence_sums([sum_f, sum_a])
    sum_a.near(1)
    fence_sums([sum_a])
    sum_a.far()

    red_left, red_right = sum_p.results()
    red_p_down, red_p_qk, bridge_top = widths(red_left, p_ff, 2 * p_local, half_d)
    red_p_up, red_p_v, red_p_attn, bridge_low = widths(red_right, p_ff, p_local, p_local, half_d)
    red_bridge = jnp.concatenate([bridge_top, bridge_low], 0)
    red_up, red_down = sum_f.results()
    red_qkv, red_rest = sum_a.results()
    red_embed, red_attn, red_gains = widths(red_rest, half_d, local, 16)
    red_pred_gains = red_gains[:p_rows, 8:15]
    split_squares = sum(
        jnp.sum(part * part)
        for part in (red_left, red_right, red_down, red_up, red_attn, red_qkv, red_embed)
    )
    shared_squares = jnp.sum(red_gains * red_gains)
    sums = jnp.stack([split_squares + shared_squares * 0.5, loss_local])
    for bit in range(dp_count.bit_length() - 1):
        sums = sums + lines.flip(sums, bit)
    sums = sums + swap(sums)
    square_sum, loss_sum = sums[0], sums[1]
    both = jnp.concatenate([red_embed, red_bridge], 1)
    both_other = swap(both)
    low = jnp.where(first, both, both_other)
    high = jnp.where(first, both_other, both)
    full_embed = jnp.concatenate([low[:, :half_d], high[:, :half_d]], 1)
    full_bridge = jnp.concatenate([low[:, half_d:], high[:, half_d:]], 1)
    grad_norm = jnp.sqrt(square_sum)
    factor = jnp.minimum(1.0, CLIP_NORM / (grad_norm + 1e-06))
    reduced = (
        full_embed,
        full_bridge,
        jnp.concatenate([red_qkv, red_up], 1),
        jnp.concatenate([red_attn, red_down], 1).T,
        red_gains[:, :6].T,
        jnp.concatenate([red_p_qk, red_p_v, red_p_up], 1),
        jnp.concatenate([red_p_attn, red_p_down], 1).T,
        red_pred_gains.T,
    )
    masters = (embed, bridge, enc_in, enc_out, enc_gains, pred_in, pred_out, pred_gains)
    firsts = (
        embed_m,
        bridge_m,
        enc_in_m,
        enc_out_m,
        enc_gains_m,
        pred_in_m,
        pred_out_m,
        pred_gains_m,
    )
    seconds = (
        embed_v,
        bridge_v,
        enc_in_v,
        enc_out_v,
        enc_gains_v,
        pred_in_v,
        pred_out_v,
        pred_gains_v,
    )
    results = []
    for index_pos in range(8):
        is_gain = index_pos in (4, 7)
        decay = 0.0 if is_gain else WEIGHT_DECAY
        rate = GAIN_RATE if is_gain else LEARN_RATE
        results.extend(
            adam(
                masters[index_pos],
                firsts[index_pos],
                seconds[index_pos],
                reduced[index_pos] * factor,
                decay,
                rate,
            )
        )
    return (
        results[0],
        results[1],
        results[2],
        results[3],
        results[4],
        results[5],
        results[6],
        results[7],
        results[8],
        results[9],
        results[10],
        results[11],
        results[12],
        results[13],
        results[14],
        results[15],
        results[16],
        results[17],
        results[18],
        results[19],
        results[20],
        results[21],
        results[22],
        results[23],
        loss_sum,
        grad_norm,
    )


def solution(mesh):
    in_specs = (
        P("dp", None, None),
        P("dp", None),
        P("dp", None),
        P("dp"),
        P("dp"),
        P("dp", None),
        P("dp", None),
        P("dp", None),
        P("dp", None),
        P("dp", None),
        P("dp", None),
        P("dp", "mp"),
        P("dp", "mp"),
        P("dp", "mp"),
        P("mp", "dp"),
        P("mp", "dp"),
        P("mp", "dp"),
        P(None, "dp"),
        P(None, "dp"),
        P(None, "dp"),
        P("dp", "mp"),
        P("dp", "mp"),
        P("dp", "mp"),
        P("mp", "dp"),
        P("mp", "dp"),
        P("mp", "dp"),
        P(None, "dp"),
        P(None, "dp"),
        P(None, "dp"),
        P("dp", None),
        P("dp", "mp"),
        P("mp", "dp"),
        P(None, "dp"),
    )
    out_specs = (
        P("dp", None),
        P("dp", None),
        P("dp", None),
        P("dp", None),
        P("dp", None),
        P("dp", None),
        P("dp", "mp"),
        P("dp", "mp"),
        P("dp", "mp"),
        P("mp", "dp"),
        P("mp", "dp"),
        P("mp", "dp"),
        P(None, "dp"),
        P(None, "dp"),
        P(None, "dp"),
        P("dp", "mp"),
        P("dp", "mp"),
        P("dp", "mp"),
        P("mp", "dp"),
        P("mp", "dp"),
        P("mp", "dp"),
        P(None, "dp"),
        P(None, "dp"),
        P(None, "dp"),
        P(),
        P(),
    )
    return jax.shard_map(shards, mesh=mesh, in_specs=in_specs, out_specs=out_specs, check_vma=False)
```

```python
import functools
import itertools

import jax
import jax.numpy as jnp
from jax import lax
from jax.experimental import pallas as pl
from jax.experimental.pallas import tpu as pltpu
from jax.sharding import PartitionSpec as P

D = 768
HEADS = 12
PW = 384
PHEADS = 12
SIDE = 14
SMALLP = 196
CTX = 512
TGT = 256
STEP = 10


LOW = jnp.bfloat16
WIDE = jnp.float32
CLIP_NORM = 0.0005
LEARN_RATE = 0.05
GAIN_RATE = 1.0
BETA_ONE = 0.9
BETA_TWO = 0.999
EPSILON = 1e-08
WEIGHT_DECAY = 0.05


LANES = 128


def norm_rows(values, gain_row, shift_row):
    centred = values - jnp.mean(values, -1, keepdims=True)
    spread = jnp.mean(centred * centred, -1, keepdims=True)
    return centred * lax.rsqrt(spread + 1e-06) * gain_row + shift_row


def norm_back(values, gain_row, grad):
    centred = values - jnp.mean(values, -1, keepdims=True)
    rstd = lax.rsqrt(jnp.mean(centred * centred, -1, keepdims=True) + 1e-06)
    unit = centred * rstd
    scaled = grad * gain_row
    d_values = rstd * (
        scaled
        - jnp.mean(scaled, -1, keepdims=True)
        - unit * jnp.mean(scaled * unit, -1, keepdims=True)
    )
    return d_values, jnp.sum(grad * unit, 0), jnp.sum(grad, 0)


def gelu_parts(pre):
    bell = jnp.exp(-0.5 * pre * pre)
    turn = 1.0 / (1.0 + 0.3275911 * 0.7071067811865476 * jnp.abs(pre))
    series = 0.5 * 1.061405429
    for factor in (-1.453152027, 1.421413741, -0.284496736, 0.254829592):
        series = series * turn + 0.5 * factor
    tail = series * turn * bell
    return jnp.where(pre < 0.0, tail, 1.0 - tail), bell * 0.3989422804014327


def gelu_both(pre):
    phi, density = gelu_parts(pre)
    return (pre * phi).astype(LOW), (phi + pre * density).astype(LOW)


def place(single, positions):
    image_id = jnp.where(single, 0, positions // SMALLP)
    within = jnp.where(single, positions, positions % SMALLP)
    side_len = jnp.where(single, 2 * SIDE, SIDE)
    return (image_id, within // side_len, within % side_len)


def three_parts(values):
    high = lax.reduce_precision(values, 8, 7)
    rest = values - high
    middle = lax.reduce_precision(rest, 8, 7)
    return jnp.concatenate([high, middle, rest - middle], 0).astype(LOW)


def sincos(row_pos, col_pos, width, order):
    quarter = width // 4
    omega = 10000.0 ** (-jnp.arange(quarter).astype(WIDE) / quarter)
    steps = jnp.arange(2 * SIDE)
    angle = steps.astype(WIDE)[:, None] * omega
    table = jnp.concatenate([jnp.sin(angle), jnp.cos(angle)], -1)
    blank = jnp.zeros_like(table)
    table = jnp.concatenate(
        [jnp.concatenate([table, blank], 1), jnp.concatenate([blank, table], 1)], 0
    )
    parts = three_parts(table)
    if order is not None:
        parts = mm(parts, order).astype(LOW)
    pick = jnp.concatenate([row_pos[:, None] == steps, col_pos[:, None] == steps], 1)
    pick = pick.astype(LOW)
    return mm(jnp.concatenate([pick, pick, pick], 1), parts)


def mm(left, right):
    return jnp.dot(left, right, preferred_element_type=WIDE)


def mm_t(left, right):
    return lax.dot_general(left, right, (((1,), (1,)), ((), ())), preferred_element_type=WIDE)


def t_mm(left, right):
    return lax.dot_general(left, right, (((0,), (0,)), ((), ())), preferred_element_type=WIDE)


SPAN = 64


def head_forward(query, keys, values, bias_ref, size):
    scale = size**-0.5
    scores = mm_t(keys, query) + bias_ref[...]
    highest = jnp.max(scores, 0, keepdims=True)
    soft = jnp.exp((scores - highest) * scale)
    total = jnp.sum(soft, 0, keepdims=True)
    return (t_mm(values, soft.astype(LOW)) / total).T, highest * scale + jnp.log(total)


def head_backward(query, keys, values, d_out, mixed, logs, bias_ref, soft_ref, ds_ref, size):
    scale = size**-0.5
    count = keys.shape[0]
    row_sum = jnp.sum((d_out.astype(WIDE) * mixed.astype(WIDE)).T, 0, keepdims=True)
    for low in range(0, count, SPAN):
        high = low + SPAN
        scores = mm_t(keys[low:high], query) + bias_ref[low:high, :]
        soft = jnp.exp(scores * scale - logs)
        d_soft = mm_t(values[low:high], d_out)
        soft_ref[low:high, :] = soft.astype(LOW)
        ds_ref[low:high, :] = (soft * (d_soft - row_sum)).astype(LOW)
    d_values = mm(soft_ref[...], d_out)
    d_keys = mm(ds_ref[...], query) * scale
    d_query = (t_mm(keys, ds_ref[...]) * scale).T
    return d_query.astype(LOW), d_keys.astype(LOW), d_values.astype(LOW)


WHOLE = pl.BlockSpec(memory_space=pltpu.VMEM)
CHUNK = 64
MARGIN = 6 * 2**20


def room(values, margin=MARGIN):
    total = 0
    for value in values:
        rows, cols = value.shape[-2], value.shape[-1]
        cells = value.size // (rows * cols) * (-(-rows // 16) * 16) * (-(-cols // LANES) * LANES)
        total += cells * jnp.dtype(value.dtype).itemsize
    return min(total + margin, 58 * 2**20)


def streamed(kernel, counts, late, early, *refs):
    n_in, n_out, n_scratch = counts
    ins, outs = list(refs[:n_in]), list(refs[n_in : n_in + n_out])
    scratch = refs[n_in + n_out : n_in + n_out + n_scratch]
    extra = refs[n_in + n_out + n_scratch :]
    arriving, leaving, left = {}, {}, []
    for at, which in enumerate(late):
        arriving[which] = pltpu.make_async_copy(ins[which], extra[at], extra[-1].at[at])
        arriving[which].start()
        ins[which] = extra[at]
    for at, which in enumerate(early, len(late)):
        leaving[which] = pltpu.make_async_copy(extra[at], outs[which], extra[-1].at[at])
        outs[which] = extra[at]

    def need(*those):
        for which in those:
            arriving.pop(which).wait()

    def ship(*those):
        for which in those:
            copy = leaving.pop(which)
            copy.start()
            left.append(copy)

    kernel(need, ship, *ins, *outs, *scratch)
    need(*list(arriving))
    ship(*list(leaving))
    for copy in left:
        copy.wait()


def on_chip(kernel, ins, outs, scratch, macs, exps=0, ahead=False, late=(), early=()):
    outs = [jax.ShapeDtypeStruct(shape, kind) for shape, kind in outs]
    held = [jax.ShapeDtypeStruct(shape, kind) for shape, kind in scratch]
    moved = sum(value.size * value.dtype.itemsize for value in list(ins) + outs)
    buffers = [pltpu.VMEM(shape, kind) for shape, kind in scratch]
    in_specs, out_specs = [WHOLE] * len(ins), [WHOLE] * len(outs)
    if late or early:
        counts = len(ins), len(outs), len(scratch)
        kernel = functools.partial(streamed, kernel, counts, late, early)
        for which in late:
            in_specs[which] = pl.BlockSpec(memory_space=pl.ANY)
            buffers.append(pltpu.VMEM(ins[which].shape, ins[which].dtype))
        for which in early:
            out_specs[which] = pl.BlockSpec(memory_space=pl.ANY)
            buffers.append(pltpu.VMEM(outs[which].shape, outs[which].dtype))
        buffers.append(pltpu.SemaphoreType.DMA((len(late) + len(early),)))
    return pl.pallas_call(
        kernel,
        in_specs=in_specs,
        out_specs=out_specs,
        out_shape=outs,
        scratch_shapes=buffers,
        cost_estimate=pl.CostEstimate(flops=2 * macs, bytes_accessed=moved, transcendentals=exps),
        compiler_params=pltpu.CompilerParams(
            vmem_limit_bytes=room(list(ins) + outs + held) if ahead else 58 * 2**20
        ),
    )(*ins)


def tiles(count, width, body):
    def step(at, carry):
        body(pl.ds(pl.multiple_of(at * width, width), width))
        return carry

    lax.fori_loop(0, count // width, step, 0)


def norm_back_rows(values_ref, grad_ref, gain, write, sums_ref, at):
    rows, width = values_ref.shape

    def step(number, carry):
        span = pl.ds(pl.multiple_of(number * CHUNK, CHUNK), CHUNK)
        values, grad = values_ref[span, :], grad_ref[span, :]
        centred = values - jnp.mean(values, -1, keepdims=True)
        rstd = lax.rsqrt(jnp.mean(centred * centred, -1, keepdims=True) + 1e-06)
        unit = centred * rstd
        scaled = grad * gain
        d_values = rstd * (
            scaled
            - jnp.mean(scaled, -1, keepdims=True)
            - unit * jnp.mean(scaled * unit, -1, keepdims=True)
        )
        write(span, d_values)
        return (
            carry[0] + jnp.sum(grad * unit, 0, keepdims=True),
            carry[1] + jnp.sum(grad, 0, keepdims=True),
        )

    blank = jnp.zeros((1, width), WIDE)
    gains, shifts = lax.fori_loop(0, rows // CHUNK, step, (blank, blank))
    sums_ref[at : at + 1, :] = gains
    sums_ref[at + 1 : at + 2, :] = shifts


def ff_back_kernel(need, ship, *refs):
    (d_inward, bridge_in, hidden, middle, normed, order, gains) = refs[0:7]
    acts, slopes, ups, downs = refs[7:9], refs[9:11], refs[11:13], refs[13:15]
    grads, branch_out, d_middle, sums = refs[15:17], refs[17], refs[18], refs[19]
    grad, d_hidden, branch, branch_t, normed_t, d_pre = refs[20:26]
    ff = acts[0].shape[1]
    wide = 768

    def first(span):
        grad[:, span] = mm_t(d_inward[...], bridge_in[span, :])

    tiles(D, wide, first)

    def write_hidden(span, values):
        d_hidden[span, :] = values
        branch[span, :] = values.astype(LOW)

    norm_back_rows(hidden, grad, gains[4:5, :], write_hidden, sums, 0)
    need(5, 4)
    branch_t[...] = mm_t(order[...], branch[...]).astype(LOW)
    normed_t[...] = mm_t(order[...], normed[...]).astype(LOW)
    for side in (0, 1):
        need(7 + side, 9 + side, 13 + side)
        act, slope, down = acts[side], slopes[side], downs[side]
        out = grads[side]

        def second(span, act=act, slope=slope, down=down, out=out, side=side):
            d_act = mm(branch[...], down[:, span])
            values = (d_act * slope[:, span].astype(WIDE)).astype(LOW)
            d_pre[side, :, span] = values
            out[:, span] = mm(normed_t[...], values).astype(LOW)
            lower = pl.ds(pl.multiple_of(span.start + ff, LANES), span.size)
            out[:, lower] = mm(branch_t[...], act[:, span]).astype(LOW)

        tiles(ff, wide, second)
        ship(side)

    need(11, 12)

    def third(span):
        grad[:, span] = mm_t(d_pre[0], ups[0][span, :]) + mm_t(d_pre[1], ups[1][span, :])

    tiles(D, wide, third)

    def write_middle(span, values):
        values = values + d_hidden[span, :]
        d_middle[span, :] = values
        branch_out[span, :] = values.astype(LOW)

    need(3)
    norm_back_rows(middle, grad, gains[2:3, :], write_middle, sums, 2)


def ff_back(d_inward, bridge_in, hidden, middle, normed, order, gains, acts, slopes, ups, downs):
    rows, ff = acts[0].shape
    return on_chip(
        ff_back_kernel,
        [d_inward, bridge_in, hidden, middle, normed, order, gains]
        + [*acts, *slopes, *ups, *downs],
        [((D, 2 * ff), LOW)] * 2 + [((rows, D), LOW), ((rows, D), WIDE), ((8, D), WIDE)],
        [((rows, D), WIDE)] * 2
        + [((rows, D), LOW), ((D, rows), LOW), ((D, rows), LOW), ((2, rows, ff), LOW)],
        8 * rows * D * ff,
        late=(5, 4, 13, 9, 7, 14, 10, 8, 11, 12, 3),
        early=(0, 1),
    )


def attn_back_kernel(size, branch, ids_row, ids_col, *refs):
    rests, projs, mixeds, logs, d_projs = refs[0:2], refs[2:4], refs[4:6], refs[6:8], refs[8:10]
    d_mixed, bias, soft, d_scores = refs[10:14]
    width = D // 2
    bias[...] = jnp.where(ids_col[...] == ids_row[...], 0.0, -1e30)
    for side in (0, 1):
        proj, mixed, log, d_proj = projs[side], mixeds[side], logs[side], d_projs[side]
        d_mixed[...] = mm(branch[...], rests[side][:, width : 2 * width]).astype(LOW)

        def step(block, carry, proj=proj, mixed=mixed, log=log, d_proj=d_proj):
            at = [pl.multiple_of(part * width + block * LANES, LANES) for part in range(3)]
            query, keys, values = [proj[:, pl.ds(col, LANES)] for col in at]
            d_out = d_mixed[:, pl.ds(at[0], LANES)]
            out = mixed[:, pl.ds(at[0], LANES)]
            found = []
            for number, low in enumerate(range(0, LANES, size)):
                cols = slice(low, low + size)
                found.append(
                    head_backward(
                        query[:, cols],
                        keys[:, cols],
                        values[:, cols],
                        d_out[:, cols],
                        out[:, cols],
                        log[number, pl.ds(block, 1), :],
                        bias,
                        soft,
                        d_scores,
                        size,
                    )
                )
            for col, parts in zip(at, zip(*found)):
                d_proj[:, pl.ds(col, LANES)] = jnp.concatenate(parts, -1)
            return carry

        lax.fori_loop(0, width // LANES, step, 0)


def attn_back(size, branch, ids, rests, projs, mixeds, logs):
    rows = branch.shape[0]
    return on_chip(
        functools.partial(attn_back_kernel, size),
        [branch, ids[None, :], ids[:, None], *rests, *projs, *mixeds, *logs],
        [(projs[0].shape, LOW)] * 2,
        [
            ((rows, D // 2), LOW),
            ((rows, rows), WIDE),
            ((rows, rows), LOW),
            ((rows, rows), LOW),
        ],
        rows * D * D + rows * rows * D * 5,
        rows * rows * D // size,
        ahead=True,
    )


def qkv_back_kernel(need, ship, *refs):
    branch, d_middle, start, normed, seen, eye, gains, sums_ff, sums_p, spread = refs[0:10]
    d_projs, mixeds, qkvs, orders = refs[10:12], refs[12:14], refs[14:16], refs[16:18]
    outs = refs[18:20]
    grad, flipped, d_start, sums = refs[20:24]
    width = D // 2
    rest = 3 * width
    flipped[...] = mm_t(eye[...], branch[...]).astype(LOW)
    need(12, 13)
    for side in (0, 1):
        outs[side][:, rest + width : rest + 2 * width] = mm(
            flipped[...], mixeds[side][...]
        ).astype(LOW)
    need(3)
    flipped[...] = mm_t(eye[...], normed[...]).astype(LOW)
    need(10, 11)
    for side in (0, 1):
        outs[side][:, 0:rest] = mm(flipped[...], d_projs[side][...]).astype(LOW)
    need(14, 15)
    grad[...] = mm_t(d_projs[0][...], qkvs[0][...]) + mm_t(d_projs[1][...], qkvs[1][...])

    def write(span, values):
        d_start[span, :] = (values + d_middle[span, :]).astype(LOW)

    need(1, 2)
    norm_back_rows(start, grad, gains[0:1, :], write, sums, 0)
    need(4)
    flipped[...] = mm_t(eye[...], seen[...]).astype(LOW)
    sums[2:4, :] = sums_ff[2:4, :]
    sums[4:6, :] = sums_ff[0:2, :]
    sums[6:8, :] = jnp.zeros((2, D), WIDE)
    rows = jnp.concatenate(
        [sums[...].astype(LOW), mm(sums_p[...].astype(LOW), spread[...]).astype(LOW)], 0
    )
    cols = t_mm(rows, eye[0:16, 0:LANES]).astype(LOW)
    need(16, 17)
    for side in (0, 1):
        moved = mm_t(d_start[...], orders[side][...]).astype(LOW)
        outs[side][:, rest : rest + width] = mm(flipped[...], moved).astype(LOW)
        outs[side][:, rest + 2 * width :] = cols


def qkv_back(branch, d_middle, start, normed, seen, eye, gains, sums_ff, sums_p, spread, pairs):
    rows, width = branch.shape[0], D // 2
    return on_chip(
        qkv_back_kernel,
        [branch, d_middle, start, normed, seen, eye, gains, sums_ff, sums_p, spread]
        + [value for pair in pairs for value in pair],
        [((D, 5 * width + LANES), LOW)] * 2,
        [((rows, D), WIDE), ((D, rows), LOW), ((rows, D), LOW), ((8, D), WIDE)],
        rows * D * D * 10,
        late=(12, 13, 3, 10, 11, 14, 15, 1, 2, 4, 16, 17),
    )


def row_spans(rows, chunk, body):
    def step(number, carry):
        body(pl.ds(pl.multiple_of(number * chunk, chunk), chunk))
        return carry

    lax.fori_loop(0, rows // chunk, step, 0)


def heads_forward(query_ref, keys_ref, values_ref, out_ref, logs_ref, bias, size, at):
    width = out_ref.shape[1]

    def step(block, carry):
        cols = [pl.multiple_of(first + block * LANES, LANES) for first in at]
        query = query_ref[:, pl.ds(cols[0], LANES)]
        keys = keys_ref[:, pl.ds(cols[1], LANES)]
        values = values_ref[:, pl.ds(cols[2], LANES)]
        found = []
        for number, low in enumerate(range(0, LANES, size)):
            part = slice(low, low + size)
            out, logs = head_forward(
                query[:, part], keys[:, part], values[:, part], bias, size
            )
            found.append(out)
            if logs_ref is not None:
                logs_ref[number, pl.ds(block, 1), :] = logs
        place_at = pl.ds(pl.multiple_of(block * LANES, LANES), LANES)
        out_ref[:, place_at] = jnp.concatenate(found, -1).astype(LOW)
        return carry

    lax.fori_loop(0, width // LANES, step, 0)


def ctx_first_kernel(need, ship, seen, pos, spread, *refs):
    orders, rests, qkvs = refs[0:2], refs[2:4], refs[4:6]
    start, normed, projs, outs, embed_w = refs[6], refs[7], refs[8:10], refs[10:13], refs[13]
    gains = outs[0]
    width = orders[0].shape[0]
    parts = rests[0][:, 2 * width :].astype(WIDE).T
    outs[0][...] = parts[0:8] + parts[8:16]
    outs[1][...] = parts[16:24] + parts[24:32]
    low = parts[32:48].astype(LOW)
    low = mm_t(low, spread[...])
    outs[2][...] = low[0:8] + low[8:16]
    embed_w[...] = (
        mm(rests[0][:, 0:width], orders[0][...]) + mm(rests[1][:, 0:width], orders[1][...])
    ).astype(LOW)
    need(0, 1)
    start[...] = mm(seen[...], embed_w[...]) + pos[...]
    ship(0)

    def first_norm(span):
        normed[span, :] = norm_rows(start[span, :], gains[0:1, :], gains[1:2, :]).astype(LOW)

    row_spans(seen.shape[0], CHUNK, first_norm)
    ship(1)
    for side in (0, 1):
        need(7 + side)
        projs[side][...] = mm(normed[...], qkvs[side][...]).astype(LOW)
        ship(2 + side)


def ctx_first(seen, pos, spread, orders, rests, qkvs):
    rows, width = seen.shape[0], orders[0].shape[0]
    return on_chip(
        ctx_first_kernel,
        [seen, pos, spread, *orders, *rests, *qkvs],
        [((rows, D), WIDE), ((rows, D), LOW)]
        + [((rows, 3 * width), LOW)] * 2
        + [((8, D), WIDE), ((8, D), WIDE), ((8, PW), WIDE)],
        [((D, D), LOW)],
        rows * D * D * 4 + D * D * D,
        late=(0, 1, 7, 8),
        early=(0, 1, 2, 3),
    )


def ctx_second_kernel(size, need, ship, start, gains, ids_row, ids_col, *refs):
    rests, projs = refs[0:2], refs[2:4]
    middle, normed_two, mixeds, logs, bias = refs[4], refs[5], refs[6:8], refs[8:10], refs[10]
    width = mixeds[0].shape[1]
    bias[...] = jnp.where(ids_col[...] == ids_row[...], 0.0, -1e30)
    for side in (0, 1):
        need(6 + side)
        proj = projs[side]
        heads_forward(
            proj, proj, proj, mixeds[side], logs[side], bias, size, (0, width, 2 * width)
        )
        ship(2 + side)
    need(4, 5, 0)
    middle[...] = (
        start[...]
        + mm_t(mixeds[0][...], rests[0][:, width : 2 * width])
        + mm_t(mixeds[1][...], rests[1][:, width : 2 * width])
    )

    def second_norm(span):
        normed_two[span, :] = norm_rows(middle[span, :], gains[2:3, :], gains[3:4, :]).astype(LOW)

    row_spans(start.shape[0], CHUNK, second_norm)


def ctx_second(size, start, gains, ids, rests, projs):
    rows, width = start.shape[0], D // 2
    return on_chip(
        functools.partial(ctx_second_kernel, size),
        [start, gains, ids[None, :], ids[:, None], *rests, *projs],
        [((rows, D), WIDE), ((rows, D), LOW)]
        + [((rows, width), LOW)] * 2
        + [((LANES // size, 8, rows), WIDE)] * 2,
        [((rows, rows), WIDE)],
        rows * D * D + rows * rows * D * 2,
        rows * rows * D // size,
        late=(6, 7, 4, 5, 0),
        early=(2, 3),
    )


def gelu_rows(pre_ref, act_ref, slope_ref, span):
    def body(rows):
        act, slope = gelu_both(pre_ref[rows, :])
        act_ref[rows, span] = act
        if slope_ref is not None:
            slope_ref[rows, span] = slope

    row_spans(pre_ref.shape[0], 32, body)


def ff_kernel(need, ship, *refs):
    normed, middle, gains, ups, downs = *refs[0:3], refs[3:5], refs[5:7]
    hidden, context, acts, slopes, pre = refs[7], refs[8], refs[9:11], refs[11:13], refs[13]
    rows, ff = acts[0].shape
    for side in (0, 1):
        need(3 + side)

        def first(span, side=side):
            pre[...] = mm(normed[...], ups[side][:, span])
            gelu_rows(pre, acts[side], slopes[side], span)

        tiles(ff, 512, first)
        ship(2 + side, 4 + side)
    need(5, 6, 1)
    hidden[...] = (
        middle[...] + mm_t(acts[0][...], downs[0][...]) + mm_t(acts[1][...], downs[1][...])
    )

    def last(span):
        context[span, :] = norm_rows(hidden[span, :], gains[4:5, :], gains[5:6, :]).astype(LOW)

    row_spans(rows, CHUNK, last)


def ff_forward(normed, middle, gains, ups, downs):
    rows, ff = normed.shape[0], ups[0].shape[1]
    return on_chip(
        ff_kernel,
        [normed, middle, gains, *ups, *downs],
        [((rows, D), WIDE), ((rows, D), LOW)] + [((rows, ff), LOW)] * 4,
        [((rows, 512), WIDE)],
        rows * D * ff * 4 + rows * D * D,
        rows * ff * 2,
        late=(3, 4, 5, 6, 1),
        early=(2, 3, 4, 5),
    )


def target_kernel(size, *refs):
    patch, seen, pos_all, pos_tgt, gains, ids_row, ids_col = refs[0:7]
    orders, weights, (t_middle, t_two) = refs[7:9], refs[9:11], refs[11:13]
    embed_w, hidden, normed, start, query, keys, mixed, bias = refs[13:]
    width = D // 2
    own, other = [part[:, 3 * width : 4 * width] for part in weights]
    embed_w[...] = (mm(own, orders[0][...]) + mm(other, orders[1][...])).astype(LOW)
    hidden[...] = mm(patch[...], embed_w[...]) + pos_all[...]

    def first_norm(span):
        normed[span, :] = norm_rows(hidden[span, :], gains[0:1, :], gains[1:2, :]).astype(LOW)

    row_spans(patch.shape[0], 112, first_norm)
    start[...] = mm(seen[...], embed_w[...]) + pos_tgt[...]
    t_normed = norm_rows(start[...], gains[0:1, :], gains[1:2, :]).astype(LOW)
    bias[...] = jnp.where(ids_col[...] == ids_row[...], 0.0, -1e30)
    total = start[...]
    for part in weights:
        query[...] = mm(t_normed, part[:, 0:width]).astype(LOW)
        keys[...] = mm(normed[...], part[:, width : 3 * width]).astype(LOW)
        heads_forward(query, keys, keys, mixed, None, bias, size, (0, 0, width))
        total = total + mm_t(mixed[...], part[:, 4 * width : 5 * width])
    t_middle[...] = total
    t_two[...] = norm_rows(total, gains[2:3, :], gains[3:4, :]).astype(LOW)


def target_forward(
    size, patch, seen, pos_all, pos_tgt, gains, idq, idk, orders, weights
):
    rows, count, width = seen.shape[0], patch.shape[0], D // 2
    return on_chip(
        functools.partial(target_kernel, size),
        [patch, seen, pos_all, pos_tgt, gains, idq[None, :], idk[:, None], *orders, *weights],
        [((rows, D), WIDE), ((rows, D), LOW)],
        [
            ((D, D), LOW),
            ((count, D), WIDE),
            ((count, D), LOW),
            ((rows, D), WIDE),
            ((rows, width), LOW),
            ((count, 2 * width), LOW),
            ((rows, width), LOW),
            ((count, rows), WIDE),
        ],
        count * D * D * 3 + rows * D * D * 3 + 2 * rows * count * D,
        rows * count * D // size,
        ahead=True,
    )


def pred_forward_kernel(size, *refs):
    context, bridge_in, bridge_out, pos, gains, ids_row, ids_col = refs[0:7]
    downs, ups, qks, rights = refs[7:9], refs[9:11], refs[11:13], refs[13:15]
    joined, normed, middle, normed_two, predicted, final, guess = refs[15:22]
    out_qk, out_v, mixeds, acts, slopes = (
        refs[22:24],
        refs[24:26],
        refs[26:28],
        refs[28:30],
        refs[30:32],
    )
    logs, bias = refs[32], refs[33]
    width = out_v[0].shape[1]
    joined[0:CTX, :] = mm(context[...], bridge_in[...]) + pos[0:CTX, :]
    joined[CTX:, :] = gains[6:7, :] + pos[CTX:, :]

    def first(span):
        normed[span, :] = norm_rows(joined[span, :], gains[0:1, :], gains[1:2, :]).astype(LOW)

    row_spans(joined.shape[0], 128, first)
    bias[...] = jnp.where(ids_col[...] == ids_row[...], 0.0, -1e30)
    total = joined[CTX:, :]
    head = 0
    for qk, right, qk_ref, v_ref, mixed in zip(qks, rights, out_qk, out_v, mixeds):
        qk_ref[...] = mm(normed[...], qk[...]).astype(LOW)
        v_ref[...] = mm(normed[...], right[:, 0:width]).astype(LOW)
        found = []
        for low in range(0, width, size):
            out, log = head_forward(
                qk_ref[CTX:, low : low + size],
                qk_ref[:, width + low : width + low + size],
                v_ref[:, low : low + size],
                bias,
                size,
            )
            found.append(out)
            logs[head : head + 1, :] = log
            head += 1
        mixed[...] = jnp.concatenate(found, -1).astype(LOW)
        total = total + mm_t(mixed[...], right[:, width:])
    middle[...] = total
    normed_two[...] = norm_rows(total, gains[2:3, :], gains[3:4, :]).astype(LOW)
    total = middle[...]
    for up, down, act, slope in zip(ups, downs, acts, slopes):
        values, tilt = gelu_both(mm(normed_two[...], up[...]))
        act[...] = values
        slope[...] = tilt
        total = total + mm_t(act[...], down[...])
    predicted[...] = total
    final[...] = norm_rows(total, gains[4:5, :], gains[5:6, :]).astype(LOW)
    guess[...] = mm_t(final[...], bridge_out[...])


def pred_forward(
    size, context, bridge_in, bridge_out, pos, gains, idq, idk, downs, ups, qks, rights
):
    rows, count, width, ff = idq.shape[0], idk.shape[0], qks[0].shape[1] // 2, ups[0].shape[1]
    low, wide = LOW, WIDE
    return on_chip(
        functools.partial(pred_forward_kernel, size),
        [context, bridge_in, bridge_out, pos, gains, idq[None, :], idk[:, None]]
        + [*downs, *ups, *qks, *rights],
        [((count, PW), wide), ((count, PW), low), ((rows, PW), wide), ((rows, PW), low)]
        + [((rows, PW), wide), ((rows, PW), low), ((rows, D), wide)]
        + [((count, 2 * width), low)] * 2
        + [((count, width), low)] * 2
        + [((rows, width), low)] * 2
        + [((rows, ff), low)] * 4
        + [((16, rows), wide)],
        [((count, rows), wide)],
        1_000_000_000,
        rows * count * PW // size,
    )


def target_ff_kernel(need, ship, t_two, t_middle, gains, *refs):
    ups, downs, (target, pre, act, total) = refs[0:2], refs[2:4], refs[4:8]
    total[...] = t_middle[...]
    for side in (0, 1):
        up, down = ups[side], downs[side]
        need(3 + side)

        def first(span, up=up):
            pre[...] = mm(t_two[...], up[:, span])
            gelu_rows(pre, act, None, span)

        tiles(act.shape[1], 512, first)
        need(5 + side)
        total[...] = total[...] + mm_t(act[...], down[...])
    chosen = norm_rows(total[...], gains[4:5, :], gains[5:6, :])
    target[...] = norm_rows(chosen, 1.0, 0.0)


def target_ff(t_two, t_middle, gains, ups, downs):
    rows, ff = t_two.shape[0], ups[0].shape[1]
    return on_chip(
        target_ff_kernel,
        [t_two, t_middle, gains, *ups, *downs],
        [((rows, D), WIDE)],
        [((rows, 512), WIDE), ((rows, ff), LOW), ((rows, D), WIDE)],
        rows * D * ff * 4,
        rows * ff * 2,
        late=(3, 5, 4, 6),
    )[0]


def pred_back_all_kernel(size, count_all, *refs):
    (guess, target, used, context, final, bridge_in, bridge_out, gains, ids_row, ids_col) = refs[
        0:10
    ]
    predicted, middle, joined, normed, normed_two = refs[10:15]
    downs, ups, qks, rights = refs[15:17], refs[17:19], refs[19:21], refs[21:23]
    acts, slopes, in_qk, in_v, mixeds = (
        refs[23:25],
        refs[25:27],
        refs[27:29],
        refs[29:31],
        refs[31:33],
    )
    logs = refs[33]
    loss, d_inward, g_bridge_in, g_bridge_out, sums = refs[34:39]
    g_left, g_right = refs[39:41], refs[41:43]
    d_qk, d_v, d_normed, bias, soft, d_scores = refs[43:49]
    width = in_v[0].shape[1]
    ff = acts[0].shape[1]
    diff = guess[...] - target[...]
    size_abs = jnp.abs(diff)
    keep = lax.broadcasted_iota(jnp.int32, diff.shape, 0) < used[0]
    terms = jnp.where(
        keep, jnp.where(size_abs < 1.0, 0.5 * diff * diff, size_abs - 0.5), 0.0
    )
    loss[...] = jnp.sum(jnp.sum(terms, 0, keepdims=True), 1, keepdims=True)
    d_guess = jnp.where(keep, jnp.clip(diff, -1.0, 1.0) / count_all, 0.0).astype(LOW)
    g_bridge_out[...] = t_mm(d_guess, final[...]).astype(LOW)

    def back(values, gain, grad, at):
        d_values, gain_sum, shift_sum = norm_back(values, gain, grad)
        sums[at : at + 1, :] = gain_sum[None, :]
        sums[at + 1 : at + 2, :] = shift_sum[None, :]
        return d_values

    d_tail = back(predicted[...], gains[4:5, :], mm(d_guess, bridge_out[...]), 4)
    branch = d_tail.astype(LOW)
    total = None
    for side in (0, 1):
        d_pre = (mm(branch, downs[side][...]) * slopes[side][...].astype(WIDE)).astype(LOW)
        g_left[side][:, 0:ff] = t_mm(branch, acts[side][...]).astype(LOW)
        g_right[side][:, 0:ff] = t_mm(normed_two[...], d_pre).astype(LOW)
        part = mm_t(d_pre, ups[side][...])
        total = part if total is None else total + part
    d_middle = d_tail + back(middle[...], gains[2:3, :], total, 2)
    branch = d_middle.astype(LOW)
    bias[...] = jnp.where(ids_col[...] == ids_row[...], 0.0, -1e30)
    total = None
    head = 0
    for side in (0, 1):
        qk_ref, v_ref, right = in_qk[side], in_v[side], rights[side]
        d_mixed = mm(branch, right[:, width:]).astype(LOW)
        g_right[side][:, ff + width :] = t_mm(branch, mixeds[side][...]).astype(LOW)
        found = []
        for low in range(0, width, size):
            found.append(
                head_backward(
                    qk_ref[CTX:, low : low + size],
                    qk_ref[:, width + low : width + low + size],
                    v_ref[:, low : low + size],
                    d_mixed[:, low : low + size],
                    mixeds[side][:, low : low + size],
                    logs[head : head + 1, :],
                    bias,
                    soft,
                    d_scores,
                    size,
                )
            )
            head += 1
        d_query, d_keys, d_values = [jnp.concatenate(parts, -1) for parts in zip(*found)]
        d_qk[0:CTX, 0:width] = jnp.zeros((CTX, width), LOW)
        d_qk[CTX:, 0:width] = d_query
        d_qk[:, width:] = d_keys
        d_v[...] = d_values
        g_left[side][:, ff:] = t_mm(normed[...], d_qk[...]).astype(LOW)
        g_right[side][:, ff : ff + width] = t_mm(normed[...], d_v[...]).astype(LOW)
        part = mm_t(d_qk[...], qks[side][...]) + mm_t(d_v[...], right[:, 0:width])
        d_normed[...] = part if side == 0 else d_normed[...] + part
    d_joined = back(joined[...], gains[0:1, :], d_normed[...], 0)
    sums[6:7, :] = jnp.sum(d_joined[CTX:] + d_middle, 0, keepdims=True)
    sums[7:8, :] = jnp.zeros((1, PW), WIDE)
    d_inward[...] = d_joined[0:CTX].astype(LOW)
    g_bridge_in[...] = t_mm(context[...], d_inward[...]).astype(LOW)


def pred_back_all(size, count_all, used, values, pairs, logs, idq, idk):
    (guess, target, context, final, bridge_in, bridge_out, gains) = values[:7]
    ff, width, count = pairs[0][0].shape[1], pairs[2][0].shape[1] // 2, idk.shape[0]
    ins = [guess, target, used, context, final, bridge_in, bridge_out, gains]
    ins += [idq[None, :], idk[:, None], *values[7:]] + [part for pair in pairs for part in pair]
    ins.append(logs)
    outs = [((1, 1), WIDE), ((CTX, PW), LOW), ((D, PW), LOW), ((D, PW), LOW), ((8, PW), WIDE)]
    outs += [((PW, ff + 2 * width), LOW)] * 4
    specs = [WHOLE] * len(ins)
    specs[2] = pl.BlockSpec(memory_space=pltpu.SMEM)
    return pl.pallas_call(
        functools.partial(pred_back_all_kernel, size, count_all),
        in_specs=specs,
        out_specs=[WHOLE] * len(outs),
        out_shape=[jax.ShapeDtypeStruct(shape, kind) for shape, kind in outs],
        scratch_shapes=[
            pltpu.VMEM((count, 2 * width), LOW),
            pltpu.VMEM((count, width), LOW),
            pltpu.VMEM((count, PW), WIDE),
            pltpu.VMEM((count, idq.shape[0]), WIDE),
            pltpu.VMEM((count, idq.shape[0]), LOW),
            pltpu.VMEM((count, idq.shape[0]), LOW),
        ],
        cost_estimate=pl.CostEstimate(
            flops=4_000_000_000, bytes_accessed=20_000_000, transcendentals=3_000_000
        ),
        compiler_params=pltpu.CompilerParams(vmem_limit_bytes=58 * 2**20),
    )(*ins)


def pred_parts_kernel(dp_count, side_ref, own, other, order, *outs):
    width, half = PW // 2, D // 2
    ff = D
    flip = side_ref[0] != 0
    low = jnp.where(flip, other[:, 0:half], own[:, 0:half])
    high = jnp.where(flip, own[:, 0:half], other[:, 0:half])
    outs[0][...] = mm(low, order[...]).astype(LOW)
    outs[1][...] = mm(high, order[...]).astype(LOW)
    rows = PW // dp_count
    for at, ref in enumerate((own, other)):
        for start, wide, out in ((half, ff, 2), (half + ff, 2 * width, 6)):
            blocks = ref[:, start : start + wide].astype(WIDE).reshape(dp_count, 2 * rows, wide)
            outs[out + at][...] = blocks[:, :rows].reshape(PW, wide).astype(LOW)
            outs[out + 2 + at][...] = blocks[:, rows:].reshape(PW, wide).astype(LOW)


def pred_parts(dp_count, side, own, other, order):
    width, half = PW // 2, D // 2
    if PW // dp_count % 8:
        bridges = [part[:, :half] for part in (own, other)]
        first = side == 0
        found = [
            mm(jnp.where(first, bridges[at], bridges[1 - at]), order).astype(LOW) for at in (0, 1)
        ]
        for start, wide in ((half, D), (half + D, 2 * width)):
            cols = [part[:, start : start + wide] for part in (own, other)]
            cols = [part.reshape(dp_count, 2, PW // dp_count, wide) for part in cols]
            found += [flat(part[:, which]) for which in (0, 1) for part in cols]
    else:
        ins = [side[None], own, other, order]
        shapes = [(D, PW)] * 2 + [(PW, D)] * 4 + [(PW, 2 * width)] * 4
        outs = [jax.ShapeDtypeStruct(shape, LOW) for shape in shapes]
        found = pl.pallas_call(
            functools.partial(pred_parts_kernel, dp_count),
            in_specs=[pl.BlockSpec(memory_space=pltpu.SMEM)] + [WHOLE] * 3,
            out_specs=[WHOLE] * len(outs),
            out_shape=outs,
            cost_estimate=pl.CostEstimate(
                flops=1_000_000_000, bytes_accessed=9_000_000, transcendentals=0
            ),
            compiler_params=pltpu.CompilerParams(vmem_limit_bytes=58 * 2**20),
        )(*ins)
    return found[0], found[1], [found[at : at + 2] for at in range(2, 10, 2)]


class Lines:
    def __init__(self, count):
        self.count = count
        self.stride = count // 4
        bits = list(range(self.stride.bit_length() - 1))
        turn = len(bits) // 2
        self.bits = bits
        self.orders = (bits, bits[turn:] + bits[:turn])
        self.turn = turn

    def flip(self, values, bit):
        pairs = [(at, at ^ (1 << bit)) for at in range(self.count)]
        return lax.ppermute(values, "dp", pairs)

    def shift(self, values, steps):
        pairs = [(at, (at + steps * self.stride) % self.count) for at in range(self.count)]
        return lax.ppermute(values, "dp", pairs)

    def add_all(self, values, low, high):
        total = values
        for change in range(1, 1 << (high - low)):
            pairs = [(at, at ^ (change << low)) for at in range(2 * self.count)]
            total = total + lax.ppermute(values, ("dp", "mp"), pairs)
        return total

    def order(self, index, width):
        rows = width // self.count
        column = jnp.arange(width)
        block = column // rows
        far = (block // self.stride - index // self.stride) % 4
        near = (block ^ index) % self.stride
        target = (near * 4 + far) * rows + column % rows
        return (target[:, None] == column).astype(LOW)


def swap(values):
    return lax.ppermute(values, "mp", [(0, 1), (1, 0)])


def swap_all(values):
    return [swap(value) for value in values]


def far_kernel(*refs):
    outs = refs[4:]
    cut = outs[0].shape[-1]
    for at, block in enumerate(refs[:4]):
        outs[0][at] = block[:, :cut]
        outs[1][at] = block[:, cut:]


def gather_far(lines, shards):
    wide = jnp.concatenate(shards, 1)
    found = [wide] + [lines.shift(wide, -steps) for steps in (1, 2, 3)]
    rows, cut = shards[0].shape
    cols = [slice(0, cut), slice(cut, wide.shape[1])]
    if rows % 16:
        return [jnp.stack([block[:, part] for block in found]) for part in cols]
    return on_chip(
        far_kernel,
        found,
        [((4, rows, part.stop - part.start), LOW) for part in cols],
        [],
        0,
    )


def stack_kernel(axes, *refs):
    count = len(axes)
    ins, outs, bufs, sems = refs[: 2 * count], refs[2 * count : 3 * count], refs[3 * count : -1], refs[-1]
    arriving = [
        pltpu.make_async_copy(ins[at], bufs[at], sems.at[at]) for at in range(2 * count)
    ]
    for copy in arriving:
        copy.start()
    leaving = []
    for at, copy in enumerate(arriving):
        copy.wait()
        where = (slice(None),) * axes[at % count] + (at // count,)
        out = pltpu.make_async_copy(
            bufs[at], outs[at % count].at[where], sems.at[2 * count + at]
        )
        out.start()
        leaving.append(out)
    for copy in leaving:
        copy.wait()


def stack_pairs(held, got, axes):
    anywhere = pl.BlockSpec(memory_space=pl.ANY)
    ins = [*held, *got]
    outs = [
        jax.ShapeDtypeStruct(values.shape[:axis] + (2,) + values.shape[axis:], LOW)
        for values, axis in zip(held, axes)
    ]
    return pl.pallas_call(
        functools.partial(stack_kernel, axes),
        in_specs=[anywhere] * len(ins),
        out_specs=[anywhere] * len(outs),
        out_shape=outs,
        scratch_shapes=[pltpu.VMEM(value.shape, LOW) for value in ins]
        + [pltpu.SemaphoreType.DMA((2 * len(ins),))],
        cost_estimate=pl.CostEstimate(
            flops=0, bytes_accessed=8 * sum(value.size for value in ins), transcendentals=0
        ),
        compiler_params=pltpu.CompilerParams(vmem_limit_bytes=58 * 2**20),
    )(*ins)


def gather_near(lines, held, phase):
    done = [list(order[: lines.turn]) if phase else [] for order in lines.orders]
    steps = [order[lines.turn :] if phase else order[: lines.turn] for order in lines.orders]
    for bits in zip(*steps):
        got = [lines.flip(values, bit) for values, bit in zip(held, bits)]
        axes = [sum(1 for other in had if other > bit) for had, bit in zip(done, bits)]
        if phase and held[0].shape[-2] % 16 == 0:
            held = stack_pairs(held, got, axes)
        else:
            held = [
                jnp.stack([values, other], axis) for values, other, axis in zip(held, got, axes)
            ]
        for had, bit in zip(done, bits):
            had.append(bit)
    return list(held)


def flat(values):
    return values.reshape(-1, values.shape[-1])


class Box:
    def __init__(self, value):
        self.value, self.held = value, False


def sum_kernel(plan, squares, *refs):
    operands = 1 + max(term[0] for pieces in plan for piece in pieces for term in piece)
    if squares:
        refs[-1][...] = jnp.zeros((1, LANES), WIDE)
    for pieces, out in zip(plan, refs[operands:]):
        for lead in itertools.product(*[range(size) for size in out.shape[:-2]]):
            at = 0
            for piece in pieces:
                total = None
                for operand, low, high in piece:
                    part = refs[operand][lead + (slice(None), slice(low, high))].astype(WIDE)
                    total = part if total is None else total + part
                wide = high - low
                out[lead + (slice(None), slice(at, at + wide))] = total.astype(out.dtype)
                if squares:
                    for col in range(0, wide, LANES):
                        part = total[:, col : col + LANES]
                        weight = 0.5 if at + col == squares[1] and wide == squares[0] else 1.0
                        refs[-1][...] += weight * jnp.sum(part * part, 0, keepdims=True)
                at += wide


def sum_parts(outs, kind, squares=None):
    operands, specs, plan, shapes = [], [], [], []
    known = {}
    for pieces in outs:
        row = []
        for piece in pieces:
            terms = []
            for box, taken, (low, high) in piece:
                if (id(box), taken) not in known:
                    known[id(box), taken] = len(operands)
                    value = box.value
                    block = [
                        size if pick is None else None for size, pick in zip(value.shape, taken)
                    ]
                    where = tuple(0 if pick is None else pick for pick in taken) + (0, 0)
                    operands.append(value)
                    specs.append(
                        pl.BlockSpec(
                            tuple(block) + value.shape[-2:], lambda step, where=where: where
                        )
                    )
                terms.append((known[id(box), taken], low, high))
            row.append(tuple(terms))
        plan.append(tuple(row))
        box, taken, cols = pieces[0][0]
        lead = tuple(size for size, pick in zip(box.value.shape, taken) if pick is None)
        wide = sum(piece[0][2][1] - piece[0][2][0] for piece in pieces)
        shapes.append(
            jax.ShapeDtypeStruct(lead + (box.value.shape[-2], wide), kind)
        )
    moved = 8 * sum(shape.size for shape in shapes)
    if squares:
        shapes.append(jax.ShapeDtypeStruct((1, LANES), WIDE))
    return pl.pallas_call(
        functools.partial(sum_kernel, tuple(plan), squares),
        grid=(1,),
        in_specs=specs,
        out_specs=[
            pl.BlockSpec(shape.shape, lambda step, rank=len(shape.shape): (0,) * rank)
            for shape in shapes
        ],
        out_shape=shapes,
        cost_estimate=pl.CostEstimate(flops=moved, bytes_accessed=moved, transcendentals=0),
        compiler_params=pltpu.CompilerParams(vmem_limit_bytes=58 * 2**20),
    )(*operands)


class Terms:
    def __init__(self, lines, order, cols):
        self.lines, self.order, self.cols, self.left = lines, order, cols, list(lines.bits)
        self.terms = []

    def take(self, axis, at):
        found = []
        for box, taken, cols in self.terms:
            open_axes = [place_at for place_at, pick in enumerate(taken) if pick is None]
            picked = list(taken)
            picked[open_axes[axis]] = at
            found.append((box, tuple(picked), cols))
        return found

    def near_job(self, phase):
        turn = self.lines.turn
        (self.bit,) = self.order[turn:] if phase else self.order[:turn]
        self.axis = sum(1 for other in self.left if other > self.bit)
        return self.take(self.axis, 1)

    def near_send(self, send):
        got = self.lines.flip(send, self.bit)
        self.left.remove(self.bit)
        self.terms = self.take(self.axis, 0)
        self.terms.append((Box(got), (None,) * (got.ndim - 2), (0, got.shape[-1])))


class Sums:
    def __init__(self, lines, own, other, cut, rows):
        self.lines, self.rows, self.cut = lines, rows, cut
        self.plain = len(lines.bits) != 2
        self.own, self.other = Box(own), Box(other)
        self.lead = (2,) * len(lines.bits) + (4,)
        self.wide = own.shape[-1]
        self.parts = [
            Terms(lines, order, cols)
            for order, cols in zip(lines.orders, ((0, cut), (cut, self.wide)))
        ]

    def shaped(self, values):
        return values.reshape(self.lead + (self.rows, self.wide))

    def boxes(self):
        found = [self.own, self.other]
        for part in self.parts:
            found += [term[0] for term in part.terms]
        return found

    def swap(self):
        if self.plain:
            return
        mine = Box(self.shaped(self.own.value))
        mine.held = True
        got = Box(self.shaped(swap(self.other.value)))
        for part in self.parts:
            blank = (None,) * len(self.lead)
            part.terms = [(mine, blank, part.cols), (got, blank, part.cols)]

    def far_jobs(self):
        return [[part.take(0, steps) for part in self.parts] for steps in (1, 2, 3)]

    def far_send(self, sends):
        got = [Box(self.lines.shift(send, steps)) for send, steps in zip(sends, (1, 2, 3))]
        for part in self.parts:
            part.terms = part.take(0, 0) + [(box, (), part.cols) for box in got]

    def results(self, halved=(0, -1)):
        if not self.plain:
            return sum_parts([[part.terms] for part in self.parts], WIDE, halved)
        results = []
        both = self.own.value.astype(WIDE) + swap(self.other.value).astype(WIDE)
        for part in self.parts:
            total = self.shaped(both)[..., part.cols[0] : part.cols[1]]
            for bit in part.order:
                axis = sum(1 for other in part.left if other > bit)
                part.left.remove(bit)
                sent = lax.index_in_dim(total, 1, axis, keepdims=False).astype(LOW)
                total = lax.index_in_dim(total, 0, axis, keepdims=False)
                total = total + self.lines.flip(sent, bit).astype(WIDE)
            result = total[0]
            for steps in (1, 2, 3):
                got = self.lines.shift(total[steps].astype(LOW), steps)
                result = result + got.astype(WIDE)
            results.append(result)
        squares = sum(jnp.sum(result * result) for result in results)
        for result in results:
            if result.shape[1] == halved[0]:
                part = result[:, halved[1] : halved[1] + LANES]
                squares = squares - 0.5 * jnp.sum(part * part)
        return results + [jnp.pad(squares.reshape(1, 1), ((0, 0), (0, LANES - 1)))]


def move(*steps):
    work = []
    for total, kind in steps:
        if total.plain:
            continue
        if kind == 2:
            work.append((total.far_send, total.far_jobs()))
        else:
            for part in total.parts:
                work.append((part.near_send, [[part.near_job(kind)]]))
    if not work:
        return
    sends = sum_parts([job for send, jobs in work for job in jobs], LOW)
    at = 0
    for send, jobs in work:
        found = sends[at : at + len(jobs)]
        at += len(jobs)
        send(found if len(jobs) > 1 else found[0])


def fence_sums(sums, *values):
    boxes = {id(box): box for one in sums for box in one.boxes() if not box.held}
    boxes = list(boxes.values())
    held, values = lax.optimization_barrier(([box.value for box in boxes], values))
    for box, value in zip(boxes, held):
        box.value, box.held = value, True
    return values


def fence(*values):
    return lax.optimization_barrier(values)


def adam(weight, moment_one, moment_two, gradient, decay, rate):
    moment_one = BETA_ONE * moment_one + (1.0 - BETA_ONE) * gradient
    moment_two = BETA_TWO * moment_two + (1.0 - BETA_TWO) * gradient * gradient
    fixed_one = moment_one / (1.0 - BETA_ONE**STEP)
    fixed_two = moment_two / (1.0 - BETA_TWO**STEP)
    weight = weight - rate * (fixed_one / (jnp.sqrt(fixed_two) + EPSILON) + decay * weight)
    return [weight, moment_one, moment_two]


def adam_kernel(plan, scalars, side, *refs):
    count = len(plan)
    grads = refs[3 * count : -3 * count]
    factor = jnp.minimum(1.0, CLIP_NORM / (jnp.sqrt(scalars[0]) + 1e-06))
    for at, (rate, decay, pieces) in enumerate(plan):
        ins = refs[3 * at : 3 * at + 3]
        outs = refs[len(refs) - 3 * count + 3 * at :][:3]
        for grad, rows_from, cols_from, rows, cols in pieces:
            if isinstance(cols[0], bool):
                half = side[0] if cols[0] else 1 - side[0]
                span = pl.ds(pl.multiple_of(half * cols[1], LANES), cols[1])
            else:
                span = slice(*cols)
            where = (slice(*rows), span)
            gradient = grads[grad][slice(*rows_from), slice(*cols_from)] * factor
            results = adam(*[ref[where] for ref in ins], gradient, decay, rate)
            for out, result in zip(outs, results):
                out[where] = result


def adam_all(scalars, side, groups, grads, plan):
    outs = [jax.ShapeDtypeStruct(group[0].shape, WIDE) for group in groups for at in range(3)]
    scalar = pl.BlockSpec(memory_space=pltpu.SMEM)
    ins = [value for group in groups for value in group] + list(grads)
    found = pl.pallas_call(
        functools.partial(adam_kernel, plan),
        in_specs=[scalar, scalar] + [WHOLE] * len(ins),
        out_specs=[WHOLE] * len(outs),
        out_shape=outs,
        cost_estimate=pl.CostEstimate(
            flops=20_000_000, bytes_accessed=10_000_000, transcendentals=400_000
        ),
        compiler_params=pltpu.CompilerParams(vmem_limit_bytes=58 * 2**20),
    )(scalars, side, *ins)
    return [found[at : at + 3] for at in range(0, len(found), 3)]


def two_parts(values):
    high = lax.reduce_precision(values, 8, 7)
    fill = ((0, 0), (0, 8 - values.shape[1]))
    return jnp.concatenate([jnp.pad(high, fill), jnp.pad(values - high, fill)], 1).astype(LOW)


def widen_rows(values, rows):
    return jnp.pad(values, ((0, rows - values.shape[0]), (0, 0)))


def shards(
    patches,
    ctx_index,
    tgt_index,
    group,
    tgt_count,
    embed,
    embed_m,
    embed_v,
    bridge,
    bridge_m,
    bridge_v,
    enc_in,
    enc_in_m,
    enc_in_v,
    enc_out,
    enc_out_m,
    enc_out_v,
    enc_gains,
    enc_gains_m,
    enc_gains_v,
    pred_in,
    pred_in_m,
    pred_in_v,
    pred_out,
    pred_out_m,
    pred_out_v,
    pred_gains,
    pred_gains_m,
    pred_gains_v,
    t_embed,
    t_in,
    t_out,
    t_gains,
):
    index = lax.axis_index("dp")
    side = lax.axis_index("mp")
    dp_count = lax.axis_size("dp")
    lines = Lines(dp_count)
    assert patches.shape[0] == lax.axis_size("mp")
    count = patches.shape[0] * dp_count * TGT * D
    rows = D // dp_count
    p_rows = PW // dp_count
    half_d = D // 2
    local = D // 2
    ff = enc_in.shape[1] - 3 * local
    p_local = PW // 2
    p_ff = pred_in.shape[1] - 3 * p_local
    first = side == 0
    size = D // HEADS
    p_size = PW // PHEADS

    def own_half(values):
        return lax.dynamic_slice_in_dim(values, side * half_d, half_d, 1).astype(LOW)

    gains_pack = jnp.concatenate(
        [
            two_parts(enc_gains.T),
            two_parts(t_gains.T),
            widen_rows(two_parts(pred_gains.T), rows),
            jnp.zeros((rows, LANES - 48), LOW),
        ],
        1,
    )
    enc_in_low, t_in_low = enc_in.astype(LOW), t_in.astype(LOW)
    enc_out_low, t_out_low = enc_out.T.astype(LOW), t_out.T.astype(LOW)
    pred_in_low, pred_out_low = pred_in.astype(LOW), pred_out.T.astype(LOW)
    pred_main = jnp.concatenate([pred_out_low[:, p_local:], pred_in_low[:, 3 * p_local :]], 0)
    pred_rest = jnp.concatenate(
        [
            pred_in_low[:, : 2 * p_local],
            jnp.concatenate(
                [pred_in_low[:, 2 * p_local : 3 * p_local], pred_out_low[:, :p_local]], 1
            ),
        ],
        0,
    )
    packs = [
        [
            enc_in_low[:, : 3 * local],
            jnp.concatenate([own_half(embed), enc_out_low[:, :local], gains_pack], 1),
        ],
        [
            jnp.concatenate(
                [t_in_low[:, : 3 * local], own_half(t_embed), t_out_low[:, :local]], 1
            ),
            jnp.concatenate([own_half(bridge), pred_main, pred_rest], 1),
        ],
        [enc_in_low[:, 3 * local :], enc_out_low[:, local:]],
        [t_in_low[:, 3 * local :], t_out_low[:, local:]],
    ]

    far_a = gather_far(lines, packs[0])
    far_a, packs[1] = fence(far_a, packs[1])
    near_a = gather_near(lines, far_a, 0)
    near_a, packs[1], patches, ctx_index, tgt_index, group, tgt_count = fence(
        near_a, packs[1], patches, ctx_index, tgt_index, group, tgt_count
    )
    order = lines.order(index, D)
    p_order = lines.order(index, PW)
    eye = jnp.eye(D, dtype=LOW)
    patch = lax.dynamic_index_in_dim(patches, side, 0, keepdims=False)
    ctx = lax.dynamic_index_in_dim(ctx_index, side, 0, keepdims=False)
    tgt = lax.dynamic_index_in_dim(tgt_index, side, 0, keepdims=False)
    single = lax.dynamic_index_in_dim(group, side, 0, keepdims=False) == 1
    used = lax.dynamic_index_in_dim(tgt_count, side, 0, keepdims=False)
    positions = jnp.arange(patch.shape[0])
    chosen = jnp.concatenate([ctx, tgt])
    all_id, all_row, all_col = place(single, positions)
    joined_id, joined_row, joined_col = place(single, chosen)
    ctx_id, tgt_id = joined_id[:CTX], joined_id[CTX:]

    spread = jnp.arange(D) // rows * p_rows + jnp.arange(D) % rows
    spread = (jnp.arange(PW)[:, None] == spread) & (jnp.arange(D) % rows < p_rows)
    spread = spread.astype(LOW)
    pos_all = sincos(all_row, all_col, D, order)
    pos_ctx = sincos(joined_row[:CTX], joined_col[:CTX], D, order)
    pos_tgt = sincos(joined_row[CTX:], joined_col[CTX:], D, order)
    pos_small = sincos(joined_row, joined_col, PW, p_order)
    patch = mm(patch, order).astype(LOW)
    seen_ctx = mm((ctx[:, None] == positions).astype(LOW), patch).astype(LOW)
    seen_tgt = mm((tgt[:, None] == positions).astype(LOW), patch).astype(LOW)
    order_own = lax.dynamic_slice_in_dim(order, side * half_d, half_d, 0)
    order_other = lax.dynamic_slice_in_dim(order, (1 - side) * half_d, half_d, 0)
    held_a = gather_near(lines, near_a, 1)
    far_b = gather_far(lines, packs[1])
    (
        held_a,
        far_b,
        pos_all,
        pos_ctx,
        pos_tgt,
        pos_small,
        patch,
        seen_ctx,
        seen_tgt,
        order_own,
        order_other,
        spread,
        order,
        p_order,
        eye,
        all_id,
        ctx_id,
        tgt_id,
        joined_id,
        used,
        packs[2],
    ) = fence(
        held_a,
        far_b,
        pos_all,
        pos_ctx,
        pos_tgt,
        pos_small,
        patch,
        seen_ctx,
        seen_tgt,
        order_own,
        order_other,
        spread,
        order,
        p_order,
        eye,
        all_id,
        ctx_id,
        tgt_id,
        joined_id,
        used,
        packs[2],
    )
    other_a = swap_all(held_a)
    near_b = gather_near(lines, far_b, 0)
    held_a, other_a, near_b, packs[2] = fence(held_a, other_a, near_b, packs[2])

    def widths(values, *sizes):
        found, at = [], 0
        for wide in sizes:
            found.append(values[:, at : at + wide])
            at += wide
        return found

    enc_qkv = (flat(held_a[0]), flat(other_a[0]))
    enc_rest = (flat(held_a[1]), flat(other_a[1]))
    held_b = gather_near(lines, near_b, 1)
    far_c = gather_far(lines, packs[2])
    start, normed_one, *projected, enc_gain, target_gain, pred_gain = ctx_first(
        seen_ctx,
        pos_ctx,
        spread,
        (order_own, order_other),
        enc_rest,
        enc_qkv,
    )
    held_b, far_c, start, projected, packs[3] = fence(
        held_b, far_c, start, projected, packs[3]
    )
    other_b = swap_all(held_b)
    near_c = gather_near(lines, far_c, 0)
    middle, normed_two, *pairs = ctx_second(
        size, start, enc_gain, ctx_id, enc_rest, projected
    )
    mixed, logs = pairs[:2], pairs[2:]
    held_b, other_b, near_c, normed_two, middle, packs[3] = fence(
        held_b, other_b, near_c, normed_two, middle, packs[3]
    )
    held_c = gather_near(lines, near_c, 1)
    far_d = gather_far(lines, packs[3])
    t_middle, t_two = target_forward(
        size,
        patch,
        seen_tgt,
        pos_all,
        pos_tgt,
        target_gain,
        tgt_id,
        all_id,
        (order_own, order_other),
        (flat(held_b[0]), flat(other_b[0])),
    )
    held_c, far_d, t_middle, t_two = fence(held_c, far_d, t_middle, t_two)
    other_c = swap_all(held_c)
    near_d = gather_near(lines, far_d, 0)
    bridge_in, bridge_out, pairs = pred_parts(
        dp_count, side.astype(jnp.int32), flat(held_b[1]), flat(other_b[1]), p_order
    )
    pred_down, pred_up, pred_qk, pred_right = pairs
    held_c, other_c, near_d, bridge_in, bridge_out, pred_down, pred_up, pred_qk, pred_right = fence(
        held_c, other_c, near_d, bridge_in, bridge_out, pred_down, pred_up, pred_qk, pred_right
    )
    held_d = gather_near(lines, near_d, 1)
    enc_up, enc_down = [(flat(own), flat(other)) for own, other in zip(held_c, other_c)]
    hidden, context, *pairs = ff_forward(
        normed_two, middle, enc_gain, enc_up, enc_down
    )
    activated, slope = pairs[:2], pairs[2:]
    held_d, hidden, context, activated, slope = fence(held_d, hidden, context, activated, slope)
    other_d = swap_all(held_d)
    (
        joined,
        p_normed_one,
        p_middle,
        p_normed_two,
        predicted,
        final,
        guess,
        *pairs,
    ) = pred_forward(
        p_size,
        context,
        bridge_in,
        bridge_out,
        pos_small,
        pred_gain,
        tgt_id,
        joined_id,
        pred_down,
        pred_up,
        pred_qk,
        pred_right,
    )
    p_qk, p_values, p_mixed, p_activated, p_slope = [
        pairs[at : at + 2] for at in range(0, 10, 2)
    ]
    p_logs = pairs[10]
    other_d, guess = fence(other_d, guess)
    target = target_ff(
        t_two,
        t_middle,
        target_gain,
        (flat(held_d[0]), flat(other_d[0])),
        (flat(held_d[1]), flat(other_d[1])),
    )
    (
        loss_local,
        d_inward,
        grad_bridge_in,
        grad_bridge_out,
        sums_pred,
        *pairs,
    ) = pred_back_all(
        p_size,
        count,
        used[None],
        [
            guess,
            target,
            context,
            final,
            bridge_in,
            bridge_out,
            pred_gain,
            predicted,
            p_middle,
            joined,
            p_normed_one,
            p_normed_two,
        ],
        [
            pred_down,
            pred_up,
            pred_qk,
            pred_right,
            p_activated,
            p_slope,
            p_qk,
            p_values,
            p_mixed,
        ],
        p_logs,
        tgt_id,
        joined_id,
    )
    grads_left, grads_right = pairs[:2], pairs[2:]

    def blocks(values):
        return values.reshape(dp_count, p_rows, -1)

    bridge_pair = [
        mm_t(jnp.where(first, low, high), p_order).astype(LOW).reshape(dp_count, rows, -1)
        for low, high in (
            (grad_bridge_in, grad_bridge_out),
            (grad_bridge_out, grad_bridge_in),
        )
    ]
    pair_p = [
        jnp.concatenate(
            [
                blocks(grads_left[at]),
                bridge_pair[at][:, :p_rows],
                blocks(grads_right[at]),
                bridge_pair[at][:, p_rows:],
            ],
            2,
        )
        for at in (0, 1)
    ]
    sum_p = Sums(lines, *pair_p, 4 * local, p_rows)
    (d_inward,) = fence_sums([sum_p], d_inward)
    sum_p.swap()
    (d_inward,) = fence_sums([sum_p], d_inward)
    move((sum_p, 0))
    grads_own, grads_other, branch, d_middle, sums_ff = ff_back(
        d_inward,
        bridge_in,
        hidden,
        middle,
        normed_two,
        eye,
        enc_gain,
        activated,
        slope,
        enc_up,
        enc_down,
    )
    sum_f = Sums(lines, grads_own, grads_other, ff, rows)
    branch, d_middle = fence_sums([sum_p, sum_f], branch, d_middle)
    sum_f.swap()
    move((sum_p, 1))
    branch, d_middle = fence_sums([sum_p, sum_f], branch, d_middle)
    move((sum_f, 0), (sum_p, 2))
    d_proj = attn_back(size, branch, ctx_id, enc_rest, projected, mixed, logs)
    (d_proj,) = fence_sums([sum_p, sum_f], d_proj)
    move((sum_f, 1))
    grads_own, grads_other = qkv_back(
        branch,
        d_middle,
        start,
        normed_one,
        seen_ctx,
        eye,
        enc_gain,
        sums_ff,
        sums_pred,
        spread,
        [d_proj, mixed, enc_qkv, (order_own, order_other)],
    )
    sum_a = Sums(lines, grads_own, grads_other, 3 * local, rows)
    fence_sums([sum_f, sum_a])
    sum_a.swap()
    fence_sums([sum_f, sum_a])
    move((sum_f, 2), (sum_a, 0))
    fence_sums([sum_f, sum_a])
    move((sum_a, 1))
    fence_sums([sum_a])
    move((sum_a, 2))

    red_left, red_right, squares_p = sum_p.results()
    red_up, red_down, squares_f = sum_f.results()
    red_qkv, red_rest, squares_a = sum_a.results((2 * local + LANES, 2 * local))
    low_one = p_ff + 2 * p_local
    bridge_other = swap(jnp.concatenate([red_left[:, low_one:], red_right[:, low_one:]], 0))
    embed_other = swap(red_rest[:, :local])
    gains_t = red_rest[:, 2 * local :].T
    sums = jnp.concatenate([squares_p + squares_f + squares_a, loss_local], 1)
    sums = jnp.stack([jnp.sum(sums[:, :LANES]), sums[0, LANES]])
    for step in range(0, dp_count.bit_length(), 2):
        sums = lines.add_all(sums, step, min(step + 2, dp_count.bit_length()))
    groups = [
        (embed, embed_m, embed_v),
        (bridge, bridge_m, bridge_v),
        (enc_in, enc_in_m, enc_in_v),
        (enc_out.T, enc_out_m.T, enc_out_v.T),
        (enc_gains, enc_gains_m, enc_gains_v),
        (pred_in, pred_in_m, pred_in_v),
        (pred_out.T, pred_out_m.T, pred_out_v.T),
        (pred_gains, pred_gains_m, pred_gains_v),
    ]
    grads = [
        red_left,
        red_right,
        red_up,
        red_down,
        red_qkv,
        red_rest,
        bridge_other,
        embed_other,
        gains_t,
    ]
    every, part = (0, rows), (0, p_rows)
    lower = (p_rows, 2 * p_rows)
    qk_end, v_end = p_ff + 2 * p_local, p_ff + p_local
    learn, gain = (LEARN_RATE, WEIGHT_DECAY), (GAIN_RATE, 0.0)
    plan = (
        (
            *learn,
            (
                (5, every, (0, local), every, (True, half_d)),
                (7, every, (0, local), every, (False, half_d)),
            ),
        ),
        (
            *learn,
            (
                (0, part, (qk_end, qk_end + half_d), part, (True, half_d)),
                (1, part, (qk_end, qk_end + half_d), lower, (True, half_d)),
                (6, every, (0, half_d), every, (False, half_d)),
            ),
        ),
        (
            *learn,
            (
                (4, every, (0, 3 * local), every, (0, 3 * local)),
                (2, every, (0, ff), every, (3 * local, 3 * local + ff)),
            ),
        ),
        (
            *learn,
            (
                (5, every, (local, 2 * local), every, (0, local)),
                (3, every, (0, ff), every, (local, local + ff)),
            ),
        ),
        (*gain, ((8, (0, 6), every, (0, 6), every),)),
        (
            *learn,
            (
                (0, part, (p_ff, qk_end), part, (0, 2 * p_local)),
                (1, part, (p_ff, v_end), part, (2 * p_local, 3 * p_local)),
                (1, part, (0, p_ff), part, (3 * p_local, 3 * p_local + p_ff)),
            ),
        ),
        (
            *learn,
            (
                (1, part, (v_end, qk_end), part, (0, p_local)),
                (0, part, (0, p_ff), part, (p_local, p_local + p_ff)),
            ),
        ),
        (*gain, ((8, (8, 15), part, (0, 7), part),)),
    )
    results = adam_all(sums, side[None].astype(jnp.int32), groups, grads, plan)
    for at in (3, 6):
        results[at] = [value.T for value in results[at]]
    return (*[value for result in results for value in result], sums[1], jnp.sqrt(sums[0]))


def solution(mesh):
    in_specs = (
        P("dp", None, None),
        P("dp", None),
        P("dp", None),
        P("dp"),
        P("dp"),
        P("dp", None),
        P("dp", None),
        P("dp", None),
        P("dp", None),
        P("dp", None),
        P("dp", None),
        P("dp", "mp"),
        P("dp", "mp"),
        P("dp", "mp"),
        P("mp", "dp"),
        P("mp", "dp"),
        P("mp", "dp"),
        P(None, "dp"),
        P(None, "dp"),
        P(None, "dp"),
        P("dp", "mp"),
        P("dp", "mp"),
        P("dp", "mp"),
        P("mp", "dp"),
        P("mp", "dp"),
        P("mp", "dp"),
        P(None, "dp"),
        P(None, "dp"),
        P(None, "dp"),
        P("dp", None),
        P("dp", "mp"),
        P("mp", "dp"),
        P(None, "dp"),
    )
    out_specs = (
        P("dp", None),
        P("dp", None),
        P("dp", None),
        P("dp", None),
        P("dp", None),
        P("dp", None),
        P("dp", "mp"),
        P("dp", "mp"),
        P("dp", "mp"),
        P("mp", "dp"),
        P("mp", "dp"),
        P("mp", "dp"),
        P(None, "dp"),
        P(None, "dp"),
        P(None, "dp"),
        P("dp", "mp"),
        P("dp", "mp"),
        P("dp", "mp"),
        P("mp", "dp"),
        P("mp", "dp"),
        P("mp", "dp"),
        P(None, "dp"),
        P(None, "dp"),
        P(None, "dp"),
        P(),
        P(),
    )
    return jax.shard_map(shards, mesh=mesh, in_specs=in_specs, out_specs=out_specs, check_vma=False)
```

```python
import functools
import itertools

import jax
import jax.numpy as jnp
from jax import lax
from jax.experimental import pallas as pl
from jax.experimental.pallas import tpu as pltpu
from jax.sharding import PartitionSpec as P

D = 768
HEADS = 12
PW = 384
PHEADS = 12
SIDE = 14
SMALLP = 196
CTX = 512
TGT = 256
STEP = 10


LOW = jnp.bfloat16
WIDE = jnp.float32
CLIP_NORM = 0.0005
LEARN_RATE = 0.05
GAIN_RATE = 1.0
BETA_ONE = 0.9
BETA_TWO = 0.999
EPSILON = 1e-08
WEIGHT_DECAY = 0.05


LANES = 128


def norm_rows(values, gain_row, shift_row):
    centred = values - jnp.mean(values, -1, keepdims=True)
    spread = jnp.mean(centred * centred, -1, keepdims=True)
    return centred * lax.rsqrt(spread + 1e-06) * gain_row + shift_row


def norm_back(values, gain_row, grad):
    centred = values - jnp.mean(values, -1, keepdims=True)
    rstd = lax.rsqrt(jnp.mean(centred * centred, -1, keepdims=True) + 1e-06)
    unit = centred * rstd
    scaled = grad * gain_row
    d_values = rstd * (
        scaled
        - jnp.mean(scaled, -1, keepdims=True)
        - unit * jnp.mean(scaled * unit, -1, keepdims=True)
    )
    return d_values, jnp.sum(grad * unit, 0), jnp.sum(grad, 0)


def gelu_parts(pre):
    bell = jnp.exp(-0.5 * pre * pre)
    turn = 1.0 / (1.0 + 0.3275911 * 0.7071067811865476 * jnp.abs(pre))
    series = 0.5 * 1.061405429
    for factor in (-1.453152027, 1.421413741, -0.284496736, 0.254829592):
        series = series * turn + 0.5 * factor
    tail = series * turn * bell
    return jnp.where(pre < 0.0, tail, 1.0 - tail), bell * 0.3989422804014327


def gelu_both(pre):
    phi, density = gelu_parts(pre)
    return (pre * phi).astype(LOW), (phi + pre * density).astype(LOW)


def place(single, positions):
    image_id = jnp.where(single, 0, positions // SMALLP)
    within = jnp.where(single, positions, positions % SMALLP)
    side_len = jnp.where(single, 2 * SIDE, SIDE)
    return (image_id, within // side_len, within % side_len)


def three_parts(values):
    high = lax.reduce_precision(values, 8, 7)
    rest = values - high
    middle = lax.reduce_precision(rest, 8, 7)
    return jnp.concatenate([high, middle, rest - middle], 0).astype(LOW)


def sincos(row_pos, col_pos, width, order):
    quarter = width // 4
    omega = 10000.0 ** (-jnp.arange(quarter).astype(WIDE) / quarter)
    steps = jnp.arange(2 * SIDE)
    angle = steps.astype(WIDE)[:, None] * omega
    table = jnp.concatenate([jnp.sin(angle), jnp.cos(angle)], -1)
    blank = jnp.zeros_like(table)
    table = jnp.concatenate(
        [jnp.concatenate([table, blank], 1), jnp.concatenate([blank, table], 1)], 0
    )
    parts = three_parts(table)
    if order is not None:
        parts = mm(parts, order).astype(LOW)
    pick = jnp.concatenate([row_pos[:, None] == steps, col_pos[:, None] == steps], 1)
    pick = pick.astype(LOW)
    return mm(jnp.concatenate([pick, pick, pick], 1), parts)


def mm(left, right):
    return jnp.dot(left, right, preferred_element_type=WIDE)


def mm_t(left, right):
    return lax.dot_general(left, right, (((1,), (1,)), ((), ())), preferred_element_type=WIDE)


def t_mm(left, right):
    return lax.dot_general(left, right, (((0,), (0,)), ((), ())), preferred_element_type=WIDE)


SPAN = 64


def head_forward(query, keys, values, bias_ref, size):
    scale = size**-0.5
    scores = mm_t(keys, query) + bias_ref[...]
    highest = jnp.max(scores, 0, keepdims=True)
    soft = jnp.exp((scores - highest) * scale)
    total = jnp.sum(soft, 0, keepdims=True)
    return (t_mm(values, soft.astype(LOW)) / total).T, highest * scale + jnp.log(total)


def head_backward(query, keys, values, d_out, mixed, logs, bias_ref, soft_ref, ds_ref, size):
    scale = size**-0.5
    count = keys.shape[0]
    row_sum = jnp.sum((d_out.astype(WIDE) * mixed.astype(WIDE)).T, 0, keepdims=True)
    for low in range(0, count, SPAN):
        high = low + SPAN
        scores = mm_t(keys[low:high], query) + bias_ref[low:high, :]
        soft = jnp.exp(scores * scale - logs)
        d_soft = mm_t(values[low:high], d_out)
        soft_ref[low:high, :] = soft.astype(LOW)
        ds_ref[low:high, :] = (soft * (d_soft - row_sum)).astype(LOW)
    d_values = mm(soft_ref[...], d_out)
    d_keys = mm(ds_ref[...], query) * scale
    d_query = (t_mm(keys, ds_ref[...]) * scale).T
    return d_query.astype(LOW), d_keys.astype(LOW), d_values.astype(LOW)


WHOLE = pl.BlockSpec(memory_space=pltpu.VMEM)
CHUNK = 64
MARGIN = 6 * 2**20


def room(values, margin=MARGIN):
    total = 0
    for value in values:
        rows, cols = value.shape[-2], value.shape[-1]
        cells = value.size // (rows * cols) * (-(-rows // 16) * 16) * (-(-cols // LANES) * LANES)
        total += cells * jnp.dtype(value.dtype).itemsize
    return min(total + margin, 58 * 2**20)


def streamed(kernel, counts, late, early, *refs):
    n_in, n_out, n_scratch = counts
    ins, outs = list(refs[:n_in]), list(refs[n_in : n_in + n_out])
    scratch = refs[n_in + n_out : n_in + n_out + n_scratch]
    extra = refs[n_in + n_out + n_scratch :]
    arriving, leaving, left = {}, {}, []
    for at, which in enumerate(late):
        arriving[which] = pltpu.make_async_copy(ins[which], extra[at], extra[-1].at[at])
        arriving[which].start()
        ins[which] = extra[at]
    for at, which in enumerate(early, len(late)):
        leaving[which] = pltpu.make_async_copy(extra[at], outs[which], extra[-1].at[at])
        outs[which] = extra[at]

    def need(*those):
        for which in those:
            arriving.pop(which).wait()

    def ship(*those):
        for which in those:
            copy = leaving.pop(which)
            copy.start()
            left.append(copy)

    kernel(need, ship, *ins, *outs, *scratch)
    need(*list(arriving))
    ship(*list(leaving))
    for copy in left:
        copy.wait()


def on_chip(kernel, ins, outs, scratch, macs, exps=0, ahead=False, late=(), early=()):
    outs = [jax.ShapeDtypeStruct(shape, kind) for shape, kind in outs]
    held = [jax.ShapeDtypeStruct(shape, kind) for shape, kind in scratch]
    moved = sum(value.size * value.dtype.itemsize for value in list(ins) + outs)
    buffers = [pltpu.VMEM(shape, kind) for shape, kind in scratch]
    in_specs, out_specs = [WHOLE] * len(ins), [WHOLE] * len(outs)
    if late or early:
        counts = len(ins), len(outs), len(scratch)
        kernel = functools.partial(streamed, kernel, counts, late, early)
        for which in late:
            in_specs[which] = pl.BlockSpec(memory_space=pl.ANY)
            buffers.append(pltpu.VMEM(ins[which].shape, ins[which].dtype))
        for which in early:
            out_specs[which] = pl.BlockSpec(memory_space=pl.ANY)
            buffers.append(pltpu.VMEM(outs[which].shape, outs[which].dtype))
        buffers.append(pltpu.SemaphoreType.DMA((len(late) + len(early),)))
    return pl.pallas_call(
        kernel,
        in_specs=in_specs,
        out_specs=out_specs,
        out_shape=outs,
        scratch_shapes=buffers,
        cost_estimate=pl.CostEstimate(flops=2 * macs, bytes_accessed=moved, transcendentals=exps),
        compiler_params=pltpu.CompilerParams(
            vmem_limit_bytes=room(list(ins) + outs + held) if ahead else 58 * 2**20
        ),
    )(*ins)


def tiles(count, width, body):
    def step(at, carry):
        body(pl.ds(pl.multiple_of(at * width, width), width))
        return carry

    lax.fori_loop(0, count // width, step, 0)


def norm_back_rows(values_ref, grad_ref, gain, write, sums_ref, at):
    rows, width = values_ref.shape

    def step(number, carry):
        span = pl.ds(pl.multiple_of(number * CHUNK, CHUNK), CHUNK)
        values, grad = values_ref[span, :], grad_ref[span, :]
        centred = values - jnp.mean(values, -1, keepdims=True)
        rstd = lax.rsqrt(jnp.mean(centred * centred, -1, keepdims=True) + 1e-06)
        unit = centred * rstd
        scaled = grad * gain
        d_values = rstd * (
            scaled
            - jnp.mean(scaled, -1, keepdims=True)
            - unit * jnp.mean(scaled * unit, -1, keepdims=True)
        )
        write(span, d_values)
        return (
            carry[0] + jnp.sum(grad * unit, 0, keepdims=True),
            carry[1] + jnp.sum(grad, 0, keepdims=True),
        )

    blank = jnp.zeros((1, width), WIDE)
    gains, shifts = lax.fori_loop(0, rows // CHUNK, step, (blank, blank))
    sums_ref[at : at + 1, :] = gains
    sums_ref[at + 1 : at + 2, :] = shifts


def ff_side(branch, branch_t, normed_t, act, slope, down, d_pre, out):
    ff = act.shape[1]

    def body(span):
        d_act = mm(branch[...], down[:, span])
        values = (d_act * slope[:, span].astype(WIDE)).astype(LOW)
        d_pre[:, span] = values
        out[:, span] = mm(normed_t[...], values).astype(LOW)
        lower = pl.ds(pl.multiple_of(span.start + ff, LANES), span.size)
        out[:, lower] = mm(branch_t[...], act[:, span]).astype(LOW)

    tiles(ff, 768, body)


def ff_back_first_kernel(need, ship, *refs):
    d_inward, bridge_in, hidden, normed, eye, gains, act, slope, down = refs[0:9]
    out, d_hidden, branch, branch_t, normed_t, d_pre, sums, grad = refs[9:17]

    def first(span):
        grad[:, span] = mm_t(d_inward[...], bridge_in[span, :])

    tiles(D, 256, first)

    def write(span, values):
        d_hidden[span, :] = values
        branch[span, :] = values.astype(LOW)

    norm_back_rows(hidden, grad, gains[4:5, :], write, sums, 0)
    ship(1, 2)
    need(4, 3)
    branch_t[...] = mm_t(eye[...], branch[...]).astype(LOW)
    normed_t[...] = mm_t(eye[...], normed[...]).astype(LOW)
    ship(3, 4)
    need(8, 7, 6)
    ff_side(branch, branch_t, normed_t, act, slope, down, d_pre, out)


def ff_back_first(d_inward, bridge_in, hidden, normed, eye, gains, act, slope, down):
    rows, ff = act.shape
    return on_chip(
        ff_back_first_kernel,
        [d_inward, bridge_in, hidden, normed, eye, gains, act, slope, down],
        [((D, 2 * ff), LOW), ((rows, D), WIDE), ((rows, D), LOW)]
        + [((D, rows), LOW)] * 2
        + [((rows, ff), LOW), ((8, D), WIDE)],
        [((rows, D), WIDE)],
        4 * rows * D * ff,
        late=(4, 3, 8, 7, 6),
        early=(1, 2, 3, 4, 0, 5),
    )


def ff_back_second_kernel(need, ship, *refs):
    d_hidden, branch, branch_t, normed_t, d_pre_other, middle, gains = refs[0:7]
    act, slope, down, up_own, up_other, sums_first = refs[7:13]
    out, branch_out, d_middle, sums, grad, d_pre = refs[13:19]
    need(9, 8, 7)
    ff_side(branch, branch_t, normed_t, act, slope, down, d_pre, out)
    ship(0)
    need(10, 4, 11)

    def third(span):
        grad[:, span] = mm_t(d_pre[...], up_own[span, :]) + mm_t(d_pre_other[...], up_other[span, :])

    tiles(D, 768, third)
    need(5, 0)

    def write(span, values):
        values = values + d_hidden[span, :]
        d_middle[span, :] = values
        branch_out[span, :] = values.astype(LOW)

    norm_back_rows(middle, grad, gains[2:3, :], write, sums, 2)
    sums[0:2, :] = sums_first[0:2, :]


def ff_back_second(
    d_hidden,
    branch,
    branch_t,
    normed_t,
    d_pre,
    middle,
    gains,
    act,
    slope,
    down,
    up_own,
    up_other,
    sums,
):
    rows, ff = act.shape
    return on_chip(
        ff_back_second_kernel,
        [d_hidden, branch, branch_t, normed_t, d_pre, middle, gains, act, slope, down]
        + [up_own, up_other, sums],
        [((D, 2 * ff), LOW), ((rows, D), LOW), ((rows, D), WIDE), ((8, D), WIDE)],
        [((rows, D), WIDE), ((rows, ff), LOW)],
        5 * rows * D * ff,
        late=(9, 8, 7, 10, 4, 11, 5, 0),
        early=(0,),
    )


def attn_back_kernel(size, branch, ids_row, ids_col, *refs):
    rests, projs, mixeds, logs, d_projs = refs[0:2], refs[2:4], refs[4:6], refs[6:8], refs[8:10]
    d_mixed, bias, soft, d_scores = refs[10:14]
    width = D // 2
    bias[...] = jnp.where(ids_col[...] == ids_row[...], 0.0, -1e30)
    for side in (0, 1):
        proj, mixed, log, d_proj = projs[side], mixeds[side], logs[side], d_projs[side]
        d_mixed[...] = mm(branch[...], rests[side][:, width : 2 * width]).astype(LOW)

        def step(block, carry, proj=proj, mixed=mixed, log=log, d_proj=d_proj):
            at = [pl.multiple_of(part * width + block * LANES, LANES) for part in range(3)]
            query, keys, values = [proj[:, pl.ds(col, LANES)] for col in at]
            d_out = d_mixed[:, pl.ds(at[0], LANES)]
            out = mixed[:, pl.ds(at[0], LANES)]
            found = []
            for number, low in enumerate(range(0, LANES, size)):
                cols = slice(low, low + size)
                found.append(
                    head_backward(
                        query[:, cols],
                        keys[:, cols],
                        values[:, cols],
                        d_out[:, cols],
                        out[:, cols],
                        log[number, pl.ds(block, 1), :],
                        bias,
                        soft,
                        d_scores,
                        size,
                    )
                )
            for col, parts in zip(at, zip(*found)):
                d_proj[:, pl.ds(col, LANES)] = jnp.concatenate(parts, -1)
            return carry

        lax.fori_loop(0, width // LANES, step, 0)


def attn_back(size, branch, ids, rests, projs, mixeds, logs):
    rows = branch.shape[0]
    return on_chip(
        functools.partial(attn_back_kernel, size),
        [branch, ids[None, :], ids[:, None], *rests, *projs, *mixeds, *logs],
        [(projs[0].shape, LOW)] * 2,
        [
            ((rows, D // 2), LOW),
            ((rows, rows), WIDE),
            ((rows, rows), LOW),
            ((rows, rows), LOW),
        ],
        rows * D * D + rows * rows * D * 5,
        rows * rows * D // size,
        ahead=True,
    )


def qkv_back_kernel(need, ship, *refs):
    branch, d_middle, start, normed, seen, eye, gains, sums_ff, sums_p, spread = refs[0:10]
    d_projs, mixeds, qkvs, orders = refs[10:12], refs[12:14], refs[14:16], refs[16:18]
    outs = refs[18:20]
    grad, flipped, d_start, sums = refs[20:24]
    width = D // 2
    rest = 3 * width
    flipped[...] = mm_t(eye[...], branch[...]).astype(LOW)
    need(12, 13)
    for side in (0, 1):
        outs[side][:, rest + width : rest + 2 * width] = mm(
            flipped[...], mixeds[side][...]
        ).astype(LOW)
    need(3)
    flipped[...] = mm_t(eye[...], normed[...]).astype(LOW)
    need(10, 11)
    for side in (0, 1):
        outs[side][:, 0:rest] = mm(flipped[...], d_projs[side][...]).astype(LOW)
    need(14, 15)
    grad[...] = mm_t(d_projs[0][...], qkvs[0][...]) + mm_t(d_projs[1][...], qkvs[1][...])

    def write(span, values):
        d_start[span, :] = (values + d_middle[span, :]).astype(LOW)

    need(1, 2)
    norm_back_rows(start, grad, gains[0:1, :], write, sums, 0)
    need(4)
    flipped[...] = mm_t(eye[...], seen[...]).astype(LOW)
    sums[2:4, :] = sums_ff[2:4, :]
    sums[4:6, :] = sums_ff[0:2, :]
    sums[6:8, :] = jnp.zeros((2, D), WIDE)
    rows = jnp.concatenate(
        [sums[...].astype(LOW), mm(sums_p[...].astype(LOW), spread[...]).astype(LOW)], 0
    )
    cols = t_mm(rows, eye[0:16, 0:LANES]).astype(LOW)
    need(16, 17)
    for side in (0, 1):
        moved = mm_t(d_start[...], orders[side][...]).astype(LOW)
        outs[side][:, rest : rest + width] = mm(flipped[...], moved).astype(LOW)
        outs[side][:, rest + 2 * width :] = cols


def qkv_back(branch, d_middle, start, normed, seen, eye, gains, sums_ff, sums_p, spread, pairs):
    rows, width = branch.shape[0], D // 2
    return on_chip(
        qkv_back_kernel,
        [branch, d_middle, start, normed, seen, eye, gains, sums_ff, sums_p, spread]
        + [value for pair in pairs for value in pair],
        [((D, 5 * width + LANES), LOW)] * 2,
        [((rows, D), WIDE), ((D, rows), LOW), ((rows, D), LOW), ((8, D), WIDE)],
        rows * D * D * 10,
        late=(12, 13, 3, 10, 11, 14, 15, 1, 2, 4, 16, 17),
    )


def row_spans(rows, chunk, body):
    def step(number, carry):
        body(pl.ds(pl.multiple_of(number * chunk, chunk), chunk))
        return carry

    lax.fori_loop(0, rows // chunk, step, 0)


def heads_forward(query_ref, keys_ref, values_ref, out_ref, logs_ref, bias, size, at):
    width = out_ref.shape[1]

    def step(block, carry):
        cols = [pl.multiple_of(first + block * LANES, LANES) for first in at]
        query = query_ref[:, pl.ds(cols[0], LANES)]
        keys = keys_ref[:, pl.ds(cols[1], LANES)]
        values = values_ref[:, pl.ds(cols[2], LANES)]
        found = []
        for number, low in enumerate(range(0, LANES, size)):
            part = slice(low, low + size)
            out, logs = head_forward(
                query[:, part], keys[:, part], values[:, part], bias, size
            )
            found.append(out)
            if logs_ref is not None:
                logs_ref[number, pl.ds(block, 1), :] = logs
        place_at = pl.ds(pl.multiple_of(block * LANES, LANES), LANES)
        out_ref[:, place_at] = jnp.concatenate(found, -1).astype(LOW)
        return carry

    lax.fori_loop(0, width // LANES, step, 0)


def ctx_first_kernel(need, ship, seen, pos, spread, *refs):
    orders, rests, qkvs = refs[0:2], refs[2:4], refs[4:6]
    start, normed, projs, outs, embed_w = refs[6], refs[7], refs[8:10], refs[10:13], refs[13]
    gains = outs[0]
    width = orders[0].shape[0]
    parts = rests[0][:, 2 * width :].astype(WIDE).T
    outs[0][...] = parts[0:8] + parts[8:16]
    outs[1][...] = parts[16:24] + parts[24:32]
    low = parts[32:48].astype(LOW)
    low = mm_t(low, spread[...])
    outs[2][...] = low[0:8] + low[8:16]
    embed_w[...] = (
        mm(rests[0][:, 0:width], orders[0][...]) + mm(rests[1][:, 0:width], orders[1][...])
    ).astype(LOW)
    need(0, 1)
    start[...] = mm(seen[...], embed_w[...]) + pos[...]
    ship(0)

    def first_norm(span):
        normed[span, :] = norm_rows(start[span, :], gains[0:1, :], gains[1:2, :]).astype(LOW)

    row_spans(seen.shape[0], CHUNK, first_norm)
    ship(1)
    for side in (0, 1):
        need(7 + side)
        projs[side][...] = mm(normed[...], qkvs[side][...]).astype(LOW)
        ship(2 + side)


def ctx_first(seen, pos, spread, orders, rests, qkvs):
    rows, width = seen.shape[0], orders[0].shape[0]
    return on_chip(
        ctx_first_kernel,
        [seen, pos, spread, *orders, *rests, *qkvs],
        [((rows, D), WIDE), ((rows, D), LOW)]
        + [((rows, 3 * width), LOW)] * 2
        + [((8, D), WIDE), ((8, D), WIDE), ((8, PW), WIDE)],
        [((D, D), LOW)],
        rows * D * D * 4 + D * D * D,
        late=(0, 1, 7, 8),
        early=(0, 1, 2, 3),
    )


def ctx_second_kernel(size, need, ship, start, gains, ids_row, ids_col, *refs):
    rests, projs = refs[0:2], refs[2:4]
    middle, normed_two, mixeds, logs, bias = refs[4], refs[5], refs[6:8], refs[8:10], refs[10]
    width = mixeds[0].shape[1]
    bias[...] = jnp.where(ids_col[...] == ids_row[...], 0.0, -1e30)
    for side in (0, 1):
        need(6 + side)
        proj = projs[side]
        heads_forward(
            proj, proj, proj, mixeds[side], logs[side], bias, size, (0, width, 2 * width)
        )
        ship(2 + side)
    need(4, 5, 0)
    middle[...] = (
        start[...]
        + mm_t(mixeds[0][...], rests[0][:, width : 2 * width])
        + mm_t(mixeds[1][...], rests[1][:, width : 2 * width])
    )

    def second_norm(span):
        normed_two[span, :] = norm_rows(middle[span, :], gains[2:3, :], gains[3:4, :]).astype(LOW)

    row_spans(start.shape[0], CHUNK, second_norm)


def ctx_second(size, start, gains, ids, rests, projs):
    rows, width = start.shape[0], D // 2
    return on_chip(
        functools.partial(ctx_second_kernel, size),
        [start, gains, ids[None, :], ids[:, None], *rests, *projs],
        [((rows, D), WIDE), ((rows, D), LOW)]
        + [((rows, width), LOW)] * 2
        + [((LANES // size, 8, rows), WIDE)] * 2,
        [((rows, rows), WIDE)],
        rows * D * D + rows * rows * D * 2,
        rows * rows * D // size,
        late=(6, 7, 4, 5, 0),
        early=(2, 3),
    )


def gelu_rows(pre_ref, act_ref, slope_ref, span):
    def body(rows):
        act, slope = gelu_both(pre_ref[rows, :])
        act_ref[rows, span] = act
        if slope_ref is not None:
            slope_ref[rows, span] = slope

    row_spans(pre_ref.shape[0], 32, body)


def ff_kernel(need, ship, *refs):
    normed, middle, gains, ups, downs = *refs[0:3], refs[3:5], refs[5:7]
    hidden, context, acts, slopes, pre = refs[7], refs[8], refs[9:11], refs[11:13], refs[13]
    rows, ff = acts[0].shape
    for side in (0, 1):
        need(3 + side)

        def first(span, side=side):
            pre[...] = mm(normed[...], ups[side][:, span])
            gelu_rows(pre, acts[side], slopes[side], span)

        tiles(ff, 512, first)
        ship(2 + side, 4 + side)
    need(5, 6, 1)
    hidden[...] = (
        middle[...] + mm_t(acts[0][...], downs[0][...]) + mm_t(acts[1][...], downs[1][...])
    )

    def last(span):
        context[span, :] = norm_rows(hidden[span, :], gains[4:5, :], gains[5:6, :]).astype(LOW)

    row_spans(rows, CHUNK, last)


def ff_forward(normed, middle, gains, ups, downs):
    rows, ff = normed.shape[0], ups[0].shape[1]
    return on_chip(
        ff_kernel,
        [normed, middle, gains, *ups, *downs],
        [((rows, D), WIDE), ((rows, D), LOW)] + [((rows, ff), LOW)] * 4,
        [((rows, 512), WIDE)],
        rows * D * ff * 4 + rows * D * D,
        rows * ff * 2,
        late=(3, 4, 5, 6, 1),
        early=(2, 3, 4, 5),
    )


def target_kernel(size, *refs):
    patch, seen, pos_all, pos_tgt, gains, ids_row, ids_col = refs[0:7]
    orders, weights, (t_middle, t_two) = refs[7:9], refs[9:11], refs[11:13]
    embed_w, hidden, normed, start, query, keys, mixed, bias = refs[13:]
    width = D // 2
    own, other = [part[:, 3 * width : 4 * width] for part in weights]
    embed_w[...] = (mm(own, orders[0][...]) + mm(other, orders[1][...])).astype(LOW)
    hidden[...] = mm(patch[...], embed_w[...]) + pos_all[...]

    def first_norm(span):
        normed[span, :] = norm_rows(hidden[span, :], gains[0:1, :], gains[1:2, :]).astype(LOW)

    row_spans(patch.shape[0], 112, first_norm)
    start[...] = mm(seen[...], embed_w[...]) + pos_tgt[...]
    t_normed = norm_rows(start[...], gains[0:1, :], gains[1:2, :]).astype(LOW)
    bias[...] = jnp.where(ids_col[...] == ids_row[...], 0.0, -1e30)
    total = start[...]
    for part in weights:
        query[...] = mm(t_normed, part[:, 0:width]).astype(LOW)
        keys[...] = mm(normed[...], part[:, width : 3 * width]).astype(LOW)
        heads_forward(query, keys, keys, mixed, None, bias, size, (0, 0, width))
        total = total + mm_t(mixed[...], part[:, 4 * width : 5 * width])
    t_middle[...] = total
    t_two[...] = norm_rows(total, gains[2:3, :], gains[3:4, :]).astype(LOW)


def target_forward(
    size, patch, seen, pos_all, pos_tgt, gains, idq, idk, orders, weights
):
    rows, count, width = seen.shape[0], patch.shape[0], D // 2
    return on_chip(
        functools.partial(target_kernel, size),
        [patch, seen, pos_all, pos_tgt, gains, idq[None, :], idk[:, None], *orders, *weights],
        [((rows, D), WIDE), ((rows, D), LOW)],
        [
            ((D, D), LOW),
            ((count, D), WIDE),
            ((count, D), LOW),
            ((rows, D), WIDE),
            ((rows, width), LOW),
            ((count, 2 * width), LOW),
            ((rows, width), LOW),
            ((count, rows), WIDE),
        ],
        count * D * D * 3 + rows * D * D * 3 + 2 * rows * count * D,
        rows * count * D // size,
        ahead=True,
    )


def pred_forward_kernel(size, *refs):
    context, bridge_in, bridge_out, pos, gains, ids_row, ids_col = refs[0:7]
    downs, ups, qks, rights = refs[7:9], refs[9:11], refs[11:13], refs[13:15]
    joined, normed, middle, normed_two, predicted, final, guess = refs[15:22]
    out_qk, out_v, mixeds, acts, slopes = (
        refs[22:24],
        refs[24:26],
        refs[26:28],
        refs[28:30],
        refs[30:32],
    )
    logs, bias = refs[32], refs[33]
    width = out_v[0].shape[1]
    joined[0:CTX, :] = mm(context[...], bridge_in[...]) + pos[0:CTX, :]
    joined[CTX:, :] = gains[6:7, :] + pos[CTX:, :]

    def first(span):
        normed[span, :] = norm_rows(joined[span, :], gains[0:1, :], gains[1:2, :]).astype(LOW)

    row_spans(joined.shape[0], 128, first)
    bias[...] = jnp.where(ids_col[...] == ids_row[...], 0.0, -1e30)
    total = joined[CTX:, :]
    head = 0
    for qk, right, qk_ref, v_ref, mixed in zip(qks, rights, out_qk, out_v, mixeds):
        qk_ref[...] = mm(normed[...], qk[...]).astype(LOW)
        v_ref[...] = mm(normed[...], right[:, 0:width]).astype(LOW)
        found = []
        for low in range(0, width, size):
            out, log = head_forward(
                qk_ref[CTX:, low : low + size],
                qk_ref[:, width + low : width + low + size],
                v_ref[:, low : low + size],
                bias,
                size,
            )
            found.append(out)
            logs[head : head + 1, :] = log
            head += 1
        mixed[...] = jnp.concatenate(found, -1).astype(LOW)
        total = total + mm_t(mixed[...], right[:, width:])
    middle[...] = total
    normed_two[...] = norm_rows(total, gains[2:3, :], gains[3:4, :]).astype(LOW)
    total = middle[...]
    for up, down, act, slope in zip(ups, downs, acts, slopes):
        values, tilt = gelu_both(mm(normed_two[...], up[...]))
        act[...] = values
        slope[...] = tilt
        total = total + mm_t(act[...], down[...])
    predicted[...] = total
    final[...] = norm_rows(total, gains[4:5, :], gains[5:6, :]).astype(LOW)
    guess[...] = mm_t(final[...], bridge_out[...])


def pred_forward(
    size, context, bridge_in, bridge_out, pos, gains, idq, idk, downs, ups, qks, rights
):
    rows, count, width, ff = idq.shape[0], idk.shape[0], qks[0].shape[1] // 2, ups[0].shape[1]
    low, wide = LOW, WIDE
    return on_chip(
        functools.partial(pred_forward_kernel, size),
        [context, bridge_in, bridge_out, pos, gains, idq[None, :], idk[:, None]]
        + [*downs, *ups, *qks, *rights],
        [((count, PW), wide), ((count, PW), low), ((rows, PW), wide), ((rows, PW), low)]
        + [((rows, PW), wide), ((rows, PW), low), ((rows, D), wide)]
        + [((count, 2 * width), low)] * 2
        + [((count, width), low)] * 2
        + [((rows, width), low)] * 2
        + [((rows, ff), low)] * 4
        + [((16, rows), wide)],
        [((count, rows), wide)],
        1_000_000_000,
        rows * count * PW // size,
    )


def target_ff_kernel(last, need, ship, t_two, start, gains, up, down, target, pre, act):
    need(3)

    def first(span):
        pre[...] = mm(t_two[...], up[:, span])
        gelu_rows(pre, act, None, span)

    tiles(act.shape[1], 512, first)
    need(4)
    total = start[...] + mm_t(act[...], down[...])
    if last:
        total = norm_rows(total, gains[4:5, :], gains[5:6, :])
        total = norm_rows(total, 1.0, 0.0)
    target[...] = total


def target_ff(last, t_two, start, gains, up, down):
    rows, ff = t_two.shape[0], up.shape[1]
    return on_chip(
        functools.partial(target_ff_kernel, last),
        [t_two, start, gains, up, down],
        [((rows, D), WIDE)],
        [((rows, 512), WIDE), ((rows, ff), LOW)],
        rows * D * ff * 2,
        rows * ff,
        late=(3, 4),
    )[0]


def pred_back_all_kernel(size, count_all, dp_count, *refs):
    (guess, target, used, context, final, bridge_in, bridge_out, gains, ids_row, ids_col) = refs[
        0:10
    ]
    predicted, middle, joined, normed, normed_two = refs[10:15]
    downs, ups, qks, rights = refs[15:17], refs[17:19], refs[19:21], refs[21:23]
    acts, slopes, in_qk, in_v, mixeds = (
        refs[23:25],
        refs[25:27],
        refs[27:29],
        refs[29:31],
        refs[31:33],
    )
    logs = refs[33]
    p_order, side_ref, loss, d_inward, sums = refs[34:39]
    packs = refs[39:41]
    d_qk, d_v, d_normed, bias, soft, d_scores, g_bridge_out = refs[41:48]
    p_rows = PW // dp_count
    half = packs[0].shape[2] // 2

    def put(side, column, values):
        for block in range(dp_count):
            part = values[block * p_rows : (block + 1) * p_rows]
            packs[side][block, :, column : column + values.shape[1]] = part.astype(LOW)

    width = in_v[0].shape[1]
    ff = acts[0].shape[1]
    diff = guess[...] - target[...]
    size_abs = jnp.abs(diff)
    keep = lax.broadcasted_iota(jnp.int32, diff.shape, 0) < used[0]
    terms = jnp.where(
        keep, jnp.where(size_abs < 1.0, 0.5 * diff * diff, size_abs - 0.5), 0.0
    )
    loss[...] = jnp.sum(jnp.sum(terms, 0, keepdims=True), 1, keepdims=True)
    d_guess = jnp.where(keep, jnp.clip(diff, -1.0, 1.0) / count_all, 0.0).astype(LOW)
    g_bridge_out[...] = t_mm(d_guess, final[...]).astype(LOW)

    def back(values, gain, grad, at):
        d_values, gain_sum, shift_sum = norm_back(values, gain, grad)
        sums[at : at + 1, :] = gain_sum[None, :]
        sums[at + 1 : at + 2, :] = shift_sum[None, :]
        return d_values

    d_tail = back(predicted[...], gains[4:5, :], mm(d_guess, bridge_out[...]), 4)
    branch = d_tail.astype(LOW)
    total = None
    for side in (0, 1):
        d_pre = (mm(branch, downs[side][...]) * slopes[side][...].astype(WIDE)).astype(LOW)
        put(side, 0, t_mm(branch, acts[side][...]))
        put(side, half, t_mm(normed_two[...], d_pre))
        part = mm_t(d_pre, ups[side][...])
        total = part if total is None else total + part
    d_middle = d_tail + back(middle[...], gains[2:3, :], total, 2)
    branch = d_middle.astype(LOW)
    bias[...] = jnp.where(ids_col[...] == ids_row[...], 0.0, -1e30)
    total = None
    head = 0
    for side in (0, 1):
        qk_ref, v_ref, right = in_qk[side], in_v[side], rights[side]
        d_mixed = mm(branch, right[:, width:]).astype(LOW)
        put(side, half + ff + width, t_mm(branch, mixeds[side][...]))
        found = []
        for low in range(0, width, size):
            found.append(
                head_backward(
                    qk_ref[CTX:, low : low + size],
                    qk_ref[:, width + low : width + low + size],
                    v_ref[:, low : low + size],
                    d_mixed[:, low : low + size],
                    mixeds[side][:, low : low + size],
                    logs[head : head + 1, :],
                    bias,
                    soft,
                    d_scores,
                    size,
                )
            )
            head += 1
        d_query, d_keys, d_values = [jnp.concatenate(parts, -1) for parts in zip(*found)]
        d_qk[0:CTX, 0:width] = jnp.zeros((CTX, width), LOW)
        d_qk[CTX:, 0:width] = d_query
        d_qk[:, width:] = d_keys
        d_v[...] = d_values
        put(side, ff, t_mm(normed[...], d_qk[...]))
        put(side, half + ff, t_mm(normed[...], d_v[...]))
        part = mm_t(d_qk[...], qks[side][...]) + mm_t(d_v[...], right[:, 0:width])
        d_normed[...] = part if side == 0 else d_normed[...] + part
    d_joined = back(joined[...], gains[0:1, :], d_normed[...], 0)
    sums[6:7, :] = jnp.sum(d_joined[CTX:] + d_middle, 0, keepdims=True)
    sums[7:8, :] = jnp.zeros((1, PW), WIDE)
    d_inward[...] = d_joined[0:CTX].astype(LOW)
    g_in = mm_t(t_mm(context[...], d_inward[...]).astype(LOW), p_order[...])
    g_out = mm_t(g_bridge_out[...], p_order[...])
    flip = side_ref[0] != 0
    at = ff + 2 * width
    for side, values in ((0, jnp.where(flip, g_out, g_in)), (1, jnp.where(flip, g_in, g_out))):
        for block in range(dp_count):
            for low in (0, 1):
                start = (2 * block + low) * p_rows
                packs[side][block, :, low * half + at : (low + 1) * half] = values[
                    start : start + p_rows
                ].astype(LOW)


def pred_back_all(size, count_all, dp_count, side, order, used, values, pairs, logs, idq, idk):
    (guess, target, context, final, bridge_in, bridge_out, gains) = values[:7]
    ff, width, count = pairs[0][0].shape[1], pairs[2][0].shape[1] // 2, idk.shape[0]
    ins = [guess, target, used, context, final, bridge_in, bridge_out, gains]
    ins += [idq[None, :], idk[:, None], *values[7:]] + [part for pair in pairs for part in pair]
    ins += [logs, order, side]
    outs = [((1, 1), WIDE), ((CTX, PW), LOW), ((8, PW), WIDE)]
    outs += [((dp_count, PW // dp_count, 2 * (ff + 2 * width) + D), LOW)] * 2
    specs = [WHOLE] * len(ins)
    specs[2] = specs[-1] = pl.BlockSpec(memory_space=pltpu.SMEM)
    return pl.pallas_call(
        functools.partial(pred_back_all_kernel, size, count_all, dp_count),
        in_specs=specs,
        out_specs=[WHOLE] * len(outs),
        out_shape=[jax.ShapeDtypeStruct(shape, kind) for shape, kind in outs],
        scratch_shapes=[
            pltpu.VMEM((count, 2 * width), LOW),
            pltpu.VMEM((count, width), LOW),
            pltpu.VMEM((count, PW), WIDE),
            pltpu.VMEM((count, idq.shape[0]), WIDE),
            pltpu.VMEM((count, idq.shape[0]), LOW),
            pltpu.VMEM((count, idq.shape[0]), LOW),
            pltpu.VMEM((D, PW), LOW),
        ],
        cost_estimate=pl.CostEstimate(
            flops=4_000_000_000, bytes_accessed=20_000_000, transcendentals=3_000_000
        ),
        compiler_params=pltpu.CompilerParams(vmem_limit_bytes=58 * 2**20),
    )(*ins)


def pred_parts_kernel(dp_count, side_ref, own, other, order, *outs):
    width, half = PW // 2, D // 2
    ff = D
    flip = side_ref[0] != 0
    low = jnp.where(flip, other[:, 0:half], own[:, 0:half])
    high = jnp.where(flip, own[:, 0:half], other[:, 0:half])
    outs[0][...] = mm(low, order[...]).astype(LOW)
    outs[1][...] = mm(high, order[...]).astype(LOW)
    rows = PW // dp_count
    for at, ref in enumerate((own, other)):
        for start, wide, out in ((half, ff, 2), (half + ff, 2 * width, 6)):
            blocks = ref[:, start : start + wide].astype(WIDE).reshape(dp_count, 2 * rows, wide)
            outs[out + at][...] = blocks[:, :rows].reshape(PW, wide).astype(LOW)
            outs[out + 2 + at][...] = blocks[:, rows:].reshape(PW, wide).astype(LOW)


def pred_parts(dp_count, side, own, other, order):
    width, half = PW // 2, D // 2
    if PW // dp_count % 8:
        bridges = [part[:, :half] for part in (own, other)]
        first = side == 0
        found = [
            mm(jnp.where(first, bridges[at], bridges[1 - at]), order).astype(LOW) for at in (0, 1)
        ]
        for start, wide in ((half, D), (half + D, 2 * width)):
            cols = [part[:, start : start + wide] for part in (own, other)]
            cols = [part.reshape(dp_count, 2, PW // dp_count, wide) for part in cols]
            found += [flat(part[:, which]) for which in (0, 1) for part in cols]
    else:
        ins = [side[None], own, other, order]
        shapes = [(D, PW)] * 2 + [(PW, D)] * 4 + [(PW, 2 * width)] * 4
        outs = [jax.ShapeDtypeStruct(shape, LOW) for shape in shapes]
        found = pl.pallas_call(
            functools.partial(pred_parts_kernel, dp_count),
            in_specs=[pl.BlockSpec(memory_space=pltpu.SMEM)] + [WHOLE] * 3,
            out_specs=[WHOLE] * len(outs),
            out_shape=outs,
            cost_estimate=pl.CostEstimate(
                flops=1_000_000_000, bytes_accessed=9_000_000, transcendentals=0
            ),
            compiler_params=pltpu.CompilerParams(vmem_limit_bytes=58 * 2**20),
        )(*ins)
    return found[0], found[1], [found[at : at + 2] for at in range(2, 10, 2)]


class Lines:
    def __init__(self, count):
        self.count = count
        self.stride = count // 4
        bits = list(range(self.stride.bit_length() - 1))
        turn = len(bits) // 2
        self.bits = bits
        self.orders = (bits, bits[turn:] + bits[:turn])
        self.turn = turn

    def flip(self, values, bit):
        pairs = [(at, at ^ (1 << bit)) for at in range(self.count)]
        return lax.ppermute(values, "dp", pairs)

    def shift(self, values, steps):
        pairs = [(at, (at + steps * self.stride) % self.count) for at in range(self.count)]
        return lax.ppermute(values, "dp", pairs)

    def add_all(self, values, low, high):
        total = values
        for change in range(1, 1 << (high - low)):
            pairs = [(at, at ^ (change << low)) for at in range(2 * self.count)]
            total = total + lax.ppermute(values, ("dp", "mp"), pairs)
        return total

    def order(self, index, width):
        rows = width // self.count
        column = jnp.arange(width)
        block = column // rows
        far = (block // self.stride - index // self.stride) % 4
        near = (block ^ index) % self.stride
        target = (near * 4 + far) * rows + column % rows
        return (target[:, None] == column).astype(LOW)


def swap(values):
    return lax.ppermute(values, "mp", [(0, 1), (1, 0)])


def swap_all(values):
    return [swap(value) for value in values]


def far_kernel(*refs):
    outs = refs[4:]
    cut = outs[0].shape[-1]
    for at, block in enumerate(refs[:4]):
        outs[0][at] = block[:, :cut]
        outs[1][at] = block[:, cut:]


def gather_far(lines, shards):
    wide = jnp.concatenate(shards, 1)
    found = [wide] + [lines.shift(wide, -steps) for steps in (1, 2, 3)]
    rows, cut = shards[0].shape
    cols = [slice(0, cut), slice(cut, wide.shape[1])]
    if rows % 16:
        return [jnp.stack([block[:, part] for block in found]) for part in cols]
    return on_chip(
        far_kernel,
        found,
        [((4, rows, part.stop - part.start), LOW) for part in cols],
        [],
        0,
    )


def stack_kernel(axes, *refs):
    count = len(axes)
    ins, outs, bufs, sems = refs[: 2 * count], refs[2 * count : 3 * count], refs[3 * count : -1], refs[-1]
    arriving = [
        pltpu.make_async_copy(ins[at], bufs[at], sems.at[at]) for at in range(2 * count)
    ]
    for copy in arriving:
        copy.start()
    leaving = []
    for at, copy in enumerate(arriving):
        copy.wait()
        where = (slice(None),) * axes[at % count] + (at // count,)
        out = pltpu.make_async_copy(
            bufs[at], outs[at % count].at[where], sems.at[2 * count + at]
        )
        out.start()
        leaving.append(out)
    for copy in leaving:
        copy.wait()


def stack_pairs(held, got, axes):
    anywhere = pl.BlockSpec(memory_space=pl.ANY)
    ins = [*held, *got]
    outs = [
        jax.ShapeDtypeStruct(values.shape[:axis] + (2,) + values.shape[axis:], LOW)
        for values, axis in zip(held, axes)
    ]
    return pl.pallas_call(
        functools.partial(stack_kernel, axes),
        in_specs=[anywhere] * len(ins),
        out_specs=[anywhere] * len(outs),
        out_shape=outs,
        scratch_shapes=[pltpu.VMEM(value.shape, LOW) for value in ins]
        + [pltpu.SemaphoreType.DMA((2 * len(ins),))],
        cost_estimate=pl.CostEstimate(
            flops=0, bytes_accessed=8 * sum(value.size for value in ins), transcendentals=0
        ),
        compiler_params=pltpu.CompilerParams(vmem_limit_bytes=58 * 2**20),
    )(*ins)


def gather_near(lines, held, phase):
    done = [list(order[: lines.turn]) if phase else [] for order in lines.orders]
    steps = [order[lines.turn :] if phase else order[: lines.turn] for order in lines.orders]
    for bits in zip(*steps):
        got = [lines.flip(values, bit) for values, bit in zip(held, bits)]
        axes = [sum(1 for other in had if other > bit) for had, bit in zip(done, bits)]
        if phase and held[0].shape[-2] % 16 == 0:
            held = stack_pairs(held, got, axes)
        else:
            held = [
                jnp.stack([values, other], axis) for values, other, axis in zip(held, got, axes)
            ]
        for had, bit in zip(done, bits):
            had.append(bit)
    return list(held)


def flat(values):
    return values.reshape(-1, values.shape[-1])


class Box:
    def __init__(self, value):
        self.value, self.held = value, False


def sum_kernel(plan, squares, *refs):
    operands = 1 + max(term[0] for pieces in plan for piece in pieces for term in piece)
    if squares:
        refs[-1][...] = jnp.zeros((1, LANES), WIDE)
    for pieces, out in zip(plan, refs[operands:]):
        for lead in itertools.product(*[range(size) for size in out.shape[:-2]]):
            at = 0
            for piece in pieces:
                total = None
                for operand, low, high in piece:
                    part = refs[operand][lead + (slice(None), slice(low, high))].astype(WIDE)
                    total = part if total is None else total + part
                wide = high - low
                out[lead + (slice(None), slice(at, at + wide))] = total.astype(out.dtype)
                if squares:
                    for col in range(0, wide, LANES):
                        part = total[:, col : col + LANES]
                        weight = 0.5 if at + col == squares[1] and wide == squares[0] else 1.0
                        refs[-1][...] += weight * jnp.sum(part * part, 0, keepdims=True)
                at += wide


def sum_parts(outs, kind, squares=None):
    operands, specs, plan, shapes = [], [], [], []
    known = {}
    for pieces in outs:
        row = []
        for piece in pieces:
            terms = []
            for box, taken, (low, high) in piece:
                if (id(box), taken) not in known:
                    known[id(box), taken] = len(operands)
                    value = box.value
                    block = [
                        size if pick is None else None for size, pick in zip(value.shape, taken)
                    ]
                    where = tuple(0 if pick is None else pick for pick in taken) + (0, 0)
                    operands.append(value)
                    specs.append(
                        pl.BlockSpec(
                            tuple(block) + value.shape[-2:], lambda step, where=where: where
                        )
                    )
                terms.append((known[id(box), taken], low, high))
            row.append(tuple(terms))
        plan.append(tuple(row))
        box, taken, cols = pieces[0][0]
        lead = tuple(size for size, pick in zip(box.value.shape, taken) if pick is None)
        wide = sum(piece[0][2][1] - piece[0][2][0] for piece in pieces)
        shapes.append(
            jax.ShapeDtypeStruct(lead + (box.value.shape[-2], wide), kind)
        )
    moved = 8 * sum(shape.size for shape in shapes)
    if squares:
        shapes.append(jax.ShapeDtypeStruct((1, LANES), WIDE))
    return pl.pallas_call(
        functools.partial(sum_kernel, tuple(plan), squares),
        grid=(1,),
        in_specs=specs,
        out_specs=[
            pl.BlockSpec(shape.shape, lambda step, rank=len(shape.shape): (0,) * rank)
            for shape in shapes
        ],
        out_shape=shapes,
        cost_estimate=pl.CostEstimate(flops=moved, bytes_accessed=moved, transcendentals=0),
        compiler_params=pltpu.CompilerParams(vmem_limit_bytes=58 * 2**20),
    )(*operands)


class Terms:
    def __init__(self, lines, order, cols):
        self.lines, self.order, self.cols, self.left = lines, order, cols, list(lines.bits)
        self.terms = []

    def take(self, axis, at):
        found = []
        for box, taken, cols in self.terms:
            open_axes = [place_at for place_at, pick in enumerate(taken) if pick is None]
            picked = list(taken)
            picked[open_axes[axis]] = at
            found.append((box, tuple(picked), cols))
        return found

    def near_job(self, phase):
        turn = self.lines.turn
        (self.bit,) = self.order[turn:] if phase else self.order[:turn]
        self.axis = sum(1 for other in self.left if other > self.bit)
        return self.take(self.axis, 1)

    def near_send(self, send):
        got = self.lines.flip(send, self.bit)
        self.left.remove(self.bit)
        self.terms = self.take(self.axis, 0)
        self.terms.append((Box(got), (None,) * (got.ndim - 2), (0, got.shape[-1])))


class Sums:
    def __init__(self, lines, own, other, cut, rows):
        self.lines, self.rows, self.cut = lines, rows, cut
        self.plain = len(lines.bits) != 2
        self.own, self.other = Box(own), Box(other)
        self.lead = (2,) * len(lines.bits) + (4,)
        self.wide = own.shape[-1]
        self.parts = [
            Terms(lines, order, cols)
            for order, cols in zip(lines.orders, ((0, cut), (cut, self.wide)))
        ]

    def shaped(self, values):
        return values.reshape(self.lead + (self.rows, self.wide))

    def boxes(self):
        found = [self.own, self.other]
        for part in self.parts:
            found += [term[0] for term in part.terms]
        return found

    def swap(self, got=None):
        if self.plain:
            return
        mine = Box(self.shaped(self.own.value))
        mine.held = True
        if got is None:
            got = swap(self.other.value)
        self.other.held = True
        got = Box(self.shaped(got))
        for part in self.parts:
            blank = (None,) * len(self.lead)
            part.terms = [(mine, blank, part.cols), (got, blank, part.cols)]

    def far_jobs(self):
        return [[part.take(0, steps) for part in self.parts] for steps in (1, 2, 3)]

    def far_send(self, sends):
        got = [Box(self.lines.shift(send, steps)) for send, steps in zip(sends, (1, 2, 3))]
        for part in self.parts:
            part.terms = part.take(0, 0) + [(box, (), part.cols) for box in got]

    def results(self, halved=(0, -1)):
        if not self.plain:
            return sum_parts([[part.terms] for part in self.parts], WIDE, halved)
        results = []
        both = self.own.value.astype(WIDE) + swap(self.other.value).astype(WIDE)
        for part in self.parts:
            total = self.shaped(both)[..., part.cols[0] : part.cols[1]]
            for bit in part.order:
                axis = sum(1 for other in part.left if other > bit)
                part.left.remove(bit)
                sent = lax.index_in_dim(total, 1, axis, keepdims=False).astype(LOW)
                total = lax.index_in_dim(total, 0, axis, keepdims=False)
                total = total + self.lines.flip(sent, bit).astype(WIDE)
            result = total[0]
            for steps in (1, 2, 3):
                got = self.lines.shift(total[steps].astype(LOW), steps)
                result = result + got.astype(WIDE)
            results.append(result)
        squares = sum(jnp.sum(result * result) for result in results)
        for result in results:
            if result.shape[1] == halved[0]:
                part = result[:, halved[1] : halved[1] + LANES]
                squares = squares - 0.5 * jnp.sum(part * part)
        return results + [jnp.pad(squares.reshape(1, 1), ((0, 0), (0, LANES - 1)))]


def move(*steps, hold=None):
    work = []
    for total, kind in steps:
        if total.plain:
            continue
        if kind == 2:
            work.append((total.far_send, total.far_jobs()))
        else:
            for part in total.parts:
                work.append((part.near_send, [[part.near_job(kind)]]))
    if not work:
        return hold
    sends = sum_parts([job for send, jobs in work for job in jobs], LOW)
    if hold is not None:
        sends, hold = lax.optimization_barrier((sends, hold))
    at = 0
    for send, jobs in work:
        found = sends[at : at + len(jobs)]
        at += len(jobs)
        send(found if len(jobs) > 1 else found[0])
    return hold


def fence_sums(sums, *values):
    boxes = {id(box): box for one in sums for box in one.boxes() if not box.held}
    boxes = list(boxes.values())
    held, values = lax.optimization_barrier(([box.value for box in boxes], values))
    for box, value in zip(boxes, held):
        box.value, box.held = value, True
    return values


def fence(*values):
    return lax.optimization_barrier(values)


def adam(weight, moment_one, moment_two, gradient, decay, rate):
    moment_one = BETA_ONE * moment_one + (1.0 - BETA_ONE) * gradient
    moment_two = BETA_TWO * moment_two + (1.0 - BETA_TWO) * gradient * gradient
    fixed_one = moment_one / (1.0 - BETA_ONE**STEP)
    fixed_two = moment_two / (1.0 - BETA_TWO**STEP)
    weight = weight - rate * (fixed_one / (jnp.sqrt(fixed_two) + EPSILON) + decay * weight)
    return [weight, moment_one, moment_two]


def adam_kernel(plan, scalars, side, *refs):
    count = len(plan)
    grads = refs[3 * count : -3 * count]
    total = jnp.sum(scalars[0:1, :], 1, keepdims=True)
    factor = jnp.minimum(1.0, CLIP_NORM / (jnp.sqrt(total) + 1e-06))
    for at, (rate, decay, pieces) in enumerate(plan):
        ins = refs[3 * at : 3 * at + 3]
        outs = refs[len(refs) - 3 * count + 3 * at :][:3]
        for grad, rows_from, cols_from, rows, cols in pieces:
            if isinstance(cols[0], bool):
                half = side[0] if cols[0] else 1 - side[0]
                span = pl.ds(pl.multiple_of(half * cols[1], LANES), cols[1])
            else:
                span = slice(*cols)
            where = (slice(*rows), span)
            gradient = grads[grad][slice(*rows_from), slice(*cols_from)] * factor
            results = adam(*[ref[where] for ref in ins], gradient, decay, rate)
            for out, result in zip(outs, results):
                out[where] = result


def adam_all(scalars, side, groups, grads, plan):
    outs = [jax.ShapeDtypeStruct(group[0].shape, WIDE) for group in groups for at in range(3)]
    scalar = pl.BlockSpec(memory_space=pltpu.SMEM)
    ins = [value for group in groups for value in group] + list(grads)
    found = pl.pallas_call(
        functools.partial(adam_kernel, plan),
        in_specs=[WHOLE, scalar] + [WHOLE] * len(ins),
        out_specs=[WHOLE] * len(outs),
        out_shape=outs,
        cost_estimate=pl.CostEstimate(
            flops=20_000_000, bytes_accessed=10_000_000, transcendentals=400_000
        ),
        compiler_params=pltpu.CompilerParams(vmem_limit_bytes=58 * 2**20),
    )(scalars, side, *ins)
    return [found[at : at + 3] for at in range(0, len(found), 3)]


def two_parts(values):
    high = lax.reduce_precision(values, 8, 7)
    fill = ((0, 0), (0, 8 - values.shape[1]))
    return jnp.concatenate([jnp.pad(high, fill), jnp.pad(values - high, fill)], 1).astype(LOW)


def widen_rows(values, rows):
    return jnp.pad(values, ((0, rows - values.shape[0]), (0, 0)))


def shards(
    patches,
    ctx_index,
    tgt_index,
    group,
    tgt_count,
    embed,
    embed_m,
    embed_v,
    bridge,
    bridge_m,
    bridge_v,
    enc_in,
    enc_in_m,
    enc_in_v,
    enc_out,
    enc_out_m,
    enc_out_v,
    enc_gains,
    enc_gains_m,
    enc_gains_v,
    pred_in,
    pred_in_m,
    pred_in_v,
    pred_out,
    pred_out_m,
    pred_out_v,
    pred_gains,
    pred_gains_m,
    pred_gains_v,
    t_embed,
    t_in,
    t_out,
    t_gains,
):
    index = lax.axis_index("dp")
    side = lax.axis_index("mp")
    dp_count = lax.axis_size("dp")
    lines = Lines(dp_count)
    assert patches.shape[0] == lax.axis_size("mp")
    count = patches.shape[0] * dp_count * TGT * D
    rows = D // dp_count
    p_rows = PW // dp_count
    half_d = D // 2
    local = D // 2
    ff = enc_in.shape[1] - 3 * local
    p_local = PW // 2
    p_ff = pred_in.shape[1] - 3 * p_local
    first = side == 0
    size = D // HEADS
    p_size = PW // PHEADS

    def own_half(values):
        return lax.dynamic_slice_in_dim(values, side * half_d, half_d, 1).astype(LOW)

    gains_pack = jnp.concatenate(
        [
            two_parts(enc_gains.T),
            two_parts(t_gains.T),
            widen_rows(two_parts(pred_gains.T), rows),
            jnp.zeros((rows, LANES - 48), LOW),
        ],
        1,
    )
    enc_in_low, t_in_low = enc_in.astype(LOW), t_in.astype(LOW)
    enc_out_low, t_out_low = enc_out.T.astype(LOW), t_out.T.astype(LOW)
    pred_in_low, pred_out_low = pred_in.astype(LOW), pred_out.T.astype(LOW)
    pred_main = jnp.concatenate([pred_out_low[:, p_local:], pred_in_low[:, 3 * p_local :]], 0)
    pred_rest = jnp.concatenate(
        [
            pred_in_low[:, : 2 * p_local],
            jnp.concatenate(
                [pred_in_low[:, 2 * p_local : 3 * p_local], pred_out_low[:, :p_local]], 1
            ),
        ],
        0,
    )
    packs = [
        [
            enc_in_low[:, : 3 * local],
            jnp.concatenate([own_half(embed), enc_out_low[:, :local], gains_pack], 1),
        ],
        [
            jnp.concatenate(
                [t_in_low[:, : 3 * local], own_half(t_embed), t_out_low[:, :local]], 1
            ),
            jnp.concatenate([own_half(bridge), pred_main, pred_rest], 1),
        ],
        [enc_in_low[:, 3 * local :], enc_out_low[:, local:]],
        [t_in_low[:, 3 * local :], t_out_low[:, local:]],
    ]

    far_a = gather_far(lines, packs[0])
    far_a, packs[1] = fence(far_a, packs[1])
    near_a = gather_near(lines, far_a, 0)
    near_a, packs[1], patches, ctx_index, tgt_index, group, tgt_count = fence(
        near_a, packs[1], patches, ctx_index, tgt_index, group, tgt_count
    )
    order = lines.order(index, D)
    p_order = lines.order(index, PW)
    eye = jnp.eye(D, dtype=LOW)
    patch = lax.dynamic_index_in_dim(patches, side, 0, keepdims=False)
    ctx = lax.dynamic_index_in_dim(ctx_index, side, 0, keepdims=False)
    tgt = lax.dynamic_index_in_dim(tgt_index, side, 0, keepdims=False)
    single = lax.dynamic_index_in_dim(group, side, 0, keepdims=False) == 1
    used = lax.dynamic_index_in_dim(tgt_count, side, 0, keepdims=False)
    positions = jnp.arange(patch.shape[0])
    chosen = jnp.concatenate([ctx, tgt])
    all_id, all_row, all_col = place(single, positions)
    joined_id, joined_row, joined_col = place(single, chosen)
    ctx_id, tgt_id = joined_id[:CTX], joined_id[CTX:]

    spread = jnp.arange(D) // rows * p_rows + jnp.arange(D) % rows
    spread = (jnp.arange(PW)[:, None] == spread) & (jnp.arange(D) % rows < p_rows)
    spread = spread.astype(LOW)
    pos_all = sincos(all_row, all_col, D, order)
    pos_ctx = sincos(joined_row[:CTX], joined_col[:CTX], D, order)
    pos_tgt = sincos(joined_row[CTX:], joined_col[CTX:], D, order)
    pos_small = sincos(joined_row, joined_col, PW, p_order)
    patch = mm(patch, order).astype(LOW)
    seen_ctx = mm((ctx[:, None] == positions).astype(LOW), patch).astype(LOW)
    seen_tgt = mm((tgt[:, None] == positions).astype(LOW), patch).astype(LOW)
    order_own = lax.dynamic_slice_in_dim(order, side * half_d, half_d, 0)
    order_other = lax.dynamic_slice_in_dim(order, (1 - side) * half_d, half_d, 0)
    held_a = gather_near(lines, near_a, 1)
    far_b = gather_far(lines, packs[1])
    (
        held_a,
        far_b,
        pos_all,
        pos_ctx,
        pos_tgt,
        pos_small,
        patch,
        seen_ctx,
        seen_tgt,
        order_own,
        order_other,
        spread,
        order,
        p_order,
        eye,
        all_id,
        ctx_id,
        tgt_id,
        joined_id,
        used,
        packs[2],
    ) = fence(
        held_a,
        far_b,
        pos_all,
        pos_ctx,
        pos_tgt,
        pos_small,
        patch,
        seen_ctx,
        seen_tgt,
        order_own,
        order_other,
        spread,
        order,
        p_order,
        eye,
        all_id,
        ctx_id,
        tgt_id,
        joined_id,
        used,
        packs[2],
    )
    other_a = swap_all(held_a)
    near_b = gather_near(lines, far_b, 0)
    held_a, other_a, near_b, packs[2] = fence(held_a, other_a, near_b, packs[2])

    def widths(values, *sizes):
        found, at = [], 0
        for wide in sizes:
            found.append(values[:, at : at + wide])
            at += wide
        return found

    enc_qkv = (flat(held_a[0]), flat(other_a[0]))
    enc_rest = (flat(held_a[1]), flat(other_a[1]))
    held_b = gather_near(lines, near_b, 1)
    far_c = gather_far(lines, packs[2])
    start, normed_one, *projected, enc_gain, target_gain, pred_gain = ctx_first(
        seen_ctx,
        pos_ctx,
        spread,
        (order_own, order_other),
        enc_rest,
        enc_qkv,
    )
    held_b, far_c, start, projected, packs[3] = fence(
        held_b, far_c, start, projected, packs[3]
    )
    other_b = swap_all(held_b)
    near_c = gather_near(lines, far_c, 0)
    middle, normed_two, *pairs = ctx_second(
        size, start, enc_gain, ctx_id, enc_rest, projected
    )
    mixed, logs = pairs[:2], pairs[2:]
    held_b, other_b, near_c, normed_two, middle, packs[3] = fence(
        held_b, other_b, near_c, normed_two, middle, packs[3]
    )
    held_c = gather_near(lines, near_c, 1)
    far_d = gather_far(lines, packs[3])
    t_middle, t_two = target_forward(
        size,
        patch,
        seen_tgt,
        pos_all,
        pos_tgt,
        target_gain,
        tgt_id,
        all_id,
        (order_own, order_other),
        (flat(held_b[0]), flat(other_b[0])),
    )
    held_c, far_d, t_middle, t_two = fence(held_c, far_d, t_middle, t_two)
    other_c = swap_all(held_c)
    near_d = gather_near(lines, far_d, 0)
    bridge_in, bridge_out, pairs = pred_parts(
        dp_count, side.astype(jnp.int32), flat(held_b[1]), flat(other_b[1]), p_order
    )
    pred_down, pred_up, pred_qk, pred_right = pairs
    held_c, other_c, near_d, bridge_in, bridge_out, pred_down, pred_up, pred_qk, pred_right = fence(
        held_c, other_c, near_d, bridge_in, bridge_out, pred_down, pred_up, pred_qk, pred_right
    )
    held_d = gather_near(lines, near_d, 1)
    enc_up, enc_down = [(flat(own), flat(other)) for own, other in zip(held_c, other_c)]
    hidden, context, *pairs = ff_forward(
        normed_two, middle, enc_gain, enc_up, enc_down
    )
    activated, slope = pairs[:2], pairs[2:]
    (
        joined,
        p_normed_one,
        p_middle,
        p_normed_two,
        predicted,
        final,
        guess,
        *pairs,
    ) = pred_forward(
        p_size,
        context,
        bridge_in,
        bridge_out,
        pos_small,
        pred_gain,
        tgt_id,
        joined_id,
        pred_down,
        pred_up,
        pred_qk,
        pred_right,
    )
    p_qk, p_values, p_mixed, p_activated, p_slope = [
        pairs[at : at + 2] for at in range(0, 10, 2)
    ]
    p_logs = pairs[10]
    held_d, guess, t_middle = fence(held_d, guess, t_middle)
    other_d = swap_all(held_d)
    target = target_ff(False, t_two, t_middle, target_gain, *[flat(part) for part in held_d])
    target, other_d = fence(target, other_d)
    target = target_ff(True, t_two, target, target_gain, *[flat(part) for part in other_d])
    (
        loss_local,
        d_inward,
        sums_pred,
        *pair_p,
    ) = pred_back_all(
        p_size,
        count,
        dp_count,
        side[None].astype(jnp.int32),
        p_order,
        used[None],
        [
            guess,
            target,
            context,
            final,
            bridge_in,
            bridge_out,
            pred_gain,
            predicted,
            p_middle,
            joined,
            p_normed_one,
            p_normed_two,
        ],
        [
            pred_down,
            pred_up,
            pred_qk,
            pred_right,
            p_activated,
            p_slope,
            p_qk,
            p_values,
            p_mixed,
        ],
        p_logs,
        tgt_id,
        joined_id,
    )
    sum_p = Sums(lines, *pair_p, 4 * local, p_rows)
    (d_inward,) = fence_sums([sum_p], d_inward)
    sum_p.swap()
    (d_inward,) = fence_sums([sum_p], d_inward)
    d_inward = move((sum_p, 0), hold=d_inward)
    grads_other, *parts, sums_ff = ff_back_first(
        d_inward,
        bridge_in,
        hidden,
        normed_two,
        eye,
        enc_gain,
        activated[1],
        slope[1],
        enc_down[1],
    )
    grads_other, parts = fence_sums([sum_p], grads_other, parts)
    grads_got = swap(grads_other)
    parts = move((sum_p, 1), hold=parts)
    grads_own, branch, d_middle, sums_ff = ff_back_second(
        *parts,
        middle,
        enc_gain,
        activated[0],
        slope[0],
        enc_down[0],
        enc_up[0],
        enc_up[1],
        sums_ff,
    )
    sum_f = Sums(lines, grads_own, grads_other, ff, rows)
    sum_f.swap(grads_got)
    branch, d_middle = fence_sums([sum_p, sum_f], branch, d_middle)
    d_middle, branch = move((sum_f, 0), (sum_p, 2), hold=(d_middle, branch))
    d_proj = attn_back(size, branch, ctx_id, enc_rest, projected, mixed, logs)
    (d_proj,) = fence_sums([sum_p, sum_f], d_proj)
    d_proj = move((sum_f, 1), hold=d_proj)
    grads_own, grads_other = qkv_back(
        branch,
        d_middle,
        start,
        normed_one,
        seen_ctx,
        eye,
        enc_gain,
        sums_ff,
        sums_pred,
        spread,
        [d_proj, mixed, enc_qkv, (order_own, order_other)],
    )
    sum_a = Sums(lines, grads_own, grads_other, 3 * local, rows)
    fence_sums([sum_f, sum_a])
    sum_a.swap()
    fence_sums([sum_f, sum_a])
    move((sum_f, 2), (sum_a, 0))
    fence_sums([sum_f, sum_a])
    move((sum_a, 1))
    fence_sums([sum_a])
    move((sum_a, 2))

    red_left, red_right, squares_p = sum_p.results()
    red_up, red_down, squares_f = sum_f.results()
    red_qkv, red_rest, squares_a = sum_a.results((2 * local + LANES, 2 * local))
    low_one = p_ff + 2 * p_local
    bridge_other = swap(jnp.concatenate([red_left[:, low_one:], red_right[:, low_one:]], 0))
    embed_other = swap(red_rest[:, :local])
    gains_t = red_rest[:, 2 * local :].T
    sums = jnp.concatenate(
        [squares_p + squares_f + squares_a, jnp.pad(loss_local, ((0, 0), (0, LANES - 1)))], 0
    )
    for step in range(0, dp_count.bit_length(), 2):
        sums = lines.add_all(sums, step, min(step + 2, dp_count.bit_length()))
    groups = [
        (embed, embed_m, embed_v),
        (bridge, bridge_m, bridge_v),
        (enc_in, enc_in_m, enc_in_v),
        (enc_out.T, enc_out_m.T, enc_out_v.T),
        (enc_gains, enc_gains_m, enc_gains_v),
        (pred_in, pred_in_m, pred_in_v),
        (pred_out.T, pred_out_m.T, pred_out_v.T),
        (pred_gains, pred_gains_m, pred_gains_v),
    ]
    grads = [
        red_left,
        red_right,
        red_up,
        red_down,
        red_qkv,
        red_rest,
        bridge_other,
        embed_other,
        gains_t,
    ]
    every, part = (0, rows), (0, p_rows)
    lower = (p_rows, 2 * p_rows)
    qk_end, v_end = p_ff + 2 * p_local, p_ff + p_local
    learn, gain = (LEARN_RATE, WEIGHT_DECAY), (GAIN_RATE, 0.0)
    plan = (
        (
            *learn,
            (
                (5, every, (0, local), every, (True, half_d)),
                (7, every, (0, local), every, (False, half_d)),
            ),
        ),
        (
            *learn,
            (
                (0, part, (qk_end, qk_end + half_d), part, (True, half_d)),
                (1, part, (qk_end, qk_end + half_d), lower, (True, half_d)),
                (6, every, (0, half_d), every, (False, half_d)),
            ),
        ),
        (
            *learn,
            (
                (4, every, (0, 3 * local), every, (0, 3 * local)),
                (2, every, (0, ff), every, (3 * local, 3 * local + ff)),
            ),
        ),
        (
            *learn,
            (
                (5, every, (local, 2 * local), every, (0, local)),
                (3, every, (0, ff), every, (local, local + ff)),
            ),
        ),
        (*gain, ((8, (0, 6), every, (0, 6), every),)),
        (
            *learn,
            (
                (0, part, (p_ff, qk_end), part, (0, 2 * p_local)),
                (1, part, (p_ff, v_end), part, (2 * p_local, 3 * p_local)),
                (1, part, (0, p_ff), part, (3 * p_local, 3 * p_local + p_ff)),
            ),
        ),
        (
            *learn,
            (
                (1, part, (v_end, qk_end), part, (0, p_local)),
                (0, part, (0, p_ff), part, (p_local, p_local + p_ff)),
            ),
        ),
        (*gain, ((8, (8, 15), part, (0, 7), part),)),
    )
    results = adam_all(sums, side[None].astype(jnp.int32), groups, grads, plan)
    for at in (3, 6):
        results[at] = [value.T for value in results[at]]
    return (*[value for result in results for value in result], sums[1, 0], jnp.sqrt(jnp.sum(sums[0])))


def solution(mesh):
    in_specs = (
        P("dp", None, None),
        P("dp", None),
        P("dp", None),
        P("dp"),
        P("dp"),
        P("dp", None),
        P("dp", None),
        P("dp", None),
        P("dp", None),
        P("dp", None),
        P("dp", None),
        P("dp", "mp"),
        P("dp", "mp"),
        P("dp", "mp"),
        P("mp", "dp"),
        P("mp", "dp"),
        P("mp", "dp"),
        P(None, "dp"),
        P(None, "dp"),
        P(None, "dp"),
        P("dp", "mp"),
        P("dp", "mp"),
        P("dp", "mp"),
        P("mp", "dp"),
        P("mp", "dp"),
        P("mp", "dp"),
        P(None, "dp"),
        P(None, "dp"),
        P(None, "dp"),
        P("dp", None),
        P("dp", "mp"),
        P("mp", "dp"),
        P(None, "dp"),
    )
    out_specs = (
        P("dp", None),
        P("dp", None),
        P("dp", None),
        P("dp", None),
        P("dp", None),
        P("dp", None),
        P("dp", "mp"),
        P("dp", "mp"),
        P("dp", "mp"),
        P("mp", "dp"),
        P("mp", "dp"),
        P("mp", "dp"),
        P(None, "dp"),
        P(None, "dp"),
        P(None, "dp"),
        P("dp", "mp"),
        P("dp", "mp"),
        P("dp", "mp"),
        P("mp", "dp"),
        P("mp", "dp"),
        P("mp", "dp"),
        P(None, "dp"),
        P(None, "dp"),
        P(None, "dp"),
        P(),
        P(),
    )
    return jax.shard_map(shards, mesh=mesh, in_specs=in_specs, out_specs=out_specs, check_vma=False)
```

```python
import functools
import itertools

import jax
import jax.numpy as jnp
from jax import lax
from jax.experimental import pallas as pl
from jax.experimental.pallas import tpu as pltpu
from jax.sharding import PartitionSpec as P

D = 768
HEADS = 12
PW = 384
PHEADS = 12
SIDE = 14
SMALLP = 196
CTX = 512
TGT = 256
STEP = 10


LOW = jnp.bfloat16
WIDE = jnp.float32
CLIP_NORM = 0.0005
LEARN_RATE = 0.05
GAIN_RATE = 1.0
BETA_ONE = 0.9
BETA_TWO = 0.999
EPSILON = 1e-08
WEIGHT_DECAY = 0.05


LANES = 128


def norm_rows(values, gain_row, shift_row):
    centred = values - jnp.mean(values, -1, keepdims=True)
    spread = jnp.mean(centred * centred, -1, keepdims=True)
    return centred * lax.rsqrt(spread + 1e-06) * gain_row + shift_row


def norm_back(values, gain_row, grad):
    centred = values - jnp.mean(values, -1, keepdims=True)
    rstd = lax.rsqrt(jnp.mean(centred * centred, -1, keepdims=True) + 1e-06)
    unit = centred * rstd
    scaled = grad * gain_row
    d_values = rstd * (
        scaled
        - jnp.mean(scaled, -1, keepdims=True)
        - unit * jnp.mean(scaled * unit, -1, keepdims=True)
    )
    return d_values, jnp.sum(grad * unit, 0), jnp.sum(grad, 0)


def gelu_parts(pre):
    bell = jnp.exp(-0.5 * pre * pre)
    turn = 1.0 / (1.0 + 0.3275911 * 0.7071067811865476 * jnp.abs(pre))
    series = 0.5 * 1.061405429
    for factor in (-1.453152027, 1.421413741, -0.284496736, 0.254829592):
        series = series * turn + 0.5 * factor
    tail = series * turn * bell
    return jnp.where(pre < 0.0, tail, 1.0 - tail), bell * 0.3989422804014327


def gelu_both(pre):
    phi, density = gelu_parts(pre)
    return (pre * phi).astype(LOW), (phi + pre * density).astype(LOW)


def place(single, positions):
    image_id = jnp.where(single, 0, positions // SMALLP)
    within = jnp.where(single, positions, positions % SMALLP)
    side_len = jnp.where(single, 2 * SIDE, SIDE)
    return (image_id, within // side_len, within % side_len)


def three_parts(values):
    high = lax.reduce_precision(values, 8, 7)
    rest = values - high
    middle = lax.reduce_precision(rest, 8, 7)
    return jnp.concatenate([high, middle, rest - middle], 0).astype(LOW)


def sincos(row_pos, col_pos, width, order):
    quarter = width // 4
    omega = 10000.0 ** (-jnp.arange(quarter).astype(WIDE) / quarter)
    steps = jnp.arange(2 * SIDE)
    angle = steps.astype(WIDE)[:, None] * omega
    table = jnp.concatenate([jnp.sin(angle), jnp.cos(angle)], -1)
    blank = jnp.zeros_like(table)
    table = jnp.concatenate(
        [jnp.concatenate([table, blank], 1), jnp.concatenate([blank, table], 1)], 0
    )
    parts = three_parts(table)
    if order is not None:
        parts = mm(parts, order).astype(LOW)
    pick = jnp.concatenate([row_pos[:, None] == steps, col_pos[:, None] == steps], 1)
    pick = pick.astype(LOW)
    return mm(jnp.concatenate([pick, pick, pick], 1), parts)


def mm(left, right):
    return jnp.dot(left, right, preferred_element_type=WIDE)


def mm_t(left, right):
    return lax.dot_general(left, right, (((1,), (1,)), ((), ())), preferred_element_type=WIDE)


def t_mm(left, right):
    return lax.dot_general(left, right, (((0,), (0,)), ((), ())), preferred_element_type=WIDE)


SPAN = 64


def head_forward(query, keys, values, bias_ref, size):
    scale = size**-0.5
    scores = mm_t(keys, query) + bias_ref[...]
    highest = jnp.max(scores, 0, keepdims=True)
    soft = jnp.exp((scores - highest) * scale)
    total = jnp.sum(soft, 0, keepdims=True)
    return (t_mm(values, soft.astype(LOW)) / total).T, highest * scale + jnp.log(total)


def head_backward(query, keys, values, d_out, mixed, logs, bias_ref, soft_ref, ds_ref, size):
    scale = size**-0.5
    count = keys.shape[0]
    row_sum = jnp.sum((d_out.astype(WIDE) * mixed.astype(WIDE)).T, 0, keepdims=True)
    for low in range(0, count, SPAN):
        high = low + SPAN
        scores = mm_t(keys[low:high], query) + bias_ref[low:high, :]
        soft = jnp.exp(scores * scale - logs)
        d_soft = mm_t(values[low:high], d_out)
        soft_ref[low:high, :] = soft.astype(LOW)
        ds_ref[low:high, :] = (soft * (d_soft - row_sum)).astype(LOW)
    d_values = mm(soft_ref[...], d_out)
    d_keys = mm(ds_ref[...], query) * scale
    d_query = (t_mm(keys, ds_ref[...]) * scale).T
    return d_query.astype(LOW), d_keys.astype(LOW), d_values.astype(LOW)


WHOLE = pl.BlockSpec(memory_space=pltpu.VMEM)
CHUNK = 64
MARGIN = 6 * 2**20


def room(values, margin=MARGIN):
    total = 0
    for value in values:
        rows, cols = value.shape[-2], value.shape[-1]
        cells = value.size // (rows * cols) * (-(-rows // 16) * 16) * (-(-cols // LANES) * LANES)
        total += cells * jnp.dtype(value.dtype).itemsize
    return min(total + margin, 58 * 2**20)


def streamed(kernel, counts, late, early, *refs):
    n_in, n_out, n_scratch = counts
    ins, outs = list(refs[:n_in]), list(refs[n_in : n_in + n_out])
    scratch = refs[n_in + n_out : n_in + n_out + n_scratch]
    extra = refs[n_in + n_out + n_scratch :]
    arriving, leaving, left = {}, {}, []
    for at, which in enumerate(late):
        arriving[which] = pltpu.make_async_copy(ins[which], extra[at], extra[-1].at[at])
        arriving[which].start()
        ins[which] = extra[at]
    for at, which in enumerate(early, len(late)):
        leaving[which] = pltpu.make_async_copy(extra[at], outs[which], extra[-1].at[at])
        outs[which] = extra[at]

    def need(*those):
        for which in those:
            arriving.pop(which).wait()

    def ship(*those):
        for which in those:
            copy = leaving.pop(which)
            copy.start()
            left.append(copy)

    kernel(need, ship, *ins, *outs, *scratch)
    need(*list(arriving))
    ship(*list(leaving))
    for copy in left:
        copy.wait()


def on_chip(kernel, ins, outs, scratch, macs, exps=0, ahead=False, late=(), early=()):
    outs = [jax.ShapeDtypeStruct(shape, kind) for shape, kind in outs]
    held = [jax.ShapeDtypeStruct(shape, kind) for shape, kind in scratch]
    moved = sum(value.size * value.dtype.itemsize for value in list(ins) + outs)
    buffers = [pltpu.VMEM(shape, kind) for shape, kind in scratch]
    in_specs, out_specs = [WHOLE] * len(ins), [WHOLE] * len(outs)
    if late or early:
        counts = len(ins), len(outs), len(scratch)
        kernel = functools.partial(streamed, kernel, counts, late, early)
        for which in late:
            in_specs[which] = pl.BlockSpec(memory_space=pl.ANY)
            buffers.append(pltpu.VMEM(ins[which].shape, ins[which].dtype))
        for which in early:
            out_specs[which] = pl.BlockSpec(memory_space=pl.ANY)
            buffers.append(pltpu.VMEM(outs[which].shape, outs[which].dtype))
        buffers.append(pltpu.SemaphoreType.DMA((len(late) + len(early),)))
    return pl.pallas_call(
        kernel,
        in_specs=in_specs,
        out_specs=out_specs,
        out_shape=outs,
        scratch_shapes=buffers,
        cost_estimate=pl.CostEstimate(flops=2 * macs, bytes_accessed=moved, transcendentals=exps),
        compiler_params=pltpu.CompilerParams(
            vmem_limit_bytes=room(list(ins) + outs + held, 2 * MARGIN)
            if late or early
            else room(list(ins) + outs + held) if ahead else 58 * 2**20
        ),
    )(*ins)


def tiles(count, width, body):
    def step(at, carry):
        body(pl.ds(pl.multiple_of(at * width, width), width))
        return carry

    lax.fori_loop(0, count // width, step, 0)


def norm_back_rows(values_ref, grad_ref, gain, write, sums_ref, at):
    rows, width = values_ref.shape

    def step(number, carry):
        span = pl.ds(pl.multiple_of(number * CHUNK, CHUNK), CHUNK)
        values, grad = values_ref[span, :], grad_ref[span, :]
        centred = values - jnp.mean(values, -1, keepdims=True)
        rstd = lax.rsqrt(jnp.mean(centred * centred, -1, keepdims=True) + 1e-06)
        unit = centred * rstd
        scaled = grad * gain
        d_values = rstd * (
            scaled
            - jnp.mean(scaled, -1, keepdims=True)
            - unit * jnp.mean(scaled * unit, -1, keepdims=True)
        )
        write(span, d_values)
        return (
            carry[0] + jnp.sum(grad * unit, 0, keepdims=True),
            carry[1] + jnp.sum(grad, 0, keepdims=True),
        )

    blank = jnp.zeros((1, width), WIDE)
    gains, shifts = lax.fori_loop(0, rows // CHUNK, step, (blank, blank))
    sums_ref[at : at + 1, :] = gains
    sums_ref[at + 1 : at + 2, :] = shifts


def ff_side(branch, branch_t, normed_t, act, slope, down, d_pre, out):
    ff = act.shape[1]

    def body(span):
        d_act = mm(branch[...], down[:, span])
        values = (d_act * slope[:, span].astype(WIDE)).astype(LOW)
        d_pre[:, span] = values
        out[:, span] = mm(normed_t[...], values).astype(LOW)
        lower = pl.ds(pl.multiple_of(span.start + ff, LANES), span.size)
        out[:, lower] = mm(branch_t[...], act[:, span]).astype(LOW)

    tiles(ff, 768, body)


def ff_back_first_kernel(need, ship, *refs):
    d_inward, bridge_in, hidden, normed, eye, gains, act, slope, down = refs[0:9]
    out, d_hidden, branch, branch_t, normed_t, d_pre, sums, grad = refs[9:17]

    def first(span):
        grad[:, span] = mm_t(d_inward[...], bridge_in[span, :])

    tiles(D, 256, first)

    def write(span, values):
        d_hidden[span, :] = values
        branch[span, :] = values.astype(LOW)

    norm_back_rows(hidden, grad, gains[4:5, :], write, sums, 0)
    ship(1, 2)
    need(4, 3)
    branch_t[...] = mm_t(eye[...], branch[...]).astype(LOW)
    normed_t[...] = mm_t(eye[...], normed[...]).astype(LOW)
    ship(3, 4)
    need(8, 7, 6)
    ff_side(branch, branch_t, normed_t, act, slope, down, d_pre, out)


def ff_back_first(d_inward, bridge_in, hidden, normed, eye, gains, act, slope, down):
    rows, ff = act.shape
    return on_chip(
        ff_back_first_kernel,
        [d_inward, bridge_in, hidden, normed, eye, gains, act, slope, down],
        [((D, 2 * ff), LOW), ((rows, D), WIDE), ((rows, D), LOW)]
        + [((D, rows), LOW)] * 2
        + [((rows, ff), LOW), ((8, D), WIDE)],
        [((rows, D), WIDE)],
        4 * rows * D * ff,
        late=(4, 3, 8, 7, 6),
        early=(1, 2, 3, 4, 0, 5),
    )


def ff_back_second_kernel(need, ship, *refs):
    d_hidden, branch, branch_t, normed_t, d_pre_other, middle, gains = refs[0:7]
    act, slope, down, up_own, up_other, sums_first = refs[7:13]
    out, branch_out, d_middle, sums, grad, d_pre = refs[13:19]
    need(9, 8, 7)
    ff_side(branch, branch_t, normed_t, act, slope, down, d_pre, out)
    ship(0)
    need(10, 4, 11)

    def third(span):
        grad[:, span] = mm_t(d_pre[...], up_own[span, :]) + mm_t(d_pre_other[...], up_other[span, :])

    tiles(D, 768, third)
    need(5, 0)

    def write(span, values):
        values = values + d_hidden[span, :]
        d_middle[span, :] = values
        branch_out[span, :] = values.astype(LOW)

    norm_back_rows(middle, grad, gains[2:3, :], write, sums, 2)
    sums[0:2, :] = sums_first[0:2, :]


def ff_back_second(
    d_hidden,
    branch,
    branch_t,
    normed_t,
    d_pre,
    middle,
    gains,
    act,
    slope,
    down,
    up_own,
    up_other,
    sums,
):
    rows, ff = act.shape
    return on_chip(
        ff_back_second_kernel,
        [d_hidden, branch, branch_t, normed_t, d_pre, middle, gains, act, slope, down]
        + [up_own, up_other, sums],
        [((D, 2 * ff), LOW), ((rows, D), LOW), ((rows, D), WIDE), ((8, D), WIDE)],
        [((rows, D), WIDE), ((rows, ff), LOW)],
        5 * rows * D * ff,
        late=(9, 8, 7, 10, 4, 11, 5, 0),
        early=(0,),
    )


def attn_back_kernel(size, branch, ids_row, ids_col, *refs):
    rests, projs, mixeds, logs, d_projs = refs[0:2], refs[2:4], refs[4:6], refs[6:8], refs[8:10]
    d_mixed, bias, soft, d_scores = refs[10:14]
    width = D // 2
    bias[...] = jnp.where(ids_col[...] == ids_row[...], 0.0, -1e30)
    for side in (0, 1):
        proj, mixed, log, d_proj = projs[side], mixeds[side], logs[side], d_projs[side]
        d_mixed[...] = mm(branch[...], rests[side][:, width : 2 * width]).astype(LOW)

        def step(block, carry, proj=proj, mixed=mixed, log=log, d_proj=d_proj):
            at = [pl.multiple_of(part * width + block * LANES, LANES) for part in range(3)]
            query, keys, values = [proj[:, pl.ds(col, LANES)] for col in at]
            d_out = d_mixed[:, pl.ds(at[0], LANES)]
            out = mixed[:, pl.ds(at[0], LANES)]
            found = []
            for number, low in enumerate(range(0, LANES, size)):
                cols = slice(low, low + size)
                found.append(
                    head_backward(
                        query[:, cols],
                        keys[:, cols],
                        values[:, cols],
                        d_out[:, cols],
                        out[:, cols],
                        log[number, pl.ds(block, 1), :],
                        bias,
                        soft,
                        d_scores,
                        size,
                    )
                )
            for col, parts in zip(at, zip(*found)):
                d_proj[:, pl.ds(col, LANES)] = jnp.concatenate(parts, -1)
            return carry

        lax.fori_loop(0, width // LANES, step, 0)


def attn_back(size, branch, ids, rests, projs, mixeds, logs):
    rows = branch.shape[0]
    return on_chip(
        functools.partial(attn_back_kernel, size),
        [branch, ids[None, :], ids[:, None], *rests, *projs, *mixeds, *logs],
        [(projs[0].shape, LOW)] * 2,
        [
            ((rows, D // 2), LOW),
            ((rows, rows), WIDE),
            ((rows, rows), LOW),
            ((rows, rows), LOW),
        ],
        rows * D * D + rows * rows * D * 5,
        rows * rows * D // size,
        ahead=True,
    )


def qkv_back_kernel(need, ship, *refs):
    branch, d_middle, start, normed, seen, eye, gains, sums_ff, sums_p, spread = refs[0:10]
    d_projs, mixeds, qkvs, orders = refs[10:12], refs[12:14], refs[14:16], refs[16:18]
    outs = refs[18:20]
    grad, flipped, d_start, sums = refs[20:24]
    width = D // 2
    rest = 3 * width
    flipped[...] = mm_t(eye[...], branch[...]).astype(LOW)
    need(12, 13)
    for side in (0, 1):
        outs[side][:, rest + width : rest + 2 * width] = mm(
            flipped[...], mixeds[side][...]
        ).astype(LOW)
    need(3)
    flipped[...] = mm_t(eye[...], normed[...]).astype(LOW)
    need(10, 11)
    for side in (0, 1):
        outs[side][:, 0:rest] = mm(flipped[...], d_projs[side][...]).astype(LOW)
    need(14, 15)
    grad[...] = mm_t(d_projs[0][...], qkvs[0][...]) + mm_t(d_projs[1][...], qkvs[1][...])

    def write(span, values):
        d_start[span, :] = (values + d_middle[span, :]).astype(LOW)

    need(1, 2)
    norm_back_rows(start, grad, gains[0:1, :], write, sums, 0)
    need(4)
    flipped[...] = mm_t(eye[...], seen[...]).astype(LOW)
    sums[2:4, :] = sums_ff[2:4, :]
    sums[4:6, :] = sums_ff[0:2, :]
    sums[6:8, :] = jnp.zeros((2, D), WIDE)
    rows = jnp.concatenate(
        [sums[...].astype(LOW), mm(sums_p[...].astype(LOW), spread[...]).astype(LOW)], 0
    )
    cols = t_mm(rows, eye[0:16, 0:LANES]).astype(LOW)
    need(16, 17)
    for side in (0, 1):
        moved = mm_t(d_start[...], orders[side][...]).astype(LOW)
        outs[side][:, rest : rest + width] = mm(flipped[...], moved).astype(LOW)
        outs[side][:, rest + 2 * width :] = cols


def qkv_back(branch, d_middle, start, normed, seen, eye, gains, sums_ff, sums_p, spread, pairs):
    rows, width = branch.shape[0], D // 2
    return on_chip(
        qkv_back_kernel,
        [branch, d_middle, start, normed, seen, eye, gains, sums_ff, sums_p, spread]
        + [value for pair in pairs for value in pair],
        [((D, 5 * width + LANES), LOW)] * 2,
        [((rows, D), WIDE), ((D, rows), LOW), ((rows, D), LOW), ((8, D), WIDE)],
        rows * D * D * 10,
        late=(12, 13, 3, 10, 11, 14, 15, 1, 2, 4, 16, 17),
    )


def row_spans(rows, chunk, body):
    def step(number, carry):
        body(pl.ds(pl.multiple_of(number * chunk, chunk), chunk))
        return carry

    lax.fori_loop(0, rows // chunk, step, 0)


def heads_forward(query_ref, keys_ref, values_ref, out_ref, logs_ref, bias, size, at):
    width = out_ref.shape[1]

    def step(block, carry):
        cols = [pl.multiple_of(first + block * LANES, LANES) for first in at]
        query = query_ref[:, pl.ds(cols[0], LANES)]
        keys = keys_ref[:, pl.ds(cols[1], LANES)]
        values = values_ref[:, pl.ds(cols[2], LANES)]
        found = []
        for number, low in enumerate(range(0, LANES, size)):
            part = slice(low, low + size)
            out, logs = head_forward(
                query[:, part], keys[:, part], values[:, part], bias, size
            )
            found.append(out)
            if logs_ref is not None:
                logs_ref[number, pl.ds(block, 1), :] = logs
        place_at = pl.ds(pl.multiple_of(block * LANES, LANES), LANES)
        out_ref[:, place_at] = jnp.concatenate(found, -1).astype(LOW)
        return carry

    lax.fori_loop(0, width // LANES, step, 0)


def ctx_first_kernel(need, ship, seen, pos, spread, *refs):
    orders, rests, qkvs = refs[0:2], refs[2:4], refs[4:6]
    start, normed, projs, outs, embed_w = refs[6], refs[7], refs[8:10], refs[10:13], refs[13]
    gains = outs[0]
    width = orders[0].shape[0]
    parts = rests[0][:, 2 * width :].astype(WIDE).T
    outs[0][...] = parts[0:8] + parts[8:16]
    outs[1][...] = parts[16:24] + parts[24:32]
    low = parts[32:48].astype(LOW)
    low = mm_t(low, spread[...])
    outs[2][...] = low[0:8] + low[8:16]
    embed_w[...] = (
        mm(rests[0][:, 0:width], orders[0][...]) + mm(rests[1][:, 0:width], orders[1][...])
    ).astype(LOW)
    need(0, 1)
    start[...] = mm(seen[...], embed_w[...]) + pos[...]
    ship(0)

    def first_norm(span):
        normed[span, :] = norm_rows(start[span, :], gains[0:1, :], gains[1:2, :]).astype(LOW)

    row_spans(seen.shape[0], CHUNK, first_norm)
    ship(1)
    for side in (0, 1):
        need(7 + side)
        projs[side][...] = mm(normed[...], qkvs[side][...]).astype(LOW)
        ship(2 + side)


def ctx_first(seen, pos, spread, orders, rests, qkvs):
    rows, width = seen.shape[0], orders[0].shape[0]
    return on_chip(
        ctx_first_kernel,
        [seen, pos, spread, *orders, *rests, *qkvs],
        [((rows, D), WIDE), ((rows, D), LOW)]
        + [((rows, 3 * width), LOW)] * 2
        + [((8, D), WIDE), ((8, D), WIDE), ((8, PW), WIDE)],
        [((D, D), LOW)],
        rows * D * D * 4 + D * D * D,
        late=(0, 1, 7, 8),
        early=(0, 1, 2, 3),
    )


def ctx_second_kernel(size, need, ship, start, gains, ids_row, ids_col, *refs):
    rests, projs = refs[0:2], refs[2:4]
    middle, normed_two, mixeds, logs, bias = refs[4], refs[5], refs[6:8], refs[8:10], refs[10]
    width = mixeds[0].shape[1]
    bias[...] = jnp.where(ids_col[...] == ids_row[...], 0.0, -1e30)
    for side in (0, 1):
        need(6 + side)
        proj = projs[side]
        heads_forward(
            proj, proj, proj, mixeds[side], logs[side], bias, size, (0, width, 2 * width)
        )
        ship(2 + side)
    need(4, 5, 0)
    middle[...] = (
        start[...]
        + mm_t(mixeds[0][...], rests[0][:, width : 2 * width])
        + mm_t(mixeds[1][...], rests[1][:, width : 2 * width])
    )

    def second_norm(span):
        normed_two[span, :] = norm_rows(middle[span, :], gains[2:3, :], gains[3:4, :]).astype(LOW)

    row_spans(start.shape[0], CHUNK, second_norm)


def ctx_second(size, start, gains, ids, rests, projs):
    rows, width = start.shape[0], D // 2
    return on_chip(
        functools.partial(ctx_second_kernel, size),
        [start, gains, ids[None, :], ids[:, None], *rests, *projs],
        [((rows, D), WIDE), ((rows, D), LOW)]
        + [((rows, width), LOW)] * 2
        + [((LANES // size, 8, rows), WIDE)] * 2,
        [((rows, rows), WIDE)],
        rows * D * D + rows * rows * D * 2,
        rows * rows * D // size,
        late=(6, 7, 4, 5, 0),
        early=(2, 3),
    )


def gelu_rows(pre_ref, act_ref, slope_ref, span):
    def body(rows):
        act, slope = gelu_both(pre_ref[rows, :])
        act_ref[rows, span] = act
        if slope_ref is not None:
            slope_ref[rows, span] = slope

    row_spans(pre_ref.shape[0], 32, body)


def ff_kernel(need, ship, *refs):
    normed, middle, gains, ups, downs = *refs[0:3], refs[3:5], refs[5:7]
    hidden, context, acts, slopes, pre = refs[7], refs[8], refs[9:11], refs[11:13], refs[13]
    rows, ff = acts[0].shape
    for side in (0, 1):
        need(3 + side)

        def first(span, side=side):
            pre[...] = mm(normed[...], ups[side][:, span])
            gelu_rows(pre, acts[side], slopes[side], span)

        tiles(ff, 512, first)
        ship(2 + side, 4 + side)
    need(5, 6, 1)
    hidden[...] = (
        middle[...] + mm_t(acts[0][...], downs[0][...]) + mm_t(acts[1][...], downs[1][...])
    )

    def last(span):
        context[span, :] = norm_rows(hidden[span, :], gains[4:5, :], gains[5:6, :]).astype(LOW)

    row_spans(rows, CHUNK, last)


def ff_forward(normed, middle, gains, ups, downs):
    rows, ff = normed.shape[0], ups[0].shape[1]
    return on_chip(
        ff_kernel,
        [normed, middle, gains, *ups, *downs],
        [((rows, D), WIDE), ((rows, D), LOW)] + [((rows, ff), LOW)] * 4,
        [((rows, 512), WIDE)],
        rows * D * ff * 4 + rows * D * D,
        rows * ff * 2,
        late=(3, 4, 5, 6, 1),
        early=(2, 3, 4, 5),
    )


def target_kernel(size, *refs):
    patch, seen, pos_all, pos_tgt, gains, ids_row, ids_col = refs[0:7]
    orders, weights, (t_middle, t_two) = refs[7:9], refs[9:11], refs[11:13]
    embed_w, hidden, normed, start, query, keys, mixed, bias = refs[13:]
    width = D // 2
    own, other = [part[:, 3 * width : 4 * width] for part in weights]
    embed_w[...] = (mm(own, orders[0][...]) + mm(other, orders[1][...])).astype(LOW)
    hidden[...] = mm(patch[...], embed_w[...]) + pos_all[...]

    def first_norm(span):
        normed[span, :] = norm_rows(hidden[span, :], gains[0:1, :], gains[1:2, :]).astype(LOW)

    row_spans(patch.shape[0], 112, first_norm)
    start[...] = mm(seen[...], embed_w[...]) + pos_tgt[...]
    t_normed = norm_rows(start[...], gains[0:1, :], gains[1:2, :]).astype(LOW)
    bias[...] = jnp.where(ids_col[...] == ids_row[...], 0.0, -1e30)
    total = start[...]
    for part in weights:
        query[...] = mm(t_normed, part[:, 0:width]).astype(LOW)
        keys[...] = mm(normed[...], part[:, width : 3 * width]).astype(LOW)
        heads_forward(query, keys, keys, mixed, None, bias, size, (0, 0, width))
        total = total + mm_t(mixed[...], part[:, 4 * width : 5 * width])
    t_middle[...] = total
    t_two[...] = norm_rows(total, gains[2:3, :], gains[3:4, :]).astype(LOW)


def target_forward(
    size, patch, seen, pos_all, pos_tgt, gains, idq, idk, orders, weights
):
    rows, count, width = seen.shape[0], patch.shape[0], D // 2
    return on_chip(
        functools.partial(target_kernel, size),
        [patch, seen, pos_all, pos_tgt, gains, idq[None, :], idk[:, None], *orders, *weights],
        [((rows, D), WIDE), ((rows, D), LOW)],
        [
            ((D, D), LOW),
            ((count, D), WIDE),
            ((count, D), LOW),
            ((rows, D), WIDE),
            ((rows, width), LOW),
            ((count, 2 * width), LOW),
            ((rows, width), LOW),
            ((count, rows), WIDE),
        ],
        count * D * D * 3 + rows * D * D * 3 + 2 * rows * count * D,
        rows * count * D // size,
        ahead=True,
    )


def pred_forward_kernel(size, *refs):
    context, bridge_in, bridge_out, pos, gains, ids_row, ids_col = refs[0:7]
    downs, ups, qks, rights = refs[7:9], refs[9:11], refs[11:13], refs[13:15]
    joined, normed, middle, normed_two, predicted, final, guess = refs[15:22]
    out_qk, out_v, mixeds, acts, slopes = (
        refs[22:24],
        refs[24:26],
        refs[26:28],
        refs[28:30],
        refs[30:32],
    )
    logs, bias = refs[32], refs[33]
    width = out_v[0].shape[1]
    joined[0:CTX, :] = mm(context[...], bridge_in[...]) + pos[0:CTX, :]
    joined[CTX:, :] = gains[6:7, :] + pos[CTX:, :]

    def first(span):
        normed[span, :] = norm_rows(joined[span, :], gains[0:1, :], gains[1:2, :]).astype(LOW)

    row_spans(joined.shape[0], 128, first)
    bias[...] = jnp.where(ids_col[...] == ids_row[...], 0.0, -1e30)
    total = joined[CTX:, :]
    head = 0
    for qk, right, qk_ref, v_ref, mixed in zip(qks, rights, out_qk, out_v, mixeds):
        qk_ref[...] = mm(normed[...], qk[...]).astype(LOW)
        v_ref[...] = mm(normed[...], right[:, 0:width]).astype(LOW)
        found = []
        for low in range(0, width, size):
            out, log = head_forward(
                qk_ref[CTX:, low : low + size],
                qk_ref[:, width + low : width + low + size],
                v_ref[:, low : low + size],
                bias,
                size,
            )
            found.append(out)
            logs[head : head + 1, :] = log
            head += 1
        mixed[...] = jnp.concatenate(found, -1).astype(LOW)
        total = total + mm_t(mixed[...], right[:, width:])
    middle[...] = total
    normed_two[...] = norm_rows(total, gains[2:3, :], gains[3:4, :]).astype(LOW)
    total = middle[...]
    for up, down, act, slope in zip(ups, downs, acts, slopes):
        values, tilt = gelu_both(mm(normed_two[...], up[...]))
        act[...] = values
        slope[...] = tilt
        total = total + mm_t(act[...], down[...])
    predicted[...] = total
    final[...] = norm_rows(total, gains[4:5, :], gains[5:6, :]).astype(LOW)
    guess[...] = mm_t(final[...], bridge_out[...])


def pred_forward(
    size, context, bridge_in, bridge_out, pos, gains, idq, idk, downs, ups, qks, rights
):
    rows, count, width, ff = idq.shape[0], idk.shape[0], qks[0].shape[1] // 2, ups[0].shape[1]
    low, wide = LOW, WIDE
    return on_chip(
        functools.partial(pred_forward_kernel, size),
        [context, bridge_in, bridge_out, pos, gains, idq[None, :], idk[:, None]]
        + [*downs, *ups, *qks, *rights],
        [((count, PW), wide), ((count, PW), low), ((rows, PW), wide), ((rows, PW), low)]
        + [((rows, PW), wide), ((rows, PW), low), ((rows, D), wide)]
        + [((count, 2 * width), low)] * 2
        + [((count, width), low)] * 2
        + [((rows, width), low)] * 2
        + [((rows, ff), low)] * 4
        + [((16, rows), wide)],
        [((count, rows), wide)],
        1_000_000_000,
        rows * count * PW // size,
    )


def target_ff_kernel(last, need, ship, t_two, start, gains, up, down, target, pre, act):
    need(3)

    def first(span):
        pre[...] = mm(t_two[...], up[:, span])
        gelu_rows(pre, act, None, span)

    tiles(act.shape[1], 512, first)
    need(4)
    total = start[...] + mm_t(act[...], down[...])
    if last:
        total = norm_rows(total, gains[4:5, :], gains[5:6, :])
        total = norm_rows(total, 1.0, 0.0)
    target[...] = total


def target_ff(last, t_two, start, gains, up, down):
    rows, ff = t_two.shape[0], up.shape[1]
    return on_chip(
        functools.partial(target_ff_kernel, last),
        [t_two, start, gains, up, down],
        [((rows, D), WIDE)],
        [((rows, 512), WIDE), ((rows, ff), LOW)],
        rows * D * ff * 2,
        rows * ff,
        late=(3, 4),
    )[0]


def pred_back_all_kernel(size, count_all, dp_count, *refs):
    (guess, target, used, context, final, bridge_in, bridge_out, gains, ids_row, ids_col) = refs[
        0:10
    ]
    predicted, middle, joined, normed, normed_two = refs[10:15]
    downs, ups, qks, rights = refs[15:17], refs[17:19], refs[19:21], refs[21:23]
    acts, slopes, in_qk, in_v, mixeds = (
        refs[23:25],
        refs[25:27],
        refs[27:29],
        refs[29:31],
        refs[31:33],
    )
    logs = refs[33]
    p_order, side_ref, loss, d_inward, sums = refs[34:39]
    packs = refs[39:41]
    d_qk, d_v, d_normed, bias, soft, d_scores, g_bridge_out = refs[41:48]
    p_rows = PW // dp_count
    half = packs[0].shape[2] // 2

    def put(side, column, values):
        for block in range(dp_count):
            part = values[block * p_rows : (block + 1) * p_rows]
            packs[side][block, :, column : column + values.shape[1]] = part.astype(LOW)

    width = in_v[0].shape[1]
    ff = acts[0].shape[1]
    diff = guess[...] - target[...]
    size_abs = jnp.abs(diff)
    keep = lax.broadcasted_iota(jnp.int32, diff.shape, 0) < used[0]
    terms = jnp.where(
        keep, jnp.where(size_abs < 1.0, 0.5 * diff * diff, size_abs - 0.5), 0.0
    )
    loss[...] = jnp.sum(jnp.sum(terms, 0, keepdims=True), 1, keepdims=True)
    d_guess = jnp.where(keep, jnp.clip(diff, -1.0, 1.0) / count_all, 0.0).astype(LOW)
    g_bridge_out[...] = t_mm(d_guess, final[...]).astype(LOW)

    def back(values, gain, grad, at):
        d_values, gain_sum, shift_sum = norm_back(values, gain, grad)
        sums[at : at + 1, :] = gain_sum[None, :]
        sums[at + 1 : at + 2, :] = shift_sum[None, :]
        return d_values

    d_tail = back(predicted[...], gains[4:5, :], mm(d_guess, bridge_out[...]), 4)
    branch = d_tail.astype(LOW)
    total = None
    for side in (0, 1):
        d_pre = (mm(branch, downs[side][...]) * slopes[side][...].astype(WIDE)).astype(LOW)
        put(side, 0, t_mm(branch, acts[side][...]))
        put(side, half, t_mm(normed_two[...], d_pre))
        part = mm_t(d_pre, ups[side][...])
        total = part if total is None else total + part
    d_middle = d_tail + back(middle[...], gains[2:3, :], total, 2)
    branch = d_middle.astype(LOW)
    bias[...] = jnp.where(ids_col[...] == ids_row[...], 0.0, -1e30)
    total = None
    head = 0
    for side in (0, 1):
        qk_ref, v_ref, right = in_qk[side], in_v[side], rights[side]
        d_mixed = mm(branch, right[:, width:]).astype(LOW)
        put(side, half + ff + width, t_mm(branch, mixeds[side][...]))
        found = []
        for low in range(0, width, size):
            found.append(
                head_backward(
                    qk_ref[CTX:, low : low + size],
                    qk_ref[:, width + low : width + low + size],
                    v_ref[:, low : low + size],
                    d_mixed[:, low : low + size],
                    mixeds[side][:, low : low + size],
                    logs[head : head + 1, :],
                    bias,
                    soft,
                    d_scores,
                    size,
                )
            )
            head += 1
        d_query, d_keys, d_values = [jnp.concatenate(parts, -1) for parts in zip(*found)]
        d_qk[0:CTX, 0:width] = jnp.zeros((CTX, width), LOW)
        d_qk[CTX:, 0:width] = d_query
        d_qk[:, width:] = d_keys
        d_v[...] = d_values
        put(side, ff, t_mm(normed[...], d_qk[...]))
        put(side, half + ff, t_mm(normed[...], d_v[...]))
        part = mm_t(d_qk[...], qks[side][...]) + mm_t(d_v[...], right[:, 0:width])
        d_normed[...] = part if side == 0 else d_normed[...] + part
    d_joined = back(joined[...], gains[0:1, :], d_normed[...], 0)
    sums[6:7, :] = jnp.sum(d_joined[CTX:] + d_middle, 0, keepdims=True)
    sums[7:8, :] = jnp.zeros((1, PW), WIDE)
    d_inward[...] = d_joined[0:CTX].astype(LOW)
    g_in = mm_t(t_mm(context[...], d_inward[...]).astype(LOW), p_order[...])
    g_out = mm_t(g_bridge_out[...], p_order[...])
    flip = side_ref[0] != 0
    at = ff + 2 * width
    for side, values in ((0, jnp.where(flip, g_out, g_in)), (1, jnp.where(flip, g_in, g_out))):
        for block in range(dp_count):
            for low in (0, 1):
                start = (2 * block + low) * p_rows
                packs[side][block, :, low * half + at : (low + 1) * half] = values[
                    start : start + p_rows
                ].astype(LOW)


def pred_back_all(size, count_all, dp_count, side, order, used, values, pairs, logs, idq, idk):
    (guess, target, context, final, bridge_in, bridge_out, gains) = values[:7]
    ff, width, count = pairs[0][0].shape[1], pairs[2][0].shape[1] // 2, idk.shape[0]
    ins = [guess, target, used, context, final, bridge_in, bridge_out, gains]
    ins += [idq[None, :], idk[:, None], *values[7:]] + [part for pair in pairs for part in pair]
    ins += [logs, order, side]
    outs = [((1, 1), WIDE), ((CTX, PW), LOW), ((8, PW), WIDE)]
    outs += [((dp_count, PW // dp_count, 2 * (ff + 2 * width) + D), LOW)] * 2
    specs = [WHOLE] * len(ins)
    specs[2] = specs[-1] = pl.BlockSpec(memory_space=pltpu.SMEM)
    return pl.pallas_call(
        functools.partial(pred_back_all_kernel, size, count_all, dp_count),
        in_specs=specs,
        out_specs=[WHOLE] * len(outs),
        out_shape=[jax.ShapeDtypeStruct(shape, kind) for shape, kind in outs],
        scratch_shapes=[
            pltpu.VMEM((count, 2 * width), LOW),
            pltpu.VMEM((count, width), LOW),
            pltpu.VMEM((count, PW), WIDE),
            pltpu.VMEM((count, idq.shape[0]), WIDE),
            pltpu.VMEM((count, idq.shape[0]), LOW),
            pltpu.VMEM((count, idq.shape[0]), LOW),
            pltpu.VMEM((D, PW), LOW),
        ],
        cost_estimate=pl.CostEstimate(
            flops=4_000_000_000, bytes_accessed=20_000_000, transcendentals=3_000_000
        ),
        compiler_params=pltpu.CompilerParams(vmem_limit_bytes=58 * 2**20),
    )(*ins)


def pred_parts_kernel(dp_count, side_ref, own, other, order, *outs):
    width, half = PW // 2, D // 2
    ff = D
    flip = side_ref[0] != 0
    low = jnp.where(flip, other[:, 0:half], own[:, 0:half])
    high = jnp.where(flip, own[:, 0:half], other[:, 0:half])
    outs[0][...] = mm(low, order[...]).astype(LOW)
    outs[1][...] = mm(high, order[...]).astype(LOW)
    rows = PW // dp_count
    for at, ref in enumerate((own, other)):
        for start, wide, out in ((half, ff, 2), (half + ff, 2 * width, 6)):
            blocks = ref[:, start : start + wide].astype(WIDE).reshape(dp_count, 2 * rows, wide)
            outs[out + at][...] = blocks[:, :rows].reshape(PW, wide).astype(LOW)
            outs[out + 2 + at][...] = blocks[:, rows:].reshape(PW, wide).astype(LOW)


def pred_parts(dp_count, side, own, other, order):
    width, half = PW // 2, D // 2
    if PW // dp_count % 8:
        bridges = [part[:, :half] for part in (own, other)]
        first = side == 0
        found = [
            mm(jnp.where(first, bridges[at], bridges[1 - at]), order).astype(LOW) for at in (0, 1)
        ]
        for start, wide in ((half, D), (half + D, 2 * width)):
            cols = [part[:, start : start + wide] for part in (own, other)]
            cols = [part.reshape(dp_count, 2, PW // dp_count, wide) for part in cols]
            found += [flat(part[:, which]) for which in (0, 1) for part in cols]
    else:
        ins = [side[None], own, other, order]
        shapes = [(D, PW)] * 2 + [(PW, D)] * 4 + [(PW, 2 * width)] * 4
        outs = [jax.ShapeDtypeStruct(shape, LOW) for shape in shapes]
        found = pl.pallas_call(
            functools.partial(pred_parts_kernel, dp_count),
            in_specs=[pl.BlockSpec(memory_space=pltpu.SMEM)] + [WHOLE] * 3,
            out_specs=[WHOLE] * len(outs),
            out_shape=outs,
            cost_estimate=pl.CostEstimate(
                flops=1_000_000_000, bytes_accessed=9_000_000, transcendentals=0
            ),
            compiler_params=pltpu.CompilerParams(vmem_limit_bytes=58 * 2**20),
        )(*ins)
    return found[0], found[1], [found[at : at + 2] for at in range(2, 10, 2)]


class Lines:
    def __init__(self, count):
        self.count = count
        self.stride = count // 4
        bits = list(range(self.stride.bit_length() - 1))
        turn = len(bits) // 2
        self.bits = bits
        self.orders = (bits, bits[turn:] + bits[:turn])
        self.turn = turn

    def flip(self, values, bit):
        pairs = [(at, at ^ (1 << bit)) for at in range(self.count)]
        return lax.ppermute(values, "dp", pairs)

    def shift(self, values, steps):
        pairs = [(at, (at + steps * self.stride) % self.count) for at in range(self.count)]
        return lax.ppermute(values, "dp", pairs)

    def add_all(self, values, low, high):
        total = values
        for change in range(1, 1 << (high - low)):
            pairs = [(at, at ^ (change << low)) for at in range(2 * self.count)]
            total = total + lax.ppermute(values, ("dp", "mp"), pairs)
        return total

    def order(self, index, width):
        rows = width // self.count
        column = jnp.arange(width)
        block = column // rows
        far = (block // self.stride - index // self.stride) % 4
        near = (block ^ index) % self.stride
        target = (near * 4 + far) * rows + column % rows
        return (target[:, None] == column).astype(LOW)


def swap(values):
    return lax.ppermute(values, "mp", [(0, 1), (1, 0)])


def swap_all(values):
    return [swap(value) for value in values]


def far_kernel(*refs):
    outs = refs[4:]
    cut = outs[0].shape[-1]
    for at, block in enumerate(refs[:4]):
        outs[0][at] = block[:, :cut]
        outs[1][at] = block[:, cut:]


def gather_far(lines, shards):
    wide = jnp.concatenate(shards, 1)
    found = [wide] + [lines.shift(wide, -steps) for steps in (1, 2, 3)]
    rows, cut = shards[0].shape
    cols = [slice(0, cut), slice(cut, wide.shape[1])]
    if rows % 16:
        return [jnp.stack([block[:, part] for block in found]) for part in cols]
    return on_chip(
        far_kernel,
        found,
        [((4, rows, part.stop - part.start), LOW) for part in cols],
        [],
        0,
        ahead=True,
    )


def stack_kernel(axes, *refs):
    count = len(axes)
    ins, outs, bufs, sems = refs[: 2 * count], refs[2 * count : 3 * count], refs[3 * count : -1], refs[-1]
    arriving = [
        pltpu.make_async_copy(ins[at], bufs[at], sems.at[at]) for at in range(2 * count)
    ]
    for copy in arriving:
        copy.start()
    leaving = []
    for at, copy in enumerate(arriving):
        copy.wait()
        where = (slice(None),) * axes[at % count] + (at // count,)
        out = pltpu.make_async_copy(
            bufs[at], outs[at % count].at[where], sems.at[2 * count + at]
        )
        out.start()
        leaving.append(out)
    for copy in leaving:
        copy.wait()


def stack_pairs(held, got, axes):
    anywhere = pl.BlockSpec(memory_space=pl.ANY)
    ins = [*held, *got]
    outs = [
        jax.ShapeDtypeStruct(values.shape[:axis] + (2,) + values.shape[axis:], LOW)
        for values, axis in zip(held, axes)
    ]
    return pl.pallas_call(
        functools.partial(stack_kernel, axes),
        in_specs=[anywhere] * len(ins),
        out_specs=[anywhere] * len(outs),
        out_shape=outs,
        scratch_shapes=[pltpu.VMEM(value.shape, LOW) for value in ins]
        + [pltpu.SemaphoreType.DMA((2 * len(ins),))],
        cost_estimate=pl.CostEstimate(
            flops=0, bytes_accessed=8 * sum(value.size for value in ins), transcendentals=0
        ),
        compiler_params=pltpu.CompilerParams(vmem_limit_bytes=20 * 2**20),
    )(*ins)


def gather_near(lines, held, phase):
    done = [list(order[: lines.turn]) if phase else [] for order in lines.orders]
    steps = [order[lines.turn :] if phase else order[: lines.turn] for order in lines.orders]
    for bits in zip(*steps):
        got = [lines.flip(values, bit) for values, bit in zip(held, bits)]
        axes = [sum(1 for other in had if other > bit) for had, bit in zip(done, bits)]
        if phase and held[0].shape[-2] % 16 == 0:
            held = stack_pairs(held, got, axes)
        else:
            held = [
                jnp.stack([values, other], axis) for values, other, axis in zip(held, got, axes)
            ]
        for had, bit in zip(done, bits):
            had.append(bit)
    return list(held)


def flat(values):
    return values.reshape(-1, values.shape[-1])


class Box:
    def __init__(self, value):
        self.value, self.held = value, False


def sum_kernel(plan, squares, *refs):
    operands = 1 + max(term[0] for pieces in plan for piece in pieces for term in piece)
    if squares:
        refs[-1][...] = jnp.zeros((1, LANES), WIDE)
    for pieces, out in zip(plan, refs[operands:]):
        for lead in itertools.product(*[range(size) for size in out.shape[:-2]]):
            at = 0
            for piece in pieces:
                total = None
                for operand, low, high in piece:
                    part = refs[operand][lead + (slice(None), slice(low, high))].astype(WIDE)
                    total = part if total is None else total + part
                wide = high - low
                out[lead + (slice(None), slice(at, at + wide))] = total.astype(out.dtype)
                if squares:
                    for col in range(0, wide, LANES):
                        part = total[:, col : col + LANES]
                        weight = 0.5 if at + col == squares[1] and wide == squares[0] else 1.0
                        refs[-1][...] += weight * jnp.sum(part * part, 0, keepdims=True)
                at += wide


def sum_parts(outs, kind, squares=None):
    operands, specs, plan, shapes = [], [], [], []
    known = {}
    for pieces in outs:
        row = []
        for piece in pieces:
            terms = []
            for box, taken, (low, high) in piece:
                if (id(box), taken) not in known:
                    known[id(box), taken] = len(operands)
                    value = box.value
                    block = [
                        size if pick is None else None for size, pick in zip(value.shape, taken)
                    ]
                    where = tuple(0 if pick is None else pick for pick in taken) + (0, 0)
                    operands.append(value)
                    specs.append(
                        pl.BlockSpec(
                            tuple(block) + value.shape[-2:], lambda step, where=where: where
                        )
                    )
                terms.append((known[id(box), taken], low, high))
            row.append(tuple(terms))
        plan.append(tuple(row))
        box, taken, cols = pieces[0][0]
        lead = tuple(size for size, pick in zip(box.value.shape, taken) if pick is None)
        wide = sum(piece[0][2][1] - piece[0][2][0] for piece in pieces)
        shapes.append(
            jax.ShapeDtypeStruct(lead + (box.value.shape[-2], wide), kind)
        )
    moved = 8 * sum(shape.size for shape in shapes)
    if squares:
        shapes.append(jax.ShapeDtypeStruct((1, LANES), WIDE))
    return pl.pallas_call(
        functools.partial(sum_kernel, tuple(plan), squares),
        grid=(1,),
        in_specs=specs,
        out_specs=[
            pl.BlockSpec(shape.shape, lambda step, rank=len(shape.shape): (0,) * rank)
            for shape in shapes
        ],
        out_shape=shapes,
        cost_estimate=pl.CostEstimate(flops=moved, bytes_accessed=moved, transcendentals=0),
        compiler_params=pltpu.CompilerParams(vmem_limit_bytes=34 * 2**20),
    )(*operands)


class Terms:
    def __init__(self, lines, order, cols):
        self.lines, self.order, self.cols, self.left = lines, order, cols, list(lines.bits)
        self.terms = []

    def take(self, axis, at):
        found = []
        for box, taken, cols in self.terms:
            open_axes = [place_at for place_at, pick in enumerate(taken) if pick is None]
            picked = list(taken)
            picked[open_axes[axis]] = at
            found.append((box, tuple(picked), cols))
        return found

    def near_job(self, phase):
        turn = self.lines.turn
        (self.bit,) = self.order[turn:] if phase else self.order[:turn]
        self.axis = sum(1 for other in self.left if other > self.bit)
        return self.take(self.axis, 1)

    def near_send(self, send):
        got = self.lines.flip(send, self.bit)
        self.left.remove(self.bit)
        self.terms = self.take(self.axis, 0)
        self.terms.append((Box(got), (None,) * (got.ndim - 2), (0, got.shape[-1])))


class Sums:
    def __init__(self, lines, own, other, cut, rows):
        self.lines, self.rows, self.cut = lines, rows, cut
        self.plain = len(lines.bits) != 2
        self.own, self.other = Box(own), Box(other)
        self.lead = (2,) * len(lines.bits) + (4,)
        self.wide = own.shape[-1]
        self.parts = [
            Terms(lines, order, cols)
            for order, cols in zip(lines.orders, ((0, cut), (cut, self.wide)))
        ]

    def shaped(self, values):
        return values.reshape(self.lead + (self.rows, self.wide))

    def boxes(self):
        found = [self.own, self.other]
        for part in self.parts:
            found += [term[0] for term in part.terms]
        return found

    def swap(self, got=None):
        if self.plain:
            return
        mine = Box(self.shaped(self.own.value))
        mine.held = True
        if got is None:
            got = swap(self.other.value)
        self.other.held = True
        got = Box(self.shaped(got))
        for part in self.parts:
            blank = (None,) * len(self.lead)
            part.terms = [(mine, blank, part.cols), (got, blank, part.cols)]

    def far_jobs(self):
        return [[part.take(0, steps) for part in self.parts] for steps in (1, 2, 3)]

    def far_send(self, sends):
        got = [Box(self.lines.shift(send, steps)) for send, steps in zip(sends, (1, 2, 3))]
        for part in self.parts:
            part.terms = part.take(0, 0) + [(box, (), part.cols) for box in got]

    def results(self, halved=(0, -1)):
        if not self.plain:
            return sum_parts([[part.terms] for part in self.parts], WIDE, halved)
        results = []
        both = self.own.value.astype(WIDE) + swap(self.other.value).astype(WIDE)
        for part in self.parts:
            total = self.shaped(both)[..., part.cols[0] : part.cols[1]]
            for bit in part.order:
                axis = sum(1 for other in part.left if other > bit)
                part.left.remove(bit)
                sent = lax.index_in_dim(total, 1, axis, keepdims=False).astype(LOW)
                total = lax.index_in_dim(total, 0, axis, keepdims=False)
                total = total + self.lines.flip(sent, bit).astype(WIDE)
            result = total[0]
            for steps in (1, 2, 3):
                got = self.lines.shift(total[steps].astype(LOW), steps)
                result = result + got.astype(WIDE)
            results.append(result)
        squares = sum(jnp.sum(result * result) for result in results)
        for result in results:
            if result.shape[1] == halved[0]:
                part = result[:, halved[1] : halved[1] + LANES]
                squares = squares - 0.5 * jnp.sum(part * part)
        return results + [jnp.pad(squares.reshape(1, 1), ((0, 0), (0, LANES - 1)))]


def move(*steps, hold=None):
    work = []
    for total, kind in steps:
        if total.plain:
            continue
        if kind == 2:
            work.append((total.far_send, total.far_jobs()))
        else:
            for part in total.parts:
                work.append((part.near_send, [[part.near_job(kind)]]))
    if not work:
        return hold
    sends = sum_parts([job for send, jobs in work for job in jobs], LOW)
    if hold is not None:
        sends, hold = lax.optimization_barrier((sends, hold))
    at = 0
    for send, jobs in work:
        found = sends[at : at + len(jobs)]
        at += len(jobs)
        send(found if len(jobs) > 1 else found[0])
    return hold


def fence_sums(sums, *values):
    boxes = {id(box): box for one in sums for box in one.boxes() if not box.held}
    boxes = list(boxes.values())
    held, values = lax.optimization_barrier(([box.value for box in boxes], values))
    for box, value in zip(boxes, held):
        box.value, box.held = value, True
    return values


def fence(*values):
    return lax.optimization_barrier(values)


def adam(weight, moment_one, moment_two, gradient, decay, rate):
    moment_one = BETA_ONE * moment_one + (1.0 - BETA_ONE) * gradient
    moment_two = BETA_TWO * moment_two + (1.0 - BETA_TWO) * gradient * gradient
    fixed_one = moment_one / (1.0 - BETA_ONE**STEP)
    fixed_two = moment_two / (1.0 - BETA_TWO**STEP)
    weight = weight - rate * (fixed_one / (jnp.sqrt(fixed_two) + EPSILON) + decay * weight)
    return [weight, moment_one, moment_two]


def adam_kernel(plan, scalars, side, *refs):
    count = len(plan)
    grads = refs[3 * count : -3 * count]
    total = jnp.sum(scalars[0:1, :], 1, keepdims=True)
    factor = jnp.minimum(1.0, CLIP_NORM / (jnp.sqrt(total) + 1e-06))
    for at, (rate, decay, pieces) in enumerate(plan):
        ins = refs[3 * at : 3 * at + 3]
        outs = refs[len(refs) - 3 * count + 3 * at :][:3]
        for grad, rows_from, cols_from, rows, cols in pieces:
            if isinstance(cols[0], bool):
                half = side[0] if cols[0] else 1 - side[0]
                span = pl.ds(pl.multiple_of(half * cols[1], LANES), cols[1])
            else:
                span = slice(*cols)
            where = (slice(*rows), span)
            gradient = grads[grad][slice(*rows_from), slice(*cols_from)] * factor
            results = adam(*[ref[where] for ref in ins], gradient, decay, rate)
            for out, result in zip(outs, results):
                out[where] = result


def adam_all(scalars, side, groups, grads, plan):
    outs = [jax.ShapeDtypeStruct(group[0].shape, WIDE) for group in groups for at in range(3)]
    scalar = pl.BlockSpec(memory_space=pltpu.SMEM)
    ins = [value for group in groups for value in group] + list(grads)
    found = pl.pallas_call(
        functools.partial(adam_kernel, plan),
        in_specs=[WHOLE, scalar] + [WHOLE] * len(ins),
        out_specs=[WHOLE] * len(outs),
        out_shape=outs,
        cost_estimate=pl.CostEstimate(
            flops=20_000_000, bytes_accessed=10_000_000, transcendentals=400_000
        ),
        compiler_params=pltpu.CompilerParams(vmem_limit_bytes=58 * 2**20),
    )(scalars, side, *ins)
    return [found[at : at + 3] for at in range(0, len(found), 3)]


def two_parts(values):
    high = lax.reduce_precision(values, 8, 7)
    fill = ((0, 0), (0, 8 - values.shape[1]))
    return jnp.concatenate([jnp.pad(high, fill), jnp.pad(values - high, fill)], 1).astype(LOW)


def widen_rows(values, rows):
    return jnp.pad(values, ((0, rows - values.shape[0]), (0, 0)))


def shards(
    patches,
    ctx_index,
    tgt_index,
    group,
    tgt_count,
    embed,
    embed_m,
    embed_v,
    bridge,
    bridge_m,
    bridge_v,
    enc_in,
    enc_in_m,
    enc_in_v,
    enc_out,
    enc_out_m,
    enc_out_v,
    enc_gains,
    enc_gains_m,
    enc_gains_v,
    pred_in,
    pred_in_m,
    pred_in_v,
    pred_out,
    pred_out_m,
    pred_out_v,
    pred_gains,
    pred_gains_m,
    pred_gains_v,
    t_embed,
    t_in,
    t_out,
    t_gains,
):
    index = lax.axis_index("dp")
    side = lax.axis_index("mp")
    dp_count = lax.axis_size("dp")
    lines = Lines(dp_count)
    assert patches.shape[0] == lax.axis_size("mp")
    count = patches.shape[0] * dp_count * TGT * D
    rows = D // dp_count
    p_rows = PW // dp_count
    half_d = D // 2
    local = D // 2
    ff = enc_in.shape[1] - 3 * local
    p_local = PW // 2
    p_ff = pred_in.shape[1] - 3 * p_local
    first = side == 0
    size = D // HEADS
    p_size = PW // PHEADS

    def own_half(values):
        return lax.dynamic_slice_in_dim(values, side * half_d, half_d, 1).astype(LOW)

    gains_pack = jnp.concatenate(
        [
            two_parts(enc_gains.T),
            two_parts(t_gains.T),
            widen_rows(two_parts(pred_gains.T), rows),
            jnp.zeros((rows, LANES - 48), LOW),
        ],
        1,
    )
    enc_in_low, t_in_low = enc_in.astype(LOW), t_in.astype(LOW)
    enc_out_low, t_out_low = enc_out.T.astype(LOW), t_out.T.astype(LOW)
    pred_in_low, pred_out_low = pred_in.astype(LOW), pred_out.T.astype(LOW)
    pred_main = jnp.concatenate([pred_out_low[:, p_local:], pred_in_low[:, 3 * p_local :]], 0)
    pred_rest = jnp.concatenate(
        [
            pred_in_low[:, : 2 * p_local],
            jnp.concatenate(
                [pred_in_low[:, 2 * p_local : 3 * p_local], pred_out_low[:, :p_local]], 1
            ),
        ],
        0,
    )
    packs = [
        [
            enc_in_low[:, : 3 * local],
            jnp.concatenate([own_half(embed), enc_out_low[:, :local], gains_pack], 1),
        ],
        [
            jnp.concatenate(
                [t_in_low[:, : 3 * local], own_half(t_embed), t_out_low[:, :local]], 1
            ),
            jnp.concatenate([own_half(bridge), pred_main, pred_rest], 1),
        ],
        [enc_in_low[:, 3 * local :], enc_out_low[:, local:]],
        [t_in_low[:, 3 * local :], t_out_low[:, local:]],
    ]

    far_a = gather_far(lines, packs[0])
    far_a, packs[1] = fence(far_a, packs[1])
    near_a = gather_near(lines, far_a, 0)
    near_a, packs[1], patches, ctx_index, tgt_index, group, tgt_count = fence(
        near_a, packs[1], patches, ctx_index, tgt_index, group, tgt_count
    )
    order = lines.order(index, D)
    p_order = lines.order(index, PW)
    eye = jnp.eye(D, dtype=LOW)
    patch = lax.dynamic_index_in_dim(patches, side, 0, keepdims=False)
    ctx = lax.dynamic_index_in_dim(ctx_index, side, 0, keepdims=False)
    tgt = lax.dynamic_index_in_dim(tgt_index, side, 0, keepdims=False)
    single = lax.dynamic_index_in_dim(group, side, 0, keepdims=False) == 1
    used = lax.dynamic_index_in_dim(tgt_count, side, 0, keepdims=False)
    positions = jnp.arange(patch.shape[0])
    chosen = jnp.concatenate([ctx, tgt])
    all_id, all_row, all_col = place(single, positions)
    joined_id, joined_row, joined_col = place(single, chosen)
    ctx_id, tgt_id = joined_id[:CTX], joined_id[CTX:]

    spread = jnp.arange(D) // rows * p_rows + jnp.arange(D) % rows
    spread = (jnp.arange(PW)[:, None] == spread) & (jnp.arange(D) % rows < p_rows)
    spread = spread.astype(LOW)
    pos_all = sincos(all_row, all_col, D, order)
    pos_ctx = sincos(joined_row[:CTX], joined_col[:CTX], D, order)
    pos_tgt = sincos(joined_row[CTX:], joined_col[CTX:], D, order)
    pos_small = sincos(joined_row, joined_col, PW, p_order)
    patch = mm(patch, order).astype(LOW)
    seen_ctx = mm((ctx[:, None] == positions).astype(LOW), patch).astype(LOW)
    seen_tgt = mm((tgt[:, None] == positions).astype(LOW), patch).astype(LOW)
    order_own = lax.dynamic_slice_in_dim(order, side * half_d, half_d, 0)
    order_other = lax.dynamic_slice_in_dim(order, (1 - side) * half_d, half_d, 0)
    held_a = gather_near(lines, near_a, 1)
    far_b = gather_far(lines, packs[1])
    (
        held_a,
        far_b,
        pos_all,
        pos_ctx,
        pos_tgt,
        pos_small,
        patch,
        seen_ctx,
        seen_tgt,
        order_own,
        order_other,
        spread,
        order,
        p_order,
        eye,
        all_id,
        ctx_id,
        tgt_id,
        joined_id,
        used,
        packs[2],
    ) = fence(
        held_a,
        far_b,
        pos_all,
        pos_ctx,
        pos_tgt,
        pos_small,
        patch,
        seen_ctx,
        seen_tgt,
        order_own,
        order_other,
        spread,
        order,
        p_order,
        eye,
        all_id,
        ctx_id,
        tgt_id,
        joined_id,
        used,
        packs[2],
    )
    other_a = swap_all(held_a)
    near_b = gather_near(lines, far_b, 0)
    held_a, other_a, near_b, packs[2] = fence(held_a, other_a, near_b, packs[2])

    def widths(values, *sizes):
        found, at = [], 0
        for wide in sizes:
            found.append(values[:, at : at + wide])
            at += wide
        return found

    enc_qkv = (flat(held_a[0]), flat(other_a[0]))
    enc_rest = (flat(held_a[1]), flat(other_a[1]))
    held_b = gather_near(lines, near_b, 1)
    far_c = gather_far(lines, packs[2])
    start, normed_one, *projected, enc_gain, target_gain, pred_gain = ctx_first(
        seen_ctx,
        pos_ctx,
        spread,
        (order_own, order_other),
        enc_rest,
        enc_qkv,
    )
    held_b, far_c, start, projected, packs[3] = fence(
        held_b, far_c, start, projected, packs[3]
    )
    other_b = swap_all(held_b)
    near_c = gather_near(lines, far_c, 0)
    middle, normed_two, *pairs = ctx_second(
        size, start, enc_gain, ctx_id, enc_rest, projected
    )
    mixed, logs = pairs[:2], pairs[2:]
    held_b, other_b, near_c, normed_two, middle, packs[3] = fence(
        held_b, other_b, near_c, normed_two, middle, packs[3]
    )
    held_c = gather_near(lines, near_c, 1)
    far_d = gather_far(lines, packs[3])
    t_middle, t_two = target_forward(
        size,
        patch,
        seen_tgt,
        pos_all,
        pos_tgt,
        target_gain,
        tgt_id,
        all_id,
        (order_own, order_other),
        (flat(held_b[0]), flat(other_b[0])),
    )
    held_c, far_d, t_middle, t_two = fence(held_c, far_d, t_middle, t_two)
    other_c = swap_all(held_c)
    near_d = gather_near(lines, far_d, 0)
    bridge_in, bridge_out, pairs = pred_parts(
        dp_count, side.astype(jnp.int32), flat(held_b[1]), flat(other_b[1]), p_order
    )
    pred_down, pred_up, pred_qk, pred_right = pairs
    held_c, other_c, near_d, bridge_in, bridge_out, pred_down, pred_up, pred_qk, pred_right = fence(
        held_c, other_c, near_d, bridge_in, bridge_out, pred_down, pred_up, pred_qk, pred_right
    )
    held_d = gather_near(lines, near_d, 1)
    enc_up, enc_down = [(flat(own), flat(other)) for own, other in zip(held_c, other_c)]
    hidden, context, *pairs = ff_forward(
        normed_two, middle, enc_gain, enc_up, enc_down
    )
    activated, slope = pairs[:2], pairs[2:]
    (
        joined,
        p_normed_one,
        p_middle,
        p_normed_two,
        predicted,
        final,
        guess,
        *pairs,
    ) = pred_forward(
        p_size,
        context,
        bridge_in,
        bridge_out,
        pos_small,
        pred_gain,
        tgt_id,
        joined_id,
        pred_down,
        pred_up,
        pred_qk,
        pred_right,
    )
    p_qk, p_values, p_mixed, p_activated, p_slope = [
        pairs[at : at + 2] for at in range(0, 10, 2)
    ]
    p_logs = pairs[10]
    held_d, guess, t_middle = fence(held_d, guess, t_middle)
    other_d = swap_all(held_d)
    target = target_ff(False, t_two, t_middle, target_gain, *[flat(part) for part in held_d])
    target, other_d = fence(target, other_d)
    target = target_ff(True, t_two, target, target_gain, *[flat(part) for part in other_d])
    (
        loss_local,
        d_inward,
        sums_pred,
        *pair_p,
    ) = pred_back_all(
        p_size,
        count,
        dp_count,
        side[None].astype(jnp.int32),
        p_order,
        used[None],
        [
            guess,
            target,
            context,
            final,
            bridge_in,
            bridge_out,
            pred_gain,
            predicted,
            p_middle,
            joined,
            p_normed_one,
            p_normed_two,
        ],
        [
            pred_down,
            pred_up,
            pred_qk,
            pred_right,
            p_activated,
            p_slope,
            p_qk,
            p_values,
            p_mixed,
        ],
        p_logs,
        tgt_id,
        joined_id,
    )
    sum_p = Sums(lines, *pair_p, 4 * local, p_rows)
    (d_inward,) = fence_sums([sum_p], d_inward)
    sum_p.swap()
    (d_inward,) = fence_sums([sum_p], d_inward)
    d_inward = move((sum_p, 0), hold=d_inward)
    grads_other, *parts, sums_ff = ff_back_first(
        d_inward,
        bridge_in,
        hidden,
        normed_two,
        eye,
        enc_gain,
        activated[1],
        slope[1],
        enc_down[1],
    )
    grads_other, parts = fence_sums([sum_p], grads_other, parts)
    grads_got = swap(grads_other)
    parts = move((sum_p, 1), hold=parts)
    grads_own, branch, d_middle, sums_ff = ff_back_second(
        *parts,
        middle,
        enc_gain,
        activated[0],
        slope[0],
        enc_down[0],
        enc_up[0],
        enc_up[1],
        sums_ff,
    )
    sum_f = Sums(lines, grads_own, grads_other, ff, rows)
    sum_f.swap(grads_got)
    branch, d_middle = fence_sums([sum_p, sum_f], branch, d_middle)
    d_middle, branch = move((sum_f, 0), (sum_p, 2), hold=(d_middle, branch))
    d_proj = attn_back(size, branch, ctx_id, enc_rest, projected, mixed, logs)
    (d_proj,) = fence_sums([sum_p, sum_f], d_proj)
    d_proj = move((sum_f, 1), hold=d_proj)
    grads_own, grads_other = qkv_back(
        branch,
        d_middle,
        start,
        normed_one,
        seen_ctx,
        eye,
        enc_gain,
        sums_ff,
        sums_pred,
        spread,
        [d_proj, mixed, enc_qkv, (order_own, order_other)],
    )
    sum_a = Sums(lines, grads_own, grads_other, 3 * local, rows)
    fence_sums([sum_f, sum_a])
    sum_a.swap()
    fence_sums([sum_f, sum_a])
    move((sum_f, 2), (sum_a, 0))
    fence_sums([sum_f, sum_a])
    move((sum_a, 1))
    fence_sums([sum_a])
    move((sum_a, 2))

    red_left, red_right, squares_p = sum_p.results()
    red_up, red_down, squares_f = sum_f.results()
    red_qkv, red_rest, squares_a = sum_a.results((2 * local + LANES, 2 * local))
    low_one = p_ff + 2 * p_local
    bridge_other = swap(jnp.concatenate([red_left[:, low_one:], red_right[:, low_one:]], 0))
    embed_other = swap(red_rest[:, :local])
    gains_t = red_rest[:, 2 * local :].T
    sums = jnp.concatenate(
        [squares_p + squares_f + squares_a, jnp.pad(loss_local, ((0, 0), (0, LANES - 1)))], 0
    )
    for step in range(0, dp_count.bit_length(), 2):
        sums = lines.add_all(sums, step, min(step + 2, dp_count.bit_length()))
    groups = [
        (embed, embed_m, embed_v),
        (bridge, bridge_m, bridge_v),
        (enc_in, enc_in_m, enc_in_v),
        (enc_out.T, enc_out_m.T, enc_out_v.T),
        (enc_gains, enc_gains_m, enc_gains_v),
        (pred_in, pred_in_m, pred_in_v),
        (pred_out.T, pred_out_m.T, pred_out_v.T),
        (pred_gains, pred_gains_m, pred_gains_v),
    ]
    grads = [
        red_left,
        red_right,
        red_up,
        red_down,
        red_qkv,
        red_rest,
        bridge_other,
        embed_other,
        gains_t,
    ]
    every, part = (0, rows), (0, p_rows)
    lower = (p_rows, 2 * p_rows)
    qk_end, v_end = p_ff + 2 * p_local, p_ff + p_local
    learn, gain = (LEARN_RATE, WEIGHT_DECAY), (GAIN_RATE, 0.0)
    plan = (
        (
            *learn,
            (
                (5, every, (0, local), every, (True, half_d)),
                (7, every, (0, local), every, (False, half_d)),
            ),
        ),
        (
            *learn,
            (
                (0, part, (qk_end, qk_end + half_d), part, (True, half_d)),
                (1, part, (qk_end, qk_end + half_d), lower, (True, half_d)),
                (6, every, (0, half_d), every, (False, half_d)),
            ),
        ),
        (
            *learn,
            (
                (4, every, (0, 3 * local), every, (0, 3 * local)),
                (2, every, (0, ff), every, (3 * local, 3 * local + ff)),
            ),
        ),
        (
            *learn,
            (
                (5, every, (local, 2 * local), every, (0, local)),
                (3, every, (0, ff), every, (local, local + ff)),
            ),
        ),
        (*gain, ((8, (0, 6), every, (0, 6), every),)),
        (
            *learn,
            (
                (0, part, (p_ff, qk_end), part, (0, 2 * p_local)),
                (1, part, (p_ff, v_end), part, (2 * p_local, 3 * p_local)),
                (1, part, (0, p_ff), part, (3 * p_local, 3 * p_local + p_ff)),
            ),
        ),
        (
            *learn,
            (
                (1, part, (v_end, qk_end), part, (0, p_local)),
                (0, part, (0, p_ff), part, (p_local, p_local + p_ff)),
            ),
        ),
        (*gain, ((8, (8, 15), part, (0, 7), part),)),
    )
    results = adam_all(sums, side[None].astype(jnp.int32), groups, grads, plan)
    for at in (3, 6):
        results[at] = [value.T for value in results[at]]
    return (*[value for result in results for value in result], sums[1, 0], jnp.sqrt(jnp.sum(sums[0])))


def solution(mesh):
    in_specs = (
        P("dp", None, None),
        P("dp", None),
        P("dp", None),
        P("dp"),
        P("dp"),
        P("dp", None),
        P("dp", None),
        P("dp", None),
        P("dp", None),
        P("dp", None),
        P("dp", None),
        P("dp", "mp"),
        P("dp", "mp"),
        P("dp", "mp"),
        P("mp", "dp"),
        P("mp", "dp"),
        P("mp", "dp"),
        P(None, "dp"),
        P(None, "dp"),
        P(None, "dp"),
        P("dp", "mp"),
        P("dp", "mp"),
        P("dp", "mp"),
        P("mp", "dp"),
        P("mp", "dp"),
        P("mp", "dp"),
        P(None, "dp"),
        P(None, "dp"),
        P(None, "dp"),
        P("dp", None),
        P("dp", "mp"),
        P("mp", "dp"),
        P(None, "dp"),
    )
    out_specs = (
        P("dp", None),
        P("dp", None),
        P("dp", None),
        P("dp", None),
        P("dp", None),
        P("dp", None),
        P("dp", "mp"),
        P("dp", "mp"),
        P("dp", "mp"),
        P("mp", "dp"),
        P("mp", "dp"),
        P("mp", "dp"),
        P(None, "dp"),
        P(None, "dp"),
        P(None, "dp"),
        P("dp", "mp"),
        P("dp", "mp"),
        P("dp", "mp"),
        P("mp", "dp"),
        P("mp", "dp"),
        P("mp", "dp"),
        P(None, "dp"),
        P(None, "dp"),
        P(None, "dp"),
        P(),
        P(),
    )
    return jax.shard_map(shards, mesh=mesh, in_specs=in_specs, out_specs=out_specs, check_vma=False)
```

```python
import functools
import itertools

import jax
import jax.numpy as jnp
from jax import lax
from jax.experimental import pallas as pl
from jax.experimental.pallas import tpu as pltpu
from jax.sharding import PartitionSpec as P

D = 768
HEADS = 12
PW = 384
PHEADS = 12
SIDE = 14
SMALLP = 196
CTX = 512
TGT = 256
STEP = 10


LOW = jnp.bfloat16
WIDE = jnp.float32
CLIP_NORM = 0.0005
LEARN_RATE = 0.05
GAIN_RATE = 1.0
BETA_ONE = 0.9
BETA_TWO = 0.999
EPSILON = 1e-08
WEIGHT_DECAY = 0.05


LANES = 128


def norm_rows(values, gain_row, shift_row):
    centred = values - jnp.mean(values, -1, keepdims=True)
    spread = jnp.mean(centred * centred, -1, keepdims=True)
    return centred * lax.rsqrt(spread + 1e-06) * gain_row + shift_row


def norm_back(values, gain_row, grad):
    centred = values - jnp.mean(values, -1, keepdims=True)
    rstd = lax.rsqrt(jnp.mean(centred * centred, -1, keepdims=True) + 1e-06)
    unit = centred * rstd
    scaled = grad * gain_row
    d_values = rstd * (
        scaled
        - jnp.mean(scaled, -1, keepdims=True)
        - unit * jnp.mean(scaled * unit, -1, keepdims=True)
    )
    return d_values, jnp.sum(grad * unit, 0), jnp.sum(grad, 0)


def gelu_parts(pre):
    bell = jnp.exp(-0.5 * pre * pre)
    turn = 1.0 / (1.0 + 0.3275911 * 0.7071067811865476 * jnp.abs(pre))
    series = 0.5 * 1.061405429
    for factor in (-1.453152027, 1.421413741, -0.284496736, 0.254829592):
        series = series * turn + 0.5 * factor
    tail = series * turn * bell
    return jnp.where(pre < 0.0, tail, 1.0 - tail), bell * 0.3989422804014327


def gelu_both(pre):
    phi, density = gelu_parts(pre)
    return (pre * phi).astype(LOW), (phi + pre * density).astype(LOW)


def place(single, positions):
    image_id = jnp.where(single, 0, positions // SMALLP)
    within = jnp.where(single, positions, positions % SMALLP)
    side_len = jnp.where(single, 2 * SIDE, SIDE)
    return (image_id, within // side_len, within % side_len)


def three_parts(values):
    high = lax.reduce_precision(values, 8, 7)
    rest = values - high
    middle = lax.reduce_precision(rest, 8, 7)
    return jnp.concatenate([high, middle, rest - middle], 0).astype(LOW)


def sincos(row_pos, col_pos, width, order):
    quarter = width // 4
    omega = 10000.0 ** (-jnp.arange(quarter).astype(WIDE) / quarter)
    steps = jnp.arange(2 * SIDE)
    angle = steps.astype(WIDE)[:, None] * omega
    table = jnp.concatenate([jnp.sin(angle), jnp.cos(angle)], -1)
    blank = jnp.zeros_like(table)
    table = jnp.concatenate(
        [jnp.concatenate([table, blank], 1), jnp.concatenate([blank, table], 1)], 0
    )
    parts = three_parts(table)
    if order is not None:
        parts = mm(parts, order).astype(LOW)
    pick = jnp.concatenate([row_pos[:, None] == steps, col_pos[:, None] == steps], 1)
    pick = pick.astype(LOW)
    return mm(jnp.concatenate([pick, pick, pick], 1), parts)


def mm(left, right):
    return jnp.dot(left, right, preferred_element_type=WIDE)


def mm_t(left, right):
    return lax.dot_general(left, right, (((1,), (1,)), ((), ())), preferred_element_type=WIDE)


def t_mm(left, right):
    return lax.dot_general(left, right, (((0,), (0,)), ((), ())), preferred_element_type=WIDE)


SPAN = 64


def head_forward(query, keys, values, bias_ref, size):
    scale = size**-0.5
    scores = mm_t(keys, query) + bias_ref[...]
    highest = jnp.max(scores, 0, keepdims=True)
    soft = jnp.exp((scores - highest) * scale)
    total = jnp.sum(soft, 0, keepdims=True)
    return (t_mm(values, soft.astype(LOW)) / total).T, highest * scale + jnp.log(total)


def head_backward(query, keys, values, d_out, mixed, logs, bias_ref, soft_ref, ds_ref, size):
    scale = size**-0.5
    count = keys.shape[0]
    row_sum = jnp.sum((d_out.astype(WIDE) * mixed.astype(WIDE)).T, 0, keepdims=True)
    for low in range(0, count, SPAN):
        high = low + SPAN
        scores = mm_t(keys[low:high], query) + bias_ref[low:high, :]
        soft = jnp.exp(scores * scale - logs)
        d_soft = mm_t(values[low:high], d_out)
        soft_ref[low:high, :] = soft.astype(LOW)
        ds_ref[low:high, :] = (soft * (d_soft - row_sum)).astype(LOW)
    d_values = mm(soft_ref[...], d_out)
    d_keys = mm(ds_ref[...], query) * scale
    d_query = (t_mm(keys, ds_ref[...]) * scale).T
    return d_query.astype(LOW), d_keys.astype(LOW), d_values.astype(LOW)


WHOLE = pl.BlockSpec(memory_space=pltpu.VMEM)
CHUNK = 64
MARGIN = 6 * 2**20


def room(values, margin=MARGIN):
    total = 0
    for value in values:
        rows, cols = value.shape[-2], value.shape[-1]
        cells = value.size // (rows * cols) * (-(-rows // 16) * 16) * (-(-cols // LANES) * LANES)
        total += cells * jnp.dtype(value.dtype).itemsize
    return min(total + margin, 58 * 2**20)


def streamed(kernel, counts, late, early, *refs):
    n_in, n_out, n_scratch = counts
    ins, outs = list(refs[:n_in]), list(refs[n_in : n_in + n_out])
    scratch = refs[n_in + n_out : n_in + n_out + n_scratch]
    extra = refs[n_in + n_out + n_scratch :]
    arriving, leaving, left = {}, {}, []
    for at, which in enumerate(late):
        arriving[which] = pltpu.make_async_copy(ins[which], extra[at], extra[-1].at[at])
        arriving[which].start()
        ins[which] = extra[at]
    for at, which in enumerate(early, len(late)):
        leaving[which] = pltpu.make_async_copy(extra[at], outs[which], extra[-1].at[at])
        outs[which] = extra[at]

    def need(*those):
        for which in those:
            arriving.pop(which).wait()

    def ship(*those):
        for which in those:
            copy = leaving.pop(which)
            copy.start()
            left.append(copy)

    kernel(need, ship, *ins, *outs, *scratch)
    need(*list(arriving))
    ship(*list(leaving))
    for copy in left:
        copy.wait()


def on_chip(kernel, ins, outs, scratch, macs, exps=0, ahead=False, late=(), early=()):
    outs = [jax.ShapeDtypeStruct(shape, kind) for shape, kind in outs]
    held = [jax.ShapeDtypeStruct(shape, kind) for shape, kind in scratch]
    moved = sum(value.size * value.dtype.itemsize for value in list(ins) + outs)
    buffers = [pltpu.VMEM(shape, kind) for shape, kind in scratch]
    in_specs, out_specs = [WHOLE] * len(ins), [WHOLE] * len(outs)
    if late or early:
        counts = len(ins), len(outs), len(scratch)
        kernel = functools.partial(streamed, kernel, counts, late, early)
        for which in late:
            in_specs[which] = pl.BlockSpec(memory_space=pl.ANY)
            buffers.append(pltpu.VMEM(ins[which].shape, ins[which].dtype))
        for which in early:
            out_specs[which] = pl.BlockSpec(memory_space=pl.ANY)
            buffers.append(pltpu.VMEM(outs[which].shape, outs[which].dtype))
        buffers.append(pltpu.SemaphoreType.DMA((len(late) + len(early),)))
    return pl.pallas_call(
        kernel,
        in_specs=in_specs,
        out_specs=out_specs,
        out_shape=outs,
        scratch_shapes=buffers,
        cost_estimate=pl.CostEstimate(flops=2 * macs, bytes_accessed=moved, transcendentals=exps),
        compiler_params=pltpu.CompilerParams(
            vmem_limit_bytes=room(list(ins) + outs + held, 2 * MARGIN)
            if late or early
            else room(list(ins) + outs + held) if ahead else 58 * 2**20
        ),
    )(*ins)


def tiles(count, width, body):
    def step(at, carry):
        body(pl.ds(pl.multiple_of(at * width, width), width))
        return carry

    lax.fori_loop(0, count // width, step, 0)


def norm_back_rows(values_ref, grad_ref, gain, write, sums_ref, at):
    rows, width = values_ref.shape

    def step(number, carry):
        span = pl.ds(pl.multiple_of(number * CHUNK, CHUNK), CHUNK)
        values, grad = values_ref[span, :], grad_ref[span, :]
        centred = values - jnp.mean(values, -1, keepdims=True)
        rstd = lax.rsqrt(jnp.mean(centred * centred, -1, keepdims=True) + 1e-06)
        unit = centred * rstd
        scaled = grad * gain
        d_values = rstd * (
            scaled
            - jnp.mean(scaled, -1, keepdims=True)
            - unit * jnp.mean(scaled * unit, -1, keepdims=True)
        )
        write(span, d_values)
        return (
            carry[0] + jnp.sum(grad * unit, 0, keepdims=True),
            carry[1] + jnp.sum(grad, 0, keepdims=True),
        )

    blank = jnp.zeros((1, width), WIDE)
    gains, shifts = lax.fori_loop(0, rows // CHUNK, step, (blank, blank))
    sums_ref[at : at + 1, :] = gains
    sums_ref[at + 1 : at + 2, :] = shifts


def ff_side(branch, branch_t, normed_t, act, slope, down, d_pre, out):
    ff = act.shape[1]

    def body(span):
        d_act = mm(branch[...], down[:, span])
        values = (d_act * slope[:, span].astype(WIDE)).astype(LOW)
        d_pre[:, span] = values
        out[:, span] = mm(normed_t[...], values).astype(LOW)
        lower = pl.ds(pl.multiple_of(span.start + ff, LANES), span.size)
        out[:, lower] = mm(branch_t[...], act[:, span]).astype(LOW)

    tiles(ff, 768, body)


def ff_back_first_kernel(need, ship, *refs):
    d_inward, bridge_in, hidden, normed, eye, gains, act, slope, down = refs[0:9]
    out, d_hidden, branch, branch_t, normed_t, d_pre, sums, grad = refs[9:17]

    def first(span):
        grad[:, span] = mm_t(d_inward[...], bridge_in[span, :])

    tiles(D, 256, first)

    def write(span, values):
        d_hidden[span, :] = values
        branch[span, :] = values.astype(LOW)

    norm_back_rows(hidden, grad, gains[4:5, :], write, sums, 0)
    ship(1, 2)
    need(4, 3)
    branch_t[...] = mm_t(eye[...], branch[...]).astype(LOW)
    normed_t[...] = mm_t(eye[...], normed[...]).astype(LOW)
    ship(3, 4)
    need(8, 7, 6)
    ff_side(branch, branch_t, normed_t, act, slope, down, d_pre, out)


def ff_back_first(d_inward, bridge_in, hidden, normed, eye, gains, act, slope, down):
    rows, ff = act.shape
    return on_chip(
        ff_back_first_kernel,
        [d_inward, bridge_in, hidden, normed, eye, gains, act, slope, down],
        [((D, 2 * ff), LOW), ((rows, D), WIDE), ((rows, D), LOW)]
        + [((D, rows), LOW)] * 2
        + [((rows, ff), LOW), ((8, D), WIDE)],
        [((rows, D), WIDE)],
        4 * rows * D * ff,
        late=(4, 3, 8, 7, 6),
        early=(1, 2, 3, 4, 0, 5),
    )


def ff_back_second_kernel(need, ship, *refs):
    d_hidden, branch, branch_t, normed_t, d_pre_other, middle, gains = refs[0:7]
    act, slope, down, up_own, up_other, sums_first = refs[7:13]
    out, branch_out, d_middle, sums, grad, d_pre = refs[13:19]
    need(9, 8, 7)
    ff_side(branch, branch_t, normed_t, act, slope, down, d_pre, out)
    ship(0)
    need(10, 4, 11)

    def third(span):
        grad[:, span] = mm_t(d_pre[...], up_own[span, :]) + mm_t(d_pre_other[...], up_other[span, :])

    tiles(D, 768, third)
    need(5, 0)

    def write(span, values):
        values = values + d_hidden[span, :]
        d_middle[span, :] = values
        branch_out[span, :] = values.astype(LOW)

    norm_back_rows(middle, grad, gains[2:3, :], write, sums, 2)
    sums[0:2, :] = sums_first[0:2, :]


def ff_back_second(
    d_hidden,
    branch,
    branch_t,
    normed_t,
    d_pre,
    middle,
    gains,
    act,
    slope,
    down,
    up_own,
    up_other,
    sums,
):
    rows, ff = act.shape
    return on_chip(
        ff_back_second_kernel,
        [d_hidden, branch, branch_t, normed_t, d_pre, middle, gains, act, slope, down]
        + [up_own, up_other, sums],
        [((D, 2 * ff), LOW), ((rows, D), LOW), ((rows, D), WIDE), ((8, D), WIDE)],
        [((rows, D), WIDE), ((rows, ff), LOW)],
        5 * rows * D * ff,
        late=(9, 8, 7, 10, 4, 11, 5, 0),
        early=(0,),
    )


def attn_back_kernel(size, branch, ids_row, ids_col, *refs):
    rests, projs, mixeds, logs, d_projs = refs[0:2], refs[2:4], refs[4:6], refs[6:8], refs[8:10]
    d_mixed, bias, soft, d_scores = refs[10:14]
    width = D // 2
    bias[...] = jnp.where(ids_col[...] == ids_row[...], 0.0, -1e30)
    for side in (0, 1):
        proj, mixed, log, d_proj = projs[side], mixeds[side], logs[side], d_projs[side]
        d_mixed[...] = mm(branch[...], rests[side][:, width : 2 * width]).astype(LOW)

        def step(block, carry, proj=proj, mixed=mixed, log=log, d_proj=d_proj):
            at = [pl.multiple_of(part * width + block * LANES, LANES) for part in range(3)]
            query, keys, values = [proj[:, pl.ds(col, LANES)] for col in at]
            d_out = d_mixed[:, pl.ds(at[0], LANES)]
            out = mixed[:, pl.ds(at[0], LANES)]
            found = []
            for number, low in enumerate(range(0, LANES, size)):
                cols = slice(low, low + size)
                found.append(
                    head_backward(
                        query[:, cols],
                        keys[:, cols],
                        values[:, cols],
                        d_out[:, cols],
                        out[:, cols],
                        log[number, pl.ds(block, 1), :],
                        bias,
                        soft,
                        d_scores,
                        size,
                    )
                )
            for col, parts in zip(at, zip(*found)):
                d_proj[:, pl.ds(col, LANES)] = jnp.concatenate(parts, -1)
            return carry

        lax.fori_loop(0, width // LANES, step, 0)


def attn_back(size, branch, ids, rests, projs, mixeds, logs):
    rows = branch.shape[0]
    return on_chip(
        functools.partial(attn_back_kernel, size),
        [branch, ids[None, :], ids[:, None], *rests, *projs, *mixeds, *logs],
        [(projs[0].shape, LOW)] * 2,
        [
            ((rows, D // 2), LOW),
            ((rows, rows), WIDE),
            ((rows, rows), LOW),
            ((rows, rows), LOW),
        ],
        rows * D * D + rows * rows * D * 5,
        rows * rows * D // size,
        ahead=True,
    )


def qkv_back_kernel(need, ship, *refs):
    branch, d_middle, start, normed, seen, eye, gains, sums_ff, sums_p, spread = refs[0:10]
    d_projs, mixeds, qkvs, orders = refs[10:12], refs[12:14], refs[14:16], refs[16:18]
    outs = refs[18:20]
    grad, flipped, d_start, sums = refs[20:24]
    width = D // 2
    rest = 3 * width
    flipped[...] = mm_t(eye[...], branch[...]).astype(LOW)
    need(12, 13)
    for side in (0, 1):
        outs[side][:, rest + width : rest + 2 * width] = mm(
            flipped[...], mixeds[side][...]
        ).astype(LOW)
    need(3)
    flipped[...] = mm_t(eye[...], normed[...]).astype(LOW)
    need(10, 11)
    for side in (0, 1):
        outs[side][:, 0:rest] = mm(flipped[...], d_projs[side][...]).astype(LOW)
    need(14, 15)
    grad[...] = mm_t(d_projs[0][...], qkvs[0][...]) + mm_t(d_projs[1][...], qkvs[1][...])

    def write(span, values):
        d_start[span, :] = (values + d_middle[span, :]).astype(LOW)

    need(1, 2)
    norm_back_rows(start, grad, gains[0:1, :], write, sums, 0)
    need(4)
    flipped[...] = mm_t(eye[...], seen[...]).astype(LOW)
    sums[2:4, :] = sums_ff[2:4, :]
    sums[4:6, :] = sums_ff[0:2, :]
    sums[6:8, :] = jnp.zeros((2, D), WIDE)
    rows = jnp.concatenate(
        [sums[...].astype(LOW), mm(sums_p[...].astype(LOW), spread[...]).astype(LOW)], 0
    )
    cols = t_mm(rows, eye[0:16, 0:LANES]).astype(LOW)
    need(16, 17)
    for side in (0, 1):
        moved = mm_t(d_start[...], orders[side][...]).astype(LOW)
        outs[side][:, rest : rest + width] = mm(flipped[...], moved).astype(LOW)
        outs[side][:, rest + 2 * width :] = cols


def qkv_back(branch, d_middle, start, normed, seen, eye, gains, sums_ff, sums_p, spread, pairs):
    rows, width = branch.shape[0], D // 2
    return on_chip(
        qkv_back_kernel,
        [branch, d_middle, start, normed, seen, eye, gains, sums_ff, sums_p, spread]
        + [value for pair in pairs for value in pair],
        [((D, 5 * width + LANES), LOW)] * 2,
        [((rows, D), WIDE), ((D, rows), LOW), ((rows, D), LOW), ((8, D), WIDE)],
        rows * D * D * 10,
        late=(12, 13, 3, 10, 11, 14, 15, 1, 2, 4, 16, 17),
    )


def row_spans(rows, chunk, body):
    def step(number, carry):
        body(pl.ds(pl.multiple_of(number * chunk, chunk), chunk))
        return carry

    lax.fori_loop(0, rows // chunk, step, 0)


def heads_forward(query_ref, keys_ref, values_ref, out_ref, logs_ref, bias, size, at):
    width = out_ref.shape[1]

    def step(block, carry):
        cols = [pl.multiple_of(first + block * LANES, LANES) for first in at]
        query = query_ref[:, pl.ds(cols[0], LANES)]
        keys = keys_ref[:, pl.ds(cols[1], LANES)]
        values = values_ref[:, pl.ds(cols[2], LANES)]
        found = []
        for number, low in enumerate(range(0, LANES, size)):
            part = slice(low, low + size)
            out, logs = head_forward(
                query[:, part], keys[:, part], values[:, part], bias, size
            )
            found.append(out)
            if logs_ref is not None:
                logs_ref[number, pl.ds(block, 1), :] = logs
        place_at = pl.ds(pl.multiple_of(block * LANES, LANES), LANES)
        out_ref[:, place_at] = jnp.concatenate(found, -1).astype(LOW)
        return carry

    lax.fori_loop(0, width // LANES, step, 0)


def ctx_first_kernel(need, ship, seen, pos, spread, *refs):
    orders, rests, qkvs = refs[0:2], refs[2:4], refs[4:6]
    start, normed, projs, outs, embed_w = refs[6], refs[7], refs[8:10], refs[10:13], refs[13]
    gains = outs[0]
    width = orders[0].shape[0]
    parts = rests[0][:, 2 * width :].astype(WIDE).T
    outs[0][...] = parts[0:8] + parts[8:16]
    outs[1][...] = parts[16:24] + parts[24:32]
    low = parts[32:48].astype(LOW)
    low = mm_t(low, spread[...])
    outs[2][...] = low[0:8] + low[8:16]
    embed_w[...] = (
        mm(rests[0][:, 0:width], orders[0][...]) + mm(rests[1][:, 0:width], orders[1][...])
    ).astype(LOW)
    need(0, 1)
    start[...] = mm(seen[...], embed_w[...]) + pos[...]
    ship(0)

    def first_norm(span):
        normed[span, :] = norm_rows(start[span, :], gains[0:1, :], gains[1:2, :]).astype(LOW)

    row_spans(seen.shape[0], CHUNK, first_norm)
    ship(1)
    for side in (0, 1):
        need(7 + side)
        projs[side][...] = mm(normed[...], qkvs[side][...]).astype(LOW)
        ship(2 + side)


def ctx_first(seen, pos, spread, orders, rests, qkvs):
    rows, width = seen.shape[0], orders[0].shape[0]
    return on_chip(
        ctx_first_kernel,
        [seen, pos, spread, *orders, *rests, *qkvs],
        [((rows, D), WIDE), ((rows, D), LOW)]
        + [((rows, 3 * width), LOW)] * 2
        + [((8, D), WIDE), ((8, D), WIDE), ((8, PW), WIDE)],
        [((D, D), LOW)],
        rows * D * D * 4 + D * D * D,
        late=(0, 1, 7, 8),
        early=(0, 1, 2, 3),
    )


def ctx_second_kernel(size, need, ship, start, gains, ids_row, ids_col, *refs):
    rests, projs = refs[0:2], refs[2:4]
    middle, normed_two, mixeds, logs, bias = refs[4], refs[5], refs[6:8], refs[8:10], refs[10]
    width = mixeds[0].shape[1]
    bias[...] = jnp.where(ids_col[...] == ids_row[...], 0.0, -1e30)
    for side in (0, 1):
        need(6 + side)
        proj = projs[side]
        heads_forward(
            proj, proj, proj, mixeds[side], logs[side], bias, size, (0, width, 2 * width)
        )
        ship(2 + side)
    need(4, 5, 0)
    middle[...] = (
        start[...]
        + mm_t(mixeds[0][...], rests[0][:, width : 2 * width])
        + mm_t(mixeds[1][...], rests[1][:, width : 2 * width])
    )

    def second_norm(span):
        normed_two[span, :] = norm_rows(middle[span, :], gains[2:3, :], gains[3:4, :]).astype(LOW)

    row_spans(start.shape[0], CHUNK, second_norm)


def ctx_second(size, start, gains, ids, rests, projs):
    rows, width = start.shape[0], D // 2
    return on_chip(
        functools.partial(ctx_second_kernel, size),
        [start, gains, ids[None, :], ids[:, None], *rests, *projs],
        [((rows, D), WIDE), ((rows, D), LOW)]
        + [((rows, width), LOW)] * 2
        + [((LANES // size, 8, rows), WIDE)] * 2,
        [((rows, rows), WIDE)],
        rows * D * D + rows * rows * D * 2,
        rows * rows * D // size,
        late=(6, 7, 4, 5, 0),
        early=(2, 3),
    )


def gelu_rows(pre_ref, act_ref, slope_ref, span):
    def body(rows):
        act, slope = gelu_both(pre_ref[rows, :])
        act_ref[rows, span] = act
        if slope_ref is not None:
            slope_ref[rows, span] = slope

    row_spans(pre_ref.shape[0], 32, body)


def ff_kernel(need, ship, *refs):
    normed, middle, gains, ups, downs = *refs[0:3], refs[3:5], refs[5:7]
    hidden, context, acts, slopes, pre = refs[7], refs[8], refs[9:11], refs[11:13], refs[13]
    rows, ff = acts[0].shape
    for side in (0, 1):
        need(3 + side)

        def first(span, side=side):
            pre[...] = mm(normed[...], ups[side][:, span])
            gelu_rows(pre, acts[side], slopes[side], span)

        tiles(ff, 512, first)
        ship(2 + side, 4 + side)
    need(5, 6, 1)
    hidden[...] = (
        middle[...] + mm_t(acts[0][...], downs[0][...]) + mm_t(acts[1][...], downs[1][...])
    )

    def last(span):
        context[span, :] = norm_rows(hidden[span, :], gains[4:5, :], gains[5:6, :]).astype(LOW)

    row_spans(rows, CHUNK, last)


def ff_forward(normed, middle, gains, ups, downs):
    rows, ff = normed.shape[0], ups[0].shape[1]
    return on_chip(
        ff_kernel,
        [normed, middle, gains, *ups, *downs],
        [((rows, D), WIDE), ((rows, D), LOW)] + [((rows, ff), LOW)] * 4,
        [((rows, 512), WIDE)],
        rows * D * ff * 4 + rows * D * D,
        rows * ff * 2,
        late=(3, 4, 5, 6, 1),
        early=(2, 3, 4, 5),
    )


def target_kernel(size, *refs):
    patch, seen, pos_all, pos_tgt, gains, ids_row, ids_col = refs[0:7]
    orders, weights, (t_middle, t_two) = refs[7:9], refs[9:11], refs[11:13]
    embed_w, hidden, normed, start, query, keys, mixed, bias = refs[13:]
    width = D // 2
    own, other = [part[:, 3 * width : 4 * width] for part in weights]
    embed_w[...] = (mm(own, orders[0][...]) + mm(other, orders[1][...])).astype(LOW)
    hidden[...] = mm(patch[...], embed_w[...]) + pos_all[...]

    def first_norm(span):
        normed[span, :] = norm_rows(hidden[span, :], gains[0:1, :], gains[1:2, :]).astype(LOW)

    row_spans(patch.shape[0], 112, first_norm)
    start[...] = mm(seen[...], embed_w[...]) + pos_tgt[...]
    t_normed = norm_rows(start[...], gains[0:1, :], gains[1:2, :]).astype(LOW)
    bias[...] = jnp.where(ids_col[...] == ids_row[...], 0.0, -1e30)
    total = start[...]
    for part in weights:
        query[...] = mm(t_normed, part[:, 0:width]).astype(LOW)
        keys[...] = mm(normed[...], part[:, width : 3 * width]).astype(LOW)
        heads_forward(query, keys, keys, mixed, None, bias, size, (0, 0, width))
        total = total + mm_t(mixed[...], part[:, 4 * width : 5 * width])
    t_middle[...] = total
    t_two[...] = norm_rows(total, gains[2:3, :], gains[3:4, :]).astype(LOW)


def target_forward(
    size, patch, seen, pos_all, pos_tgt, gains, idq, idk, orders, weights
):
    rows, count, width = seen.shape[0], patch.shape[0], D // 2
    return on_chip(
        functools.partial(target_kernel, size),
        [patch, seen, pos_all, pos_tgt, gains, idq[None, :], idk[:, None], *orders, *weights],
        [((rows, D), WIDE), ((rows, D), LOW)],
        [
            ((D, D), LOW),
            ((count, D), WIDE),
            ((count, D), LOW),
            ((rows, D), WIDE),
            ((rows, width), LOW),
            ((count, 2 * width), LOW),
            ((rows, width), LOW),
            ((count, rows), WIDE),
        ],
        count * D * D * 3 + rows * D * D * 3 + 2 * rows * count * D,
        rows * count * D // size,
        ahead=True,
    )


def pred_forward_kernel(size, *refs):
    context, bridge_in, bridge_out, pos, gains, ids_row, ids_col = refs[0:7]
    downs, ups, qks, rights = refs[7:9], refs[9:11], refs[11:13], refs[13:15]
    joined, normed, middle, normed_two, predicted, final, guess = refs[15:22]
    out_qk, out_v, mixeds, acts, slopes = (
        refs[22:24],
        refs[24:26],
        refs[26:28],
        refs[28:30],
        refs[30:32],
    )
    logs, bias = refs[32], refs[33]
    width = out_v[0].shape[1]
    joined[0:CTX, :] = mm(context[...], bridge_in[...]) + pos[0:CTX, :]
    joined[CTX:, :] = gains[6:7, :] + pos[CTX:, :]

    def first(span):
        normed[span, :] = norm_rows(joined[span, :], gains[0:1, :], gains[1:2, :]).astype(LOW)

    row_spans(joined.shape[0], 128, first)
    bias[...] = jnp.where(ids_col[...] == ids_row[...], 0.0, -1e30)
    total = joined[CTX:, :]
    head = 0
    for qk, right, qk_ref, v_ref, mixed in zip(qks, rights, out_qk, out_v, mixeds):
        qk_ref[...] = mm(normed[...], qk[...]).astype(LOW)
        v_ref[...] = mm(normed[...], right[:, 0:width]).astype(LOW)
        found = []
        for low in range(0, width, size):
            out, log = head_forward(
                qk_ref[CTX:, low : low + size],
                qk_ref[:, width + low : width + low + size],
                v_ref[:, low : low + size],
                bias,
                size,
            )
            found.append(out)
            logs[head : head + 1, :] = log
            head += 1
        mixed[...] = jnp.concatenate(found, -1).astype(LOW)
        total = total + mm_t(mixed[...], right[:, width:])
    middle[...] = total
    normed_two[...] = norm_rows(total, gains[2:3, :], gains[3:4, :]).astype(LOW)
    total = middle[...]
    for up, down, act, slope in zip(ups, downs, acts, slopes):
        values, tilt = gelu_both(mm(normed_two[...], up[...]))
        act[...] = values
        slope[...] = tilt
        total = total + mm_t(act[...], down[...])
    predicted[...] = total
    final[...] = norm_rows(total, gains[4:5, :], gains[5:6, :]).astype(LOW)
    guess[...] = mm_t(final[...], bridge_out[...])


def pred_forward(
    size, context, bridge_in, bridge_out, pos, gains, idq, idk, downs, ups, qks, rights
):
    rows, count, width, ff = idq.shape[0], idk.shape[0], qks[0].shape[1] // 2, ups[0].shape[1]
    low, wide = LOW, WIDE
    return on_chip(
        functools.partial(pred_forward_kernel, size),
        [context, bridge_in, bridge_out, pos, gains, idq[None, :], idk[:, None]]
        + [*downs, *ups, *qks, *rights],
        [((count, PW), wide), ((count, PW), low), ((rows, PW), wide), ((rows, PW), low)]
        + [((rows, PW), wide), ((rows, PW), low), ((rows, D), wide)]
        + [((count, 2 * width), low)] * 2
        + [((count, width), low)] * 2
        + [((rows, width), low)] * 2
        + [((rows, ff), low)] * 4
        + [((16, rows), wide)],
        [((count, rows), wide)],
        1_000_000_000,
        rows * count * PW // size,
    )


def target_ff_kernel(last, need, ship, t_two, start, gains, up, down, target, pre, act):
    need(3)

    def first(span):
        pre[...] = mm(t_two[...], up[:, span])
        gelu_rows(pre, act, None, span)

    tiles(act.shape[1], 512, first)
    need(4)
    total = start[...] + mm_t(act[...], down[...])
    if last:
        total = norm_rows(total, gains[4:5, :], gains[5:6, :])
        total = norm_rows(total, 1.0, 0.0)
    target[...] = total


def target_ff(last, t_two, start, gains, up, down):
    rows, ff = t_two.shape[0], up.shape[1]
    return on_chip(
        functools.partial(target_ff_kernel, last),
        [t_two, start, gains, up, down],
        [((rows, D), WIDE)],
        [((rows, 512), WIDE), ((rows, ff), LOW)],
        rows * D * ff * 2,
        rows * ff,
        late=(3, 4),
    )[0]


def pred_back_all_kernel(size, count_all, dp_count, *refs):
    (guess, target, used, context, final, bridge_in, bridge_out, gains, ids_row, ids_col) = refs[
        0:10
    ]
    predicted, middle, joined, normed, normed_two = refs[10:15]
    downs, ups, qks, rights = refs[15:17], refs[17:19], refs[19:21], refs[21:23]
    acts, slopes, in_qk, in_v, mixeds = (
        refs[23:25],
        refs[25:27],
        refs[27:29],
        refs[29:31],
        refs[31:33],
    )
    logs = refs[33]
    p_order, side_ref, loss, d_inward, sums = refs[34:39]
    packs = refs[39:41]
    d_qk, d_v, d_normed, bias, soft, d_scores, g_bridge_out = refs[41:48]
    p_rows = PW // dp_count
    half = packs[0].shape[2] // 2

    def put(side, column, values):
        for block in range(dp_count):
            part = values[block * p_rows : (block + 1) * p_rows]
            packs[side][block, :, column : column + values.shape[1]] = part.astype(LOW)

    width = in_v[0].shape[1]
    ff = acts[0].shape[1]
    diff = guess[...] - target[...]
    size_abs = jnp.abs(diff)
    keep = lax.broadcasted_iota(jnp.int32, diff.shape, 0) < used[0]
    terms = jnp.where(
        keep, jnp.where(size_abs < 1.0, 0.5 * diff * diff, size_abs - 0.5), 0.0
    )
    loss[...] = jnp.sum(jnp.sum(terms, 0, keepdims=True), 1, keepdims=True)
    d_guess = jnp.where(keep, jnp.clip(diff, -1.0, 1.0) / count_all, 0.0).astype(LOW)
    g_bridge_out[...] = t_mm(d_guess, final[...]).astype(LOW)

    def back(values, gain, grad, at):
        d_values, gain_sum, shift_sum = norm_back(values, gain, grad)
        sums[at : at + 1, :] = gain_sum[None, :]
        sums[at + 1 : at + 2, :] = shift_sum[None, :]
        return d_values

    d_tail = back(predicted[...], gains[4:5, :], mm(d_guess, bridge_out[...]), 4)
    branch = d_tail.astype(LOW)
    total = None
    for side in (0, 1):
        d_pre = (mm(branch, downs[side][...]) * slopes[side][...].astype(WIDE)).astype(LOW)
        put(side, 0, t_mm(branch, acts[side][...]))
        put(side, half, t_mm(normed_two[...], d_pre))
        part = mm_t(d_pre, ups[side][...])
        total = part if total is None else total + part
    d_middle = d_tail + back(middle[...], gains[2:3, :], total, 2)
    branch = d_middle.astype(LOW)
    bias[...] = jnp.where(ids_col[...] == ids_row[...], 0.0, -1e30)
    total = None
    head = 0
    for side in (0, 1):
        qk_ref, v_ref, right = in_qk[side], in_v[side], rights[side]
        d_mixed = mm(branch, right[:, width:]).astype(LOW)
        put(side, half + ff + width, t_mm(branch, mixeds[side][...]))
        found = []
        for low in range(0, width, size):
            found.append(
                head_backward(
                    qk_ref[CTX:, low : low + size],
                    qk_ref[:, width + low : width + low + size],
                    v_ref[:, low : low + size],
                    d_mixed[:, low : low + size],
                    mixeds[side][:, low : low + size],
                    logs[head : head + 1, :],
                    bias,
                    soft,
                    d_scores,
                    size,
                )
            )
            head += 1
        d_query, d_keys, d_values = [jnp.concatenate(parts, -1) for parts in zip(*found)]
        d_qk[0:CTX, 0:width] = jnp.zeros((CTX, width), LOW)
        d_qk[CTX:, 0:width] = d_query
        d_qk[:, width:] = d_keys
        d_v[...] = d_values
        put(side, ff, t_mm(normed[...], d_qk[...]))
        put(side, half + ff, t_mm(normed[...], d_v[...]))
        part = mm_t(d_qk[...], qks[side][...]) + mm_t(d_v[...], right[:, 0:width])
        d_normed[...] = part if side == 0 else d_normed[...] + part
    d_joined = back(joined[...], gains[0:1, :], d_normed[...], 0)
    sums[6:7, :] = jnp.sum(d_joined[CTX:] + d_middle, 0, keepdims=True)
    sums[7:8, :] = jnp.zeros((1, PW), WIDE)
    d_inward[...] = d_joined[0:CTX].astype(LOW)
    g_in = mm_t(t_mm(context[...], d_inward[...]).astype(LOW), p_order[...])
    g_out = mm_t(g_bridge_out[...], p_order[...])
    flip = side_ref[0] != 0
    at = ff + 2 * width
    for side, values in ((0, jnp.where(flip, g_out, g_in)), (1, jnp.where(flip, g_in, g_out))):
        for block in range(dp_count):
            for low in (0, 1):
                start = (2 * block + low) * p_rows
                packs[side][block, :, low * half + at : (low + 1) * half] = values[
                    start : start + p_rows
                ].astype(LOW)


def pred_back_all(size, count_all, dp_count, side, order, used, values, pairs, logs, idq, idk):
    (guess, target, context, final, bridge_in, bridge_out, gains) = values[:7]
    ff, width, count = pairs[0][0].shape[1], pairs[2][0].shape[1] // 2, idk.shape[0]
    ins = [guess, target, used, context, final, bridge_in, bridge_out, gains]
    ins += [idq[None, :], idk[:, None], *values[7:]] + [part for pair in pairs for part in pair]
    ins += [logs, order, side]
    outs = [((1, 1), WIDE), ((CTX, PW), LOW), ((8, PW), WIDE)]
    outs += [((dp_count, PW // dp_count, 2 * (ff + 2 * width) + D), LOW)] * 2
    specs = [WHOLE] * len(ins)
    specs[2] = specs[-1] = pl.BlockSpec(memory_space=pltpu.SMEM)
    return pl.pallas_call(
        functools.partial(pred_back_all_kernel, size, count_all, dp_count),
        in_specs=specs,
        out_specs=[WHOLE] * len(outs),
        out_shape=[jax.ShapeDtypeStruct(shape, kind) for shape, kind in outs],
        scratch_shapes=[
            pltpu.VMEM((count, 2 * width), LOW),
            pltpu.VMEM((count, width), LOW),
            pltpu.VMEM((count, PW), WIDE),
            pltpu.VMEM((count, idq.shape[0]), WIDE),
            pltpu.VMEM((count, idq.shape[0]), LOW),
            pltpu.VMEM((count, idq.shape[0]), LOW),
            pltpu.VMEM((D, PW), LOW),
        ],
        cost_estimate=pl.CostEstimate(
            flops=4_000_000_000, bytes_accessed=20_000_000, transcendentals=3_000_000
        ),
        compiler_params=pltpu.CompilerParams(vmem_limit_bytes=36 * 2**20),
    )(*ins)


def pred_parts_kernel(dp_count, side_ref, own, other, order, *outs):
    width, half = PW // 2, D // 2
    ff = D
    flip = side_ref[0] != 0
    low = jnp.where(flip, other[:, 0:half], own[:, 0:half])
    high = jnp.where(flip, own[:, 0:half], other[:, 0:half])
    outs[0][...] = mm(low, order[...]).astype(LOW)
    outs[1][...] = mm(high, order[...]).astype(LOW)
    rows = PW // dp_count
    for at, ref in enumerate((own, other)):
        for start, wide, out in ((half, ff, 2), (half + ff, 2 * width, 6)):
            blocks = ref[:, start : start + wide].astype(WIDE).reshape(dp_count, 2 * rows, wide)
            outs[out + at][...] = blocks[:, :rows].reshape(PW, wide).astype(LOW)
            outs[out + 2 + at][...] = blocks[:, rows:].reshape(PW, wide).astype(LOW)


def pred_parts(dp_count, side, own, other, order):
    width, half = PW // 2, D // 2
    if PW // dp_count % 8:
        bridges = [part[:, :half] for part in (own, other)]
        first = side == 0
        found = [
            mm(jnp.where(first, bridges[at], bridges[1 - at]), order).astype(LOW) for at in (0, 1)
        ]
        for start, wide in ((half, D), (half + D, 2 * width)):
            cols = [part[:, start : start + wide] for part in (own, other)]
            cols = [part.reshape(dp_count, 2, PW // dp_count, wide) for part in cols]
            found += [flat(part[:, which]) for which in (0, 1) for part in cols]
    else:
        ins = [side[None], own, other, order]
        shapes = [(D, PW)] * 2 + [(PW, D)] * 4 + [(PW, 2 * width)] * 4
        outs = [jax.ShapeDtypeStruct(shape, LOW) for shape in shapes]
        found = pl.pallas_call(
            functools.partial(pred_parts_kernel, dp_count),
            in_specs=[pl.BlockSpec(memory_space=pltpu.SMEM)] + [WHOLE] * 3,
            out_specs=[WHOLE] * len(outs),
            out_shape=outs,
            cost_estimate=pl.CostEstimate(
                flops=1_000_000_000, bytes_accessed=9_000_000, transcendentals=0
            ),
            compiler_params=pltpu.CompilerParams(vmem_limit_bytes=36 * 2**20),
        )(*ins)
    return found[0], found[1], [found[at : at + 2] for at in range(2, 10, 2)]


class Lines:
    def __init__(self, count):
        self.count = count
        self.stride = count // 4
        bits = list(range(self.stride.bit_length() - 1))
        turn = len(bits) // 2
        self.bits = bits
        self.orders = (bits, bits[turn:] + bits[:turn])
        self.turn = turn

    def flip(self, values, bit):
        pairs = [(at, at ^ (1 << bit)) for at in range(self.count)]
        return lax.ppermute(values, "dp", pairs)

    def shift(self, values, steps):
        pairs = [(at, (at + steps * self.stride) % self.count) for at in range(self.count)]
        return lax.ppermute(values, "dp", pairs)

    def add_all(self, values, low, high):
        total = values
        for change in range(1, 1 << (high - low)):
            pairs = [(at, at ^ (change << low)) for at in range(2 * self.count)]
            total = total + lax.ppermute(values, ("dp", "mp"), pairs)
        return total

    def order(self, index, width):
        rows = width // self.count
        column = jnp.arange(width)
        block = column // rows
        far = (block // self.stride - index // self.stride) % 4
        near = (block ^ index) % self.stride
        target = (near * 4 + far) * rows + column % rows
        return (target[:, None] == column).astype(LOW)


def swap(values):
    return lax.ppermute(values, "mp", [(0, 1), (1, 0)])


def swap_all(values):
    return [swap(value) for value in values]


def far_kernel(*refs):
    outs = refs[4:]
    cut = outs[0].shape[-1]
    for at, block in enumerate(refs[:4]):
        outs[0][at] = block[:, :cut]
        outs[1][at] = block[:, cut:]


def gather_far(lines, shards):
    wide = jnp.concatenate(shards, 1)
    found = [wide] + [lines.shift(wide, -steps) for steps in (1, 2, 3)]
    rows, cut = shards[0].shape
    cols = [slice(0, cut), slice(cut, wide.shape[1])]
    if rows % 16:
        return [jnp.stack([block[:, part] for block in found]) for part in cols]
    return on_chip(
        far_kernel,
        found,
        [((4, rows, part.stop - part.start), LOW) for part in cols],
        [],
        0,
        ahead=True,
    )


def stack_kernel(axes, *refs):
    count = len(axes)
    ins, outs, bufs, sems = refs[: 2 * count], refs[2 * count : 3 * count], refs[3 * count : -1], refs[-1]
    arriving = [
        pltpu.make_async_copy(ins[at], bufs[at], sems.at[at]) for at in range(2 * count)
    ]
    for copy in arriving:
        copy.start()
    leaving = []
    for at, copy in enumerate(arriving):
        copy.wait()
        where = (slice(None),) * axes[at % count] + (at // count,)
        out = pltpu.make_async_copy(
            bufs[at], outs[at % count].at[where], sems.at[2 * count + at]
        )
        out.start()
        leaving.append(out)
    for copy in leaving:
        copy.wait()


def stack_pairs(held, got, axes):
    anywhere = pl.BlockSpec(memory_space=pl.ANY)
    ins = [*held, *got]
    outs = [
        jax.ShapeDtypeStruct(values.shape[:axis] + (2,) + values.shape[axis:], LOW)
        for values, axis in zip(held, axes)
    ]
    return pl.pallas_call(
        functools.partial(stack_kernel, axes),
        in_specs=[anywhere] * len(ins),
        out_specs=[anywhere] * len(outs),
        out_shape=outs,
        scratch_shapes=[pltpu.VMEM(value.shape, LOW) for value in ins]
        + [pltpu.SemaphoreType.DMA((2 * len(ins),))],
        cost_estimate=pl.CostEstimate(
            flops=0, bytes_accessed=8 * sum(value.size for value in ins), transcendentals=0
        ),
        compiler_params=pltpu.CompilerParams(vmem_limit_bytes=20 * 2**20),
    )(*ins)


def gather_near(lines, held, phase):
    done = [list(order[: lines.turn]) if phase else [] for order in lines.orders]
    steps = [order[lines.turn :] if phase else order[: lines.turn] for order in lines.orders]
    for bits in zip(*steps):
        got = [lines.flip(values, bit) for values, bit in zip(held, bits)]
        axes = [sum(1 for other in had if other > bit) for had, bit in zip(done, bits)]
        if phase and held[0].shape[-2] % 16 == 0:
            held = stack_pairs(held, got, axes)
        else:
            held = [
                jnp.stack([values, other], axis) for values, other, axis in zip(held, got, axes)
            ]
        for had, bit in zip(done, bits):
            had.append(bit)
    return list(held)


def flat(values):
    return values.reshape(-1, values.shape[-1])


class Box:
    def __init__(self, value):
        self.value, self.held = value, False


def sum_kernel(plan, squares, *refs):
    operands = 1 + max(term[0] for pieces in plan for piece in pieces for term in piece)
    if squares:
        refs[-1][...] = jnp.zeros((1, LANES), WIDE)
    for pieces, out in zip(plan, refs[operands:]):
        for lead in itertools.product(*[range(size) for size in out.shape[:-2]]):
            at = 0
            for piece in pieces:
                total = None
                for operand, low, high in piece:
                    part = refs[operand][lead + (slice(None), slice(low, high))].astype(WIDE)
                    total = part if total is None else total + part
                wide = high - low
                out[lead + (slice(None), slice(at, at + wide))] = total.astype(out.dtype)
                if squares:
                    for col in range(0, wide, LANES):
                        part = total[:, col : col + LANES]
                        weight = 0.5 if at + col == squares[1] and wide == squares[0] else 1.0
                        refs[-1][...] += weight * jnp.sum(part * part, 0, keepdims=True)
                at += wide


def sum_parts(outs, kind, squares=None):
    operands, specs, plan, shapes = [], [], [], []
    known = {}
    for pieces in outs:
        row = []
        for piece in pieces:
            terms = []
            for box, taken, (low, high) in piece:
                if (id(box), taken) not in known:
                    known[id(box), taken] = len(operands)
                    value = box.value
                    block = [
                        size if pick is None else None for size, pick in zip(value.shape, taken)
                    ]
                    where = tuple(0 if pick is None else pick for pick in taken) + (0, 0)
                    operands.append(value)
                    specs.append(
                        pl.BlockSpec(
                            tuple(block) + value.shape[-2:], lambda step, where=where: where
                        )
                    )
                terms.append((known[id(box), taken], low, high))
            row.append(tuple(terms))
        plan.append(tuple(row))
        box, taken, cols = pieces[0][0]
        lead = tuple(size for size, pick in zip(box.value.shape, taken) if pick is None)
        wide = sum(piece[0][2][1] - piece[0][2][0] for piece in pieces)
        shapes.append(
            jax.ShapeDtypeStruct(lead + (box.value.shape[-2], wide), kind)
        )
    moved = 8 * sum(shape.size for shape in shapes)
    if squares:
        shapes.append(jax.ShapeDtypeStruct((1, LANES), WIDE))
    return pl.pallas_call(
        functools.partial(sum_kernel, tuple(plan), squares),
        grid=(1,),
        in_specs=specs,
        out_specs=[
            pl.BlockSpec(shape.shape, lambda step, rank=len(shape.shape): (0,) * rank)
            for shape in shapes
        ],
        out_shape=shapes,
        cost_estimate=pl.CostEstimate(flops=moved, bytes_accessed=moved, transcendentals=0),
        compiler_params=pltpu.CompilerParams(vmem_limit_bytes=34 * 2**20),
    )(*operands)


class Terms:
    def __init__(self, lines, order, cols):
        self.lines, self.order, self.cols, self.left = lines, order, cols, list(lines.bits)
        self.terms = []

    def take(self, axis, at):
        found = []
        for box, taken, cols in self.terms:
            open_axes = [place_at for place_at, pick in enumerate(taken) if pick is None]
            picked = list(taken)
            picked[open_axes[axis]] = at
            found.append((box, tuple(picked), cols))
        return found

    def near_job(self, phase):
        turn = self.lines.turn
        (self.bit,) = self.order[turn:] if phase else self.order[:turn]
        self.axis = sum(1 for other in self.left if other > self.bit)
        return self.take(self.axis, 1)

    def near_send(self, send):
        got = self.lines.flip(send, self.bit)
        self.left.remove(self.bit)
        self.terms = self.take(self.axis, 0)
        self.terms.append((Box(got), (None,) * (got.ndim - 2), (0, got.shape[-1])))


class Sums:
    def __init__(self, lines, own, other, cut, rows):
        self.lines, self.rows, self.cut = lines, rows, cut
        self.plain = len(lines.bits) != 2
        self.own, self.other = Box(own), Box(other)
        self.lead = (2,) * len(lines.bits) + (4,)
        self.wide = own.shape[-1]
        self.parts = [
            Terms(lines, order, cols)
            for order, cols in zip(lines.orders, ((0, cut), (cut, self.wide)))
        ]

    def shaped(self, values):
        return values.reshape(self.lead + (self.rows, self.wide))

    def boxes(self):
        found = [self.own, self.other]
        for part in self.parts:
            found += [term[0] for term in part.terms]
        return found

    def swap(self, got=None):
        if self.plain:
            return
        mine = Box(self.shaped(self.own.value))
        mine.held = True
        if got is None:
            got = swap(self.other.value)
        self.other.held = True
        got = Box(self.shaped(got))
        for part in self.parts:
            blank = (None,) * len(self.lead)
            part.terms = [(mine, blank, part.cols), (got, blank, part.cols)]

    def far_jobs(self):
        return [[part.take(0, steps) for part in self.parts] for steps in (1, 2, 3)]

    def far_send(self, sends):
        got = [Box(self.lines.shift(send, steps)) for send, steps in zip(sends, (1, 2, 3))]
        for part in self.parts:
            part.terms = part.take(0, 0) + [(box, (), part.cols) for box in got]

    def results(self, halved=(0, -1)):
        if not self.plain:
            return sum_parts([[part.terms] for part in self.parts], WIDE, halved)
        results = []
        both = self.own.value.astype(WIDE) + swap(self.other.value).astype(WIDE)
        for part in self.parts:
            total = self.shaped(both)[..., part.cols[0] : part.cols[1]]
            for bit in part.order:
                axis = sum(1 for other in part.left if other > bit)
                part.left.remove(bit)
                sent = lax.index_in_dim(total, 1, axis, keepdims=False).astype(LOW)
                total = lax.index_in_dim(total, 0, axis, keepdims=False)
                total = total + self.lines.flip(sent, bit).astype(WIDE)
            result = total[0]
            for steps in (1, 2, 3):
                got = self.lines.shift(total[steps].astype(LOW), steps)
                result = result + got.astype(WIDE)
            results.append(result)
        squares = sum(jnp.sum(result * result) for result in results)
        for result in results:
            if result.shape[1] == halved[0]:
                part = result[:, halved[1] : halved[1] + LANES]
                squares = squares - 0.5 * jnp.sum(part * part)
        return results + [jnp.pad(squares.reshape(1, 1), ((0, 0), (0, LANES - 1)))]


def move(*steps, hold=None):
    work = []
    for total, kind in steps:
        if total.plain:
            continue
        if kind == 2:
            work.append((total.far_send, total.far_jobs()))
        else:
            for part in total.parts:
                work.append((part.near_send, [[part.near_job(kind)]]))
    if not work:
        return hold
    sends = sum_parts([job for send, jobs in work for job in jobs], LOW)
    if hold is not None:
        sends, hold = lax.optimization_barrier((sends, hold))
    at = 0
    for send, jobs in work:
        found = sends[at : at + len(jobs)]
        at += len(jobs)
        send(found if len(jobs) > 1 else found[0])
    return hold


def fence_sums(sums, *values):
    boxes = {id(box): box for one in sums for box in one.boxes() if not box.held}
    boxes = list(boxes.values())
    held, values = lax.optimization_barrier(([box.value for box in boxes], values))
    for box, value in zip(boxes, held):
        box.value, box.held = value, True
    return values


def fence(*values):
    return lax.optimization_barrier(values)


def adam(weight, moment_one, moment_two, gradient, decay, rate):
    moment_one = BETA_ONE * moment_one + (1.0 - BETA_ONE) * gradient
    moment_two = BETA_TWO * moment_two + (1.0 - BETA_TWO) * gradient * gradient
    fixed_one = moment_one / (1.0 - BETA_ONE**STEP)
    fixed_two = moment_two / (1.0 - BETA_TWO**STEP)
    weight = weight - rate * (fixed_one / (jnp.sqrt(fixed_two) + EPSILON) + decay * weight)
    return [weight, moment_one, moment_two]


def adam_kernel(plan, scalars, side, *refs):
    count = len(plan)
    grads = refs[3 * count : -3 * count]
    total = jnp.sum(scalars[0:1, :], 1, keepdims=True)
    factor = jnp.minimum(1.0, CLIP_NORM / (jnp.sqrt(total) + 1e-06))
    for at, (rate, decay, pieces) in enumerate(plan):
        ins = refs[3 * at : 3 * at + 3]
        outs = refs[len(refs) - 3 * count + 3 * at :][:3]
        for grad, rows_from, cols_from, rows, cols in pieces:
            if isinstance(cols[0], bool):
                half = side[0] if cols[0] else 1 - side[0]
                span = pl.ds(pl.multiple_of(half * cols[1], LANES), cols[1])
            else:
                span = slice(*cols)
            where = (slice(*rows), span)
            gradient = grads[grad][slice(*rows_from), slice(*cols_from)] * factor
            results = adam(*[ref[where] for ref in ins], gradient, decay, rate)
            for out, result in zip(outs, results):
                out[where] = result


def adam_all(scalars, side, groups, grads, plan):
    outs = [jax.ShapeDtypeStruct(group[0].shape, WIDE) for group in groups for at in range(3)]
    scalar = pl.BlockSpec(memory_space=pltpu.SMEM)
    ins = [value for group in groups for value in group] + list(grads)
    found = pl.pallas_call(
        functools.partial(adam_kernel, plan),
        in_specs=[WHOLE, scalar] + [WHOLE] * len(ins),
        out_specs=[WHOLE] * len(outs),
        out_shape=outs,
        cost_estimate=pl.CostEstimate(
            flops=20_000_000, bytes_accessed=10_000_000, transcendentals=400_000
        ),
        compiler_params=pltpu.CompilerParams(vmem_limit_bytes=58 * 2**20),
    )(scalars, side, *ins)
    return [found[at : at + 3] for at in range(0, len(found), 3)]


def two_parts(values):
    high = lax.reduce_precision(values, 8, 7)
    fill = ((0, 0), (0, 8 - values.shape[1]))
    return jnp.concatenate([jnp.pad(high, fill), jnp.pad(values - high, fill)], 1).astype(LOW)


def widen_rows(values, rows):
    return jnp.pad(values, ((0, rows - values.shape[0]), (0, 0)))


def shards(
    patches,
    ctx_index,
    tgt_index,
    group,
    tgt_count,
    embed,
    embed_m,
    embed_v,
    bridge,
    bridge_m,
    bridge_v,
    enc_in,
    enc_in_m,
    enc_in_v,
    enc_out,
    enc_out_m,
    enc_out_v,
    enc_gains,
    enc_gains_m,
    enc_gains_v,
    pred_in,
    pred_in_m,
    pred_in_v,
    pred_out,
    pred_out_m,
    pred_out_v,
    pred_gains,
    pred_gains_m,
    pred_gains_v,
    t_embed,
    t_in,
    t_out,
    t_gains,
):
    index = lax.axis_index("dp")
    side = lax.axis_index("mp")
    dp_count = lax.axis_size("dp")
    lines = Lines(dp_count)
    assert patches.shape[0] == lax.axis_size("mp")
    count = patches.shape[0] * dp_count * TGT * D
    rows = D // dp_count
    p_rows = PW // dp_count
    half_d = D // 2
    local = D // 2
    ff = enc_in.shape[1] - 3 * local
    p_local = PW // 2
    p_ff = pred_in.shape[1] - 3 * p_local
    first = side == 0
    size = D // HEADS
    p_size = PW // PHEADS

    def own_half(values):
        return lax.dynamic_slice_in_dim(values, side * half_d, half_d, 1).astype(LOW)

    gains_pack = jnp.concatenate(
        [
            two_parts(enc_gains.T),
            two_parts(t_gains.T),
            widen_rows(two_parts(pred_gains.T), rows),
            jnp.zeros((rows, LANES - 48), LOW),
        ],
        1,
    )
    enc_in_low, t_in_low = enc_in.astype(LOW), t_in.astype(LOW)
    enc_out_low, t_out_low = enc_out.T.astype(LOW), t_out.T.astype(LOW)
    pred_in_low, pred_out_low = pred_in.astype(LOW), pred_out.T.astype(LOW)
    pred_main = jnp.concatenate([pred_out_low[:, p_local:], pred_in_low[:, 3 * p_local :]], 0)
    pred_rest = jnp.concatenate(
        [
            pred_in_low[:, : 2 * p_local],
            jnp.concatenate(
                [pred_in_low[:, 2 * p_local : 3 * p_local], pred_out_low[:, :p_local]], 1
            ),
        ],
        0,
    )
    packs = [
        [
            enc_in_low[:, : 3 * local],
            jnp.concatenate([own_half(embed), enc_out_low[:, :local], gains_pack], 1),
        ],
        [
            jnp.concatenate(
                [t_in_low[:, : 3 * local], own_half(t_embed), t_out_low[:, :local]], 1
            ),
            jnp.concatenate([own_half(bridge), pred_main, pred_rest], 1),
        ],
        [enc_in_low[:, 3 * local :], enc_out_low[:, local:]],
        [t_in_low[:, 3 * local :], t_out_low[:, local:]],
    ]

    far_a = gather_far(lines, packs[0])
    far_a, packs[1] = fence(far_a, packs[1])
    near_a = gather_near(lines, far_a, 0)
    near_a, packs[1], patches, ctx_index, tgt_index, group, tgt_count = fence(
        near_a, packs[1], patches, ctx_index, tgt_index, group, tgt_count
    )
    order = lines.order(index, D)
    p_order = lines.order(index, PW)
    eye = jnp.eye(D, dtype=LOW)
    patch = lax.dynamic_index_in_dim(patches, side, 0, keepdims=False)
    ctx = lax.dynamic_index_in_dim(ctx_index, side, 0, keepdims=False)
    tgt = lax.dynamic_index_in_dim(tgt_index, side, 0, keepdims=False)
    single = lax.dynamic_index_in_dim(group, side, 0, keepdims=False) == 1
    used = lax.dynamic_index_in_dim(tgt_count, side, 0, keepdims=False)
    positions = jnp.arange(patch.shape[0])
    chosen = jnp.concatenate([ctx, tgt])
    all_id, all_row, all_col = place(single, positions)
    joined_id, joined_row, joined_col = place(single, chosen)
    ctx_id, tgt_id = joined_id[:CTX], joined_id[CTX:]

    spread = jnp.arange(D) // rows * p_rows + jnp.arange(D) % rows
    spread = (jnp.arange(PW)[:, None] == spread) & (jnp.arange(D) % rows < p_rows)
    spread = spread.astype(LOW)
    pos_all = sincos(all_row, all_col, D, order)
    pos_ctx = sincos(joined_row[:CTX], joined_col[:CTX], D, order)
    pos_tgt = sincos(joined_row[CTX:], joined_col[CTX:], D, order)
    pos_small = sincos(joined_row, joined_col, PW, p_order)
    patch = mm(patch, order).astype(LOW)
    seen_ctx = mm((ctx[:, None] == positions).astype(LOW), patch).astype(LOW)
    seen_tgt = mm((tgt[:, None] == positions).astype(LOW), patch).astype(LOW)
    order_own = lax.dynamic_slice_in_dim(order, side * half_d, half_d, 0)
    order_other = lax.dynamic_slice_in_dim(order, (1 - side) * half_d, half_d, 0)
    held_a = gather_near(lines, near_a, 1)
    far_b = gather_far(lines, packs[1])
    (
        held_a,
        far_b,
        pos_all,
        pos_ctx,
        pos_tgt,
        pos_small,
        patch,
        seen_ctx,
        seen_tgt,
        order_own,
        order_other,
        spread,
        order,
        p_order,
        eye,
        all_id,
        ctx_id,
        tgt_id,
        joined_id,
        used,
        packs[2],
    ) = fence(
        held_a,
        far_b,
        pos_all,
        pos_ctx,
        pos_tgt,
        pos_small,
        patch,
        seen_ctx,
        seen_tgt,
        order_own,
        order_other,
        spread,
        order,
        p_order,
        eye,
        all_id,
        ctx_id,
        tgt_id,
        joined_id,
        used,
        packs[2],
    )
    other_a = swap_all(held_a)
    near_b = gather_near(lines, far_b, 0)
    held_a, other_a, near_b, packs[2] = fence(held_a, other_a, near_b, packs[2])

    def widths(values, *sizes):
        found, at = [], 0
        for wide in sizes:
            found.append(values[:, at : at + wide])
            at += wide
        return found

    enc_qkv = (flat(held_a[0]), flat(other_a[0]))
    enc_rest = (flat(held_a[1]), flat(other_a[1]))
    held_b = gather_near(lines, near_b, 1)
    far_c = gather_far(lines, packs[2])
    start, normed_one, *projected, enc_gain, target_gain, pred_gain = ctx_first(
        seen_ctx,
        pos_ctx,
        spread,
        (order_own, order_other),
        enc_rest,
        enc_qkv,
    )
    held_b, far_c, start, projected, packs[3] = fence(
        held_b, far_c, start, projected, packs[3]
    )
    other_b = swap_all(held_b)
    near_c = gather_near(lines, far_c, 0)
    middle, normed_two, *pairs = ctx_second(
        size, start, enc_gain, ctx_id, enc_rest, projected
    )
    mixed, logs = pairs[:2], pairs[2:]
    held_b, other_b, near_c, normed_two, middle, packs[3] = fence(
        held_b, other_b, near_c, normed_two, middle, packs[3]
    )
    held_c = gather_near(lines, near_c, 1)
    far_d = gather_far(lines, packs[3])
    t_middle, t_two = target_forward(
        size,
        patch,
        seen_tgt,
        pos_all,
        pos_tgt,
        target_gain,
        tgt_id,
        all_id,
        (order_own, order_other),
        (flat(held_b[0]), flat(other_b[0])),
    )
    held_c, far_d, t_middle, t_two = fence(held_c, far_d, t_middle, t_two)
    other_c = swap_all(held_c)
    near_d = gather_near(lines, far_d, 0)
    bridge_in, bridge_out, pairs = pred_parts(
        dp_count, side.astype(jnp.int32), flat(held_b[1]), flat(other_b[1]), p_order
    )
    pred_down, pred_up, pred_qk, pred_right = pairs
    held_c, other_c, near_d, bridge_in, bridge_out, pred_down, pred_up, pred_qk, pred_right = fence(
        held_c, other_c, near_d, bridge_in, bridge_out, pred_down, pred_up, pred_qk, pred_right
    )
    held_d = gather_near(lines, near_d, 1)
    enc_up, enc_down = [(flat(own), flat(other)) for own, other in zip(held_c, other_c)]
    hidden, context, *pairs = ff_forward(
        normed_two, middle, enc_gain, enc_up, enc_down
    )
    activated, slope = pairs[:2], pairs[2:]
    (
        joined,
        p_normed_one,
        p_middle,
        p_normed_two,
        predicted,
        final,
        guess,
        *pairs,
    ) = pred_forward(
        p_size,
        context,
        bridge_in,
        bridge_out,
        pos_small,
        pred_gain,
        tgt_id,
        joined_id,
        pred_down,
        pred_up,
        pred_qk,
        pred_right,
    )
    p_qk, p_values, p_mixed, p_activated, p_slope = [
        pairs[at : at + 2] for at in range(0, 10, 2)
    ]
    p_logs = pairs[10]
    held_d, guess, t_middle = fence(held_d, guess, t_middle)
    other_d = swap_all(held_d)
    target = target_ff(False, t_two, t_middle, target_gain, *[flat(part) for part in held_d])
    target, other_d = fence(target, other_d)
    target = target_ff(True, t_two, target, target_gain, *[flat(part) for part in other_d])
    (
        loss_local,
        d_inward,
        sums_pred,
        *pair_p,
    ) = pred_back_all(
        p_size,
        count,
        dp_count,
        side[None].astype(jnp.int32),
        p_order,
        used[None],
        [
            guess,
            target,
            context,
            final,
            bridge_in,
            bridge_out,
            pred_gain,
            predicted,
            p_middle,
            joined,
            p_normed_one,
            p_normed_two,
        ],
        [
            pred_down,
            pred_up,
            pred_qk,
            pred_right,
            p_activated,
            p_slope,
            p_qk,
            p_values,
            p_mixed,
        ],
        p_logs,
        tgt_id,
        joined_id,
    )
    sum_p = Sums(lines, *pair_p, 4 * local, p_rows)
    (d_inward,) = fence_sums([sum_p], d_inward)
    sum_p.swap()
    (d_inward,) = fence_sums([sum_p], d_inward)
    d_inward = move((sum_p, 0), hold=d_inward)
    grads_other, *parts, sums_ff = ff_back_first(
        d_inward,
        bridge_in,
        hidden,
        normed_two,
        eye,
        enc_gain,
        activated[1],
        slope[1],
        enc_down[1],
    )
    grads_other, parts = fence_sums([sum_p], grads_other, parts)
    grads_got = swap(grads_other)
    parts = move((sum_p, 1), hold=parts)
    grads_own, branch, d_middle, sums_ff = ff_back_second(
        *parts,
        middle,
        enc_gain,
        activated[0],
        slope[0],
        enc_down[0],
        enc_up[0],
        enc_up[1],
        sums_ff,
    )
    sum_f = Sums(lines, grads_own, grads_other, ff, rows)
    sum_f.swap(grads_got)
    branch, d_middle = fence_sums([sum_p, sum_f], branch, d_middle)
    d_middle, branch = move((sum_f, 0), (sum_p, 2), hold=(d_middle, branch))
    d_proj = attn_back(size, branch, ctx_id, enc_rest, projected, mixed, logs)
    (d_proj,) = fence_sums([sum_p, sum_f], d_proj)
    d_proj = move((sum_f, 1), hold=d_proj)
    grads_own, grads_other = qkv_back(
        branch,
        d_middle,
        start,
        normed_one,
        seen_ctx,
        eye,
        enc_gain,
        sums_ff,
        sums_pred,
        spread,
        [d_proj, mixed, enc_qkv, (order_own, order_other)],
    )
    sum_a = Sums(lines, grads_own, grads_other, 3 * local, rows)
    fence_sums([sum_f, sum_a])
    sum_a.swap()
    fence_sums([sum_f, sum_a])
    move((sum_f, 2), (sum_a, 0))
    fence_sums([sum_f, sum_a])
    move((sum_a, 1))
    fence_sums([sum_a])
    move((sum_a, 2))

    red_left, red_right, squares_p = sum_p.results()
    red_up, red_down, squares_f = sum_f.results()
    red_qkv, red_rest, squares_a = sum_a.results((2 * local + LANES, 2 * local))
    low_one = p_ff + 2 * p_local
    bridge_other = swap(jnp.concatenate([red_left[:, low_one:], red_right[:, low_one:]], 0))
    embed_other = swap(red_rest[:, :local])
    gains_t = red_rest[:, 2 * local :].T
    sums = jnp.concatenate(
        [squares_p + squares_f + squares_a, jnp.pad(loss_local, ((0, 0), (0, LANES - 1)))], 0
    )
    for step in range(0, dp_count.bit_length(), 2):
        sums = lines.add_all(sums, step, min(step + 2, dp_count.bit_length()))
    groups = [
        (embed, embed_m, embed_v),
        (bridge, bridge_m, bridge_v),
        (enc_in, enc_in_m, enc_in_v),
        (enc_out.T, enc_out_m.T, enc_out_v.T),
        (enc_gains, enc_gains_m, enc_gains_v),
        (pred_in, pred_in_m, pred_in_v),
        (pred_out.T, pred_out_m.T, pred_out_v.T),
        (pred_gains, pred_gains_m, pred_gains_v),
    ]
    grads = [
        red_left,
        red_right,
        red_up,
        red_down,
        red_qkv,
        red_rest,
        bridge_other,
        embed_other,
        gains_t,
    ]
    every, part = (0, rows), (0, p_rows)
    lower = (p_rows, 2 * p_rows)
    qk_end, v_end = p_ff + 2 * p_local, p_ff + p_local
    learn, gain = (LEARN_RATE, WEIGHT_DECAY), (GAIN_RATE, 0.0)
    plan = (
        (
            *learn,
            (
                (5, every, (0, local), every, (True, half_d)),
                (7, every, (0, local), every, (False, half_d)),
            ),
        ),
        (
            *learn,
            (
                (0, part, (qk_end, qk_end + half_d), part, (True, half_d)),
                (1, part, (qk_end, qk_end + half_d), lower, (True, half_d)),
                (6, every, (0, half_d), every, (False, half_d)),
            ),
        ),
        (
            *learn,
            (
                (4, every, (0, 3 * local), every, (0, 3 * local)),
                (2, every, (0, ff), every, (3 * local, 3 * local + ff)),
            ),
        ),
        (
            *learn,
            (
                (5, every, (local, 2 * local), every, (0, local)),
                (3, every, (0, ff), every, (local, local + ff)),
            ),
        ),
        (*gain, ((8, (0, 6), every, (0, 6), every),)),
        (
            *learn,
            (
                (0, part, (p_ff, qk_end), part, (0, 2 * p_local)),
                (1, part, (p_ff, v_end), part, (2 * p_local, 3 * p_local)),
                (1, part, (0, p_ff), part, (3 * p_local, 3 * p_local + p_ff)),
            ),
        ),
        (
            *learn,
            (
                (1, part, (v_end, qk_end), part, (0, p_local)),
                (0, part, (0, p_ff), part, (p_local, p_local + p_ff)),
            ),
        ),
        (*gain, ((8, (8, 15), part, (0, 7), part),)),
    )
    results = adam_all(sums, side[None].astype(jnp.int32), groups, grads, plan)
    for at in (3, 6):
        results[at] = [value.T for value in results[at]]
    return (*[value for result in results for value in result], sums[1, 0], jnp.sqrt(jnp.sum(sums[0])))


def solution(mesh):
    in_specs = (
        P("dp", None, None),
        P("dp", None),
        P("dp", None),
        P("dp"),
        P("dp"),
        P("dp", None),
        P("dp", None),
        P("dp", None),
        P("dp", None),
        P("dp", None),
        P("dp", None),
        P("dp", "mp"),
        P("dp", "mp"),
        P("dp", "mp"),
        P("mp", "dp"),
        P("mp", "dp"),
        P("mp", "dp"),
        P(None, "dp"),
        P(None, "dp"),
        P(None, "dp"),
        P("dp", "mp"),
        P("dp", "mp"),
        P("dp", "mp"),
        P("mp", "dp"),
        P("mp", "dp"),
        P("mp", "dp"),
        P(None, "dp"),
        P(None, "dp"),
        P(None, "dp"),
        P("dp", None),
        P("dp", "mp"),
        P("mp", "dp"),
        P(None, "dp"),
    )
    out_specs = (
        P("dp", None),
        P("dp", None),
        P("dp", None),
        P("dp", None),
        P("dp", None),
        P("dp", None),
        P("dp", "mp"),
        P("dp", "mp"),
        P("dp", "mp"),
        P("mp", "dp"),
        P("mp", "dp"),
        P("mp", "dp"),
        P(None, "dp"),
        P(None, "dp"),
        P(None, "dp"),
        P("dp", "mp"),
        P("dp", "mp"),
        P("dp", "mp"),
        P("mp", "dp"),
        P("mp", "dp"),
        P("mp", "dp"),
        P(None, "dp"),
        P(None, "dp"),
        P(None, "dp"),
        P(),
        P(),
    )
    return jax.shard_map(shards, mesh=mesh, in_specs=in_specs, out_specs=out_specs, check_vma=False)
```
